32 devices in a mesh: walker: 8 (over z, y), orb: 4 (over x, core).
Axes of the slice: x: 2, y: 2, z: 4, core: 2. Of those that a mesh axis runs over, the one named last changes fastest.
Arguments:
- positions: float32 [64, 3, 512], P('walker'), may hold values from 0 to 24
- inverse: float32 [64, 512, 512], P('walker', 'orb')
- spline_table: bfloat16 [512, 13824], P('orb'), may hold values from -6 to 6
- gaussian: float32 [64, 3, 64], P('walker'), may hold values from -4 to 4
- accepted: int32 [64, 64], P('walker'), may hold values 0 or 1
- block_order: int32 [32], replicated, may hold values from 0 to 31, each once
- parent: int32 [64], P('walker'), may hold values from 0 to 63, as said below
Outputs:
- new_positions: float32 [64, 3, 512], P('walker')
- new_inverse: float32 [64, 512, 512], P('walker', 'orb')
The draws below stay inside these ranges and needn't reach their ends.
Inputs may be any that keep to these rules, and one draw needn't show every extreme that they name: Walkers s and parent[s] lie in the same group of 8 (one index of walker) except for 3 to 6 walkers of each group, exactly 6 in some group; a group takes at most 1 parents from any one other group, exactly 1 from some. A parent may be named several times or not at all.
All inputs are finite; a program needn't handle non-finite values. No bound on the sum of `accepted` on one device may be relied on, other than what follows from the above.
Results may differ from the reference program's by a relative error of at most 0.0004.
Values may be sent and summed in bfloat16 or wider, within the bound.
No kernel may reach another device: no remote copies, remote signals or barrier semaphores. Data moves between devices by JAX's collectives and lax.ppermute only.
A program may use at most 128 MiB of HBM per device.

```python
import jax
import jax.numpy as jnp
from jax import lax

NE = 512
GRID = 24
K = 16
NMOVE = 4
WALK_DEV = 8
CAP = 1
RMAX = 6
WALKERS = 64
NBLOCK = 32
MOVED = 64
N_WALKER = 8


def draw_inverse(key, part):
    key = jax.random.fold_in(key, 11)
    first_key, second_key = jax.random.split(key)
    spread = 0.5 / NE ** 0.5
    offdiag = jax.random.normal(first_key, (WALKERS, NE, NE), jnp.float32) * spread
    diagonal = jax.random.uniform(second_key, (WALKERS, NE), jnp.float32, 0.85, 1.15)
    identity = (lax.broadcasted_iota(jnp.int32, (NE, NE), 0) == lax.broadcasted_iota(jnp.int32, (NE, NE), 1)).astype(jnp.float32)
    return offdiag * (1.0 - identity) + diagonal[:, :, None] * identity


def draw_parent(key, part):
    key = jax.random.fold_in(key, 23)
    keys = jax.random.split(key, 6)
    groups = N_WALKER
    width = WALK_DEV
    lowest = RMAX - RMAX // 2
    counts = jax.random.randint(keys[0], (groups,), lowest, RMAX + 1)
    fullest = jax.random.randint(keys[1], (), 0, groups)
    targets = jnp.arange(groups, dtype=jnp.int32)
    counts = jnp.where(targets == fullest, RMAX, counts)
    surplus = (jax.random.randint(keys[2], (groups,), 0, 4) == 0).astype(jnp.int32)
    ahead = jnp.arange(groups - 1, dtype=jnp.int32)
    others = jnp.mod(targets[:, None] + 1 + ahead[None, :], groups)
    jumble = jax.random.randint(keys[3], (groups, groups - 1), 0, groups * groups)
    score = ((1 - surplus[others]) * (groups * groups) + jumble) * groups + ahead[None, :]
    ranked = jnp.argsort(score, axis=1)
    sources = jnp.take_along_axis(others, ranked, axis=1)
    placing = jax.vmap(lambda piece_key: jax.random.permutation(piece_key, width))(jax.random.split(keys[4], groups))
    slot_source = jnp.take_along_axis(sources, jnp.minimum(placing // CAP, groups - 2), axis=1)
    remote = placing < counts[:, None]
    group_of = jnp.where(remote, slot_source, targets[:, None])
    local = jax.random.randint(keys[5], (groups, width), 0, width)
    return (group_of * width + local).reshape(groups * width).astype(jnp.int32)


def plant(drawn, rng, low, largest):
    place = [jax.random.randint(jax.random.fold_in(rng, axis), (), 0, length) for axis, length in enumerate(drawn.shape)]
    main_axis = drawn.shape.index(max(drawn.shape))
    beside = place[:main_axis] + [(place[main_axis] + 1) % drawn.shape[main_axis]] + place[main_axis + 1:]
    return drawn.at[tuple(place)].set(low).at[tuple(beside)].set(largest)


def block_scale(stream_key, dims, cuts, smallest, high):
    gain, own = 1.0, jax.random.fold_in(stream_key, 6)
    for axis_at, parts in cuts:
        steps = jnp.exp(jax.random.uniform(jax.random.fold_in(own, axis_at), (parts,), jnp.float32, smallest / len(cuts), high / len(cuts)))
        gain = gain * jnp.repeat(steps, dims[axis_at] // parts).reshape([-1 if axis == axis_at else 1 for axis in range(len(dims))])
    return gain


def bell_draw(key, extent, deviation, most, shards=(), kind=jnp.bfloat16):
    entries = deviation * jax.random.normal(key, extent, jnp.float32)
    if shards:
        entries = entries * block_scale(key, extent, shards, -0.22, 0.18)
    return jnp.clip(entries, -most, most).astype(kind)


def setup_inputs(seed: int = 0) -> dict:
    streams_of = jax.random.split(jax.random.key(seed), 8)
    return {
        "positions": jnp.clip(24.0 * jax.random.uniform(streams_of[0], (WALKERS, 3, NE), jnp.float32) ** block_scale(streams_of[0], (WALKERS, 3, NE), ((0, 8),), -0.2, 0.2), 0.0, 24.0),
        "inverse": draw_inverse(jax.random.fold_in(streams_of[7], 71), 0),
        "spline_table": bell_draw(streams_of[2], (NE, GRID * GRID * GRID), 1.0, 6.0, ((0, 4),)),
        "gaussian": bell_draw(streams_of[3], (WALKERS, 3, MOVED), 1.0, 4.0, ((0, 8),), jnp.float32),
        "accepted": plant((jax.random.randint(streams_of[4], (WALKERS, MOVED), 0, 4) < 3).astype(jnp.int32), jax.random.fold_in(streams_of[4], 1), 0, 1),
        "block_order": jax.random.permutation(streams_of[5], NBLOCK).astype(jnp.int32),
        "parent": draw_parent(jax.random.fold_in(streams_of[7], 71), 0),
    }


TAU = 0.25
ROOT_TAU = 0.5

def spline_weights(coords):
    floors = jnp.floor(coords)
    within = coords - floors
    remain = 1.0 - within
    square = within * within
    cubed = square * within
    values = jnp.stack([remain * remain * remain / 6.0, (3.0 * cubed - 6.0 * square + 4.0) / 6.0, (-3.0 * cubed + 3.0 * square + 3.0 * within + 1.0) / 6.0, cubed / 6.0])
    slopes = jnp.stack([-0.5 * remain * remain, 1.5 * square - 2.0 * within, -1.5 * square + within + 0.5, 0.5 * square])
    return (floors.astype(jnp.int32) - 1, values, slopes)

def evaluate(table_rows, coords, with_slopes):
    corner, values, slopes = spline_weights(coords)
    shifts = jnp.arange(4, dtype=jnp.int32)
    indices = jnp.mod(corner[None, :, :] + shifts[:, None, None], GRID)
    along_x = indices[:, 0]
    along_y = indices[:, 1]
    along_z = indices[:, 2]
    points = (along_x[:, None, None] * (GRID * GRID) + along_y[None, :, None] * GRID + along_z[None, None, :]).reshape(64, -1)
    value_x = values[:, 0][:, None, None]
    value_y = values[:, 1][None, :, None]
    value_z = values[:, 2][None, None, :]
    plain = (value_x * value_y * value_z).reshape(64, -1)
    if with_slopes:
        slope_x = (slopes[:, 0][:, None, None] * value_y * value_z).reshape(64, -1)
        slope_y = (value_x * slopes[:, 1][None, :, None] * value_z).reshape(64, -1)
        slope_z = (value_x * value_y * slopes[:, 2][None, None, :]).reshape(64, -1)
        weights = jnp.stack([plain, slope_x, slope_y, slope_z])
    else:
        weights = plain[None]
    gathered = jnp.take(table_rows, points, axis=1).astype(jnp.float32)
    return jnp.einsum('rne,cne->cre', gathered, weights, precision=lax.Precision.HIGHEST)

def blocked_sweep(table_rows, positions, inverse, gaussian, accepted, block_order):
    walkers = positions.shape[0]
    for sweep_step in range(NMOVE):
        offset = (block_order[sweep_step] * K).astype(jnp.int32)
        current = lax.dynamic_slice_in_dim(positions, offset, K, 2)
        columns = lax.dynamic_slice_in_dim(inverse, offset, K, 2)
        coords = jnp.transpose(current, (1, 0, 2)).reshape(3, walkers * K)
        pieces = evaluate(table_rows, coords, True)
        orbitals = pieces.shape[1]
        slopes = pieces[1:].reshape(3, orbitals, walkers, K)
        drifts = jnp.einsum('djwk,wjk->wdk', slopes, columns, precision=lax.Precision.HIGHEST)
        speeds = lax.optimization_barrier(jnp.sum(drifts * drifts, axis=1, keepdims=True))
        capped = drifts / jnp.sqrt(1.0 + TAU * speeds)
        jitter = lax.slice_in_dim(gaussian, sweep_step * K, sweep_step * K + K, axis=2)
        decide = lax.slice_in_dim(accepted, sweep_step * K, sweep_step * K + K, axis=1)[:, None, :]
        proposal = current + decide * (TAU * capped + ROOT_TAU * jitter)
        new_coords = jnp.transpose(proposal, (1, 0, 2)).reshape(3, walkers * K)
        fresh_vals = evaluate(table_rows, new_coords, False)[0]
        change = (fresh_vals - pieces[0]).reshape(orbitals, walkers, K)
        updates = jnp.einsum('jwk,wjn->wkn', change, inverse, precision=lax.Precision.HIGHEST)
        inverse = inverse - jnp.einsum('wjk,wkn->wjn', columns, updates, precision=lax.Precision.HIGHEST)
        positions = lax.dynamic_update_slice_in_dim(positions, proposal, offset, 2)
    return (positions, inverse)

def reference(positions, inverse, spline_table, gaussian, accepted, block_order, parent):
    decided = accepted.astype(jnp.float32)
    grouped = (positions.reshape(N_WALKER, WALK_DEV, 3, NE), inverse.reshape(N_WALKER, WALK_DEV, NE, NE), gaussian.reshape(N_WALKER, WALK_DEV, 3, MOVED), decided.reshape(N_WALKER, WALK_DEV, MOVED))

    def one_group(items):
        return blocked_sweep(spline_table, items[0], items[1], items[2], items[3], block_order)
    swept_pos, swept_inv = lax.map(one_group, grouped)
    swept_pos = swept_pos.reshape(WALKERS, 3, NE)
    swept_inv = swept_inv.reshape(WALKERS, NE, NE)
    return (jnp.take(swept_pos, parent, axis=0), jnp.take(swept_inv, parent, axis=0))
```

```python
import functools

import jax
import jax.numpy as jnp
from jax import lax
from jax.experimental import pallas as pl
from jax.experimental.pallas import tpu as pltpu
from jax.sharding import PartitionSpec as P

GRID = 24
PLANE = GRID * GRID
WIDE = 640
K = 16
NMOVE = 4
MOVED = K * NMOVE
CAP = 1
TAU = 0.25
ROOT_TAU = 0.5
F32 = jnp.float32
BF16 = jnp.bfloat16
HIGHEST = lax.Precision.HIGHEST
VMEM = pl.BlockSpec(memory_space=pltpu.VMEM)
LIMIT = 24 * 2**20


def axis_weights(u, with_slopes):
    floors = jnp.floor(u)
    t = u - floors
    remain = 1.0 - t
    square = t * t
    cubed = square * t
    values = (
        remain * remain * remain / 6.0,
        (3.0 * cubed - 6.0 * square + 4.0) / 6.0,
        (-3.0 * cubed + 3.0 * square + 3.0 * t + 1.0) / 6.0,
        cubed / 6.0,
    )
    lanes = u.shape[1]
    line = lax.broadcasted_iota(jnp.int32, (GRID, lanes), 0)
    step = line - (floors.astype(jnp.int32) - 1)
    step = jnp.where(step < 0, step + GRID, step)
    step = jnp.where(step < 0, step + GRID, step)
    step = jnp.where(step >= GRID, step - GRID, step)

    def spread(weights):
        out = jnp.zeros((GRID, lanes), F32)
        for a in range(4):
            out = jnp.where(step == a, jnp.broadcast_to(weights[a], (GRID, lanes)), out)
        return out

    if not with_slopes:
        return spread(values), None
    slopes = (
        -0.5 * remain * remain,
        1.5 * square - 2.0 * t,
        -1.5 * square + t + 0.5,
        0.5 * square,
    )
    return spread(values), spread(slopes)


def halves(first, second):
    product = jnp.concatenate([first[y : y + 1, :] * second for y in range(GRID)], axis=0)
    high = product.astype(BF16)
    return [high, (product - high.astype(F32)).astype(BF16)]


def fill(even_ref, odd_ref, pieces):
    lanes = pieces[0].shape[1]
    pad = jnp.zeros((WIDE - PLANE, lanes), BF16)
    for i, piece in enumerate(pieces):
        at = slice(i * lanes, (i + 1) * lanes)
        even_ref[0:PLANE, at] = piece
        even_ref[PLANE:WIDE, at] = pad
        odd_ref[0 : WIDE - PLANE, at] = pad
        odd_ref[WIDE - PLANE : WIDE, at] = piece


def plane_pair(table_ref, pair, even_ref, odd_ref):
    start = pl.multiple_of(pair * 2 * PLANE, 128)
    even = table_ref[:, pl.ds(start, WIDE)]
    start = pl.multiple_of(pair * 2 * PLANE + 2 * PLANE - WIDE, 128)
    odd = table_ref[:, pl.ds(start, WIDE)]
    return (
        jnp.dot(even, even_ref[...], preferred_element_type=F32),
        jnp.dot(odd, odd_ref[...], preferred_element_type=F32),
    )


def slopes_kernel(state_ref, table_ref, phi_ref, grad_ref, even_ref, odd_ref, wx_ref, sx_ref):
    n = state_ref.shape[1]
    wx, sx = axis_weights(state_ref[0:1, :], True)
    wy, sy = axis_weights(state_ref[1:2, :], True)
    wz, sz = axis_weights(state_ref[2:3, :], True)
    wx_ref[...] = wx
    sx_ref[...] = sx
    fill(even_ref, odd_ref, halves(wy, wz) + halves(sy, wz) + halves(wy, sz))
    phi_ref[...] = jnp.zeros_like(phi_ref)
    grad_ref[...] = jnp.zeros_like(grad_ref)

    def body(pair, carry):
        both = plane_pair(table_ref, pair, even_ref, odd_ref)
        for plane, x in zip(both, (2 * pair, 2 * pair + 1)):
            w = wx_ref[pl.ds(x, 1), :]
            s = sx_ref[pl.ds(x, 1), :]
            base = plane[:, 0:n] + plane[:, n : 2 * n]
            phi_ref[...] += w * base
            grad_ref[:, 0:n] += s * base
            grad_ref[:, n : 2 * n] += w * (plane[:, 2 * n : 3 * n] + plane[:, 3 * n : 4 * n])
            grad_ref[:, 2 * n : 3 * n] += w * (plane[:, 4 * n : 5 * n] + plane[:, 5 * n : 6 * n])
        return carry

    lax.fori_loop(0, GRID // 2, body, 0, unroll=4)


def slopes_call(state, table):
    orbitals = table.shape[0]
    n = state.shape[1]
    return pl.pallas_call(
        slopes_kernel,
        name="slopes",
        out_shape=(
            jax.ShapeDtypeStruct((orbitals, n), F32),
            jax.ShapeDtypeStruct((orbitals, 3 * n), F32),
        ),
        in_specs=[VMEM, VMEM],
        out_specs=(VMEM, VMEM),
        scratch_shapes=[
            pltpu.VMEM((WIDE, 6 * n), BF16),
            pltpu.VMEM((WIDE, 6 * n), BF16),
            pltpu.VMEM((GRID, n), F32),
            pltpu.VMEM((GRID, n), F32),
        ],
        compiler_params=pltpu.CompilerParams(vmem_limit_bytes=LIMIT),
    )(state, table)


def dot(a, b):
    return jnp.dot(a, b, precision=HIGHEST, preferred_element_type=F32)


def dot_nt(a, b):
    return lax.dot_general(
        a, b, (((1,), (1,)), ((), ())), precision=HIGHEST, preferred_element_type=F32
    )


def own_lanes(n, walker):
    lane = lax.broadcasted_iota(jnp.int32, (MOVED, n), 1)
    return jnp.logical_and(lane >= walker * K, lane < (walker + 1) * K)


def fold(big):
    n = big.shape[1]
    total = jnp.zeros((MOVED, n), F32)
    for w in range(n // K):
        total = jnp.where(own_lanes(n, w), big[w * MOVED : (w + 1) * MOVED, :], total)
    return total


def unit(block, n):
    row = lax.broadcasted_iota(jnp.int32, (MOVED, n), 0)
    lane = lax.broadcasted_iota(jnp.int32, (MOVED, n), 1)
    return jnp.where(row - block * K == lane % K, 1.0, 0.0).astype(F32)


def tree(parts):
    while len(parts) > 1:
        parts = [parts[i] + parts[i + 1] for i in range(0, len(parts), 2)]
    return parts[0]


def total(refs):
    return tree([ref[...] for ref in refs])


def drift_kernel(first, vm_ref, grad_ref, out_ref):
    n = grad_ref.shape[1] // 3
    for d in range(3):
        q = fold(dot(vm_ref[...], grad_ref[:, d * n : (d + 1) * n]))
        if first:
            out_ref[d : d + 1, :] = jnp.sum(q * unit(0, n), axis=0, keepdims=True)
        else:
            out_ref[d * MOVED : (d + 1) * MOVED, :] = q
    if first:
        out_ref[3:8, :] = jnp.zeros((5, n), F32)


def drift_call(first, vm, grad):
    n = grad.shape[1] // 3
    return pl.pallas_call(
        functools.partial(drift_kernel, first),
        name="drift",
        out_shape=jax.ShapeDtypeStruct((8 if first else 3 * MOVED, n), F32),
        in_specs=[VMEM, VMEM],
        out_specs=VMEM,
        compiler_params=pltpu.CompilerParams(vmem_limit_bytes=LIMIT),
    )(vm, grad)


def absorb(block, s, y_all, l_all, t):
    n = s.shape[1]
    u = s - fold(dot(y_all, s))
    r = unit(block, n) - fold(dot(l_all, s))

    def spread(x):
        return jnp.concatenate(
            [jnp.where(own_lanes(n, w), x, 0.0) for w in range(n // K)], axis=0
        )

    return y_all + dot_nt(spread(u), t), l_all + dot_nt(spread(r), t)


def step_kernel(block, shards, *refs):
    refs = list(refs)
    s_parts = [refs.pop(0) for _ in range(shards)]
    if block:
        q_parts = [refs.pop(0) for _ in range(shards)]
        y_ref, l_ref, t_ref = [refs.pop(0) for _ in range(3)]
    state_ref, phi_ref, vm_ref, table_ref = [refs.pop(0) for _ in range(4)]
    s_ref, moved_ref, d_ref, y_out, l_out, t_out = [refs.pop(0) for _ in range(6)]
    even_ref, odd_ref, wx_ref = refs
    n = state_ref.shape[1]
    if block == 0:
        drifts = total(s_parts)[0:3, :]
        t_out[...] = unit(0, n)
        y_out[...] = jnp.zeros_like(y_out)
        l_out[...] = jnp.zeros_like(l_out)
    else:
        y_all, l_all = absorb(block - 1, total(s_parts), y_ref[...], l_ref[...], t_ref[...])
        y_out[...] = y_all
        l_out[...] = l_all
        rows = jnp.concatenate(
            [
                y_all[w * MOVED + block * K : w * MOVED + (block + 1) * K, :]
                for w in range(n // K)
            ],
            axis=0,
        )
        t = unit(block, n) - jnp.transpose(rows)
        t_out[...] = t
        q = total(q_parts)
        drifts = jnp.concatenate(
            [
                jnp.sum(q[d * MOVED : (d + 1) * MOVED, :] * t, axis=0, keepdims=True)
                for d in range(3)
            ],
            axis=0,
        )
    speeds = jnp.sum(drifts * drifts, axis=0, keepdims=True)
    capped = drifts / jnp.sqrt(1.0 + TAU * speeds)
    moved = state_ref[0:3, :] + state_ref[6:7, :] * (TAU * capped + ROOT_TAU * state_ref[3:6, :])
    moved_ref[0:3, :] = moved
    moved_ref[3:8, :] = jnp.zeros((5, n), F32)
    wx, _ = axis_weights(moved[0:1, :], False)
    wy, _ = axis_weights(moved[1:2, :], False)
    wz, _ = axis_weights(moved[2:3, :], False)
    wx_ref[...] = wx
    fill(even_ref, odd_ref, halves(wy, wz))
    d_ref[...] = jnp.zeros_like(d_ref)

    def body(pair, carry):
        both = plane_pair(table_ref, pair, even_ref, odd_ref)
        for plane, x in zip(both, (2 * pair, 2 * pair + 1)):
            d_ref[...] += wx_ref[pl.ds(x, 1), :] * (plane[:, 0:n] + plane[:, n : 2 * n])
        return carry

    lax.fori_loop(0, GRID // 2, body, 0, unroll=4)
    change = d_ref[...] - phi_ref[...]
    d_ref[...] = change
    s_ref[...] = fold(dot(vm_ref[...], change))


def step_call(block, s_parts, q_parts, carried, state, phi, vm, table):
    n = state.shape[1]
    rows, orbitals = vm.shape
    operands = [*s_parts, *q_parts, *carried, state, phi, vm, table]
    shapes = [(MOVED, n), (8, n), (orbitals, n), (rows, MOVED), (rows, MOVED), (MOVED, n)]
    return pl.pallas_call(
        functools.partial(step_kernel, block, len(s_parts)),
        name="step",
        out_shape=tuple(jax.ShapeDtypeStruct(shape, F32) for shape in shapes),
        in_specs=[VMEM] * len(operands),
        out_specs=(VMEM,) * len(shapes),
        scratch_shapes=[
            pltpu.VMEM((WIDE, 2 * n), BF16),
            pltpu.VMEM((WIDE, 2 * n), BF16),
            pltpu.VMEM((GRID, n), F32),
        ],
        compiler_params=pltpu.CompilerParams(vmem_limit_bytes=LIMIT),
    )(*operands)


def last_kernel(shards, *refs):
    y_ref, l_ref, t_ref, vm_ref, out_ref = refs[shards:]
    n = t_ref.shape[1]
    _, l_all = absorb(NMOVE - 1, total(refs[:shards]), y_ref[...], l_ref[...], t_ref[...])
    for w in range(n // K):
        at = slice(w * MOVED, (w + 1) * MOVED)
        out_ref[w] = jnp.transpose(dot(l_all[at, :], vm_ref[at, :]))


def last_call(s_parts, carried, vm):
    rows, orbitals = vm.shape
    return pl.pallas_call(
        functools.partial(last_kernel, len(s_parts)),
        name="last",
        out_shape=jax.ShapeDtypeStruct((rows // MOVED, orbitals, MOVED), F32),
        in_specs=[VMEM] * (len(s_parts) + 4),
        out_specs=VMEM,
        compiler_params=pltpu.CompilerParams(vmem_limit_bytes=LIMIT),
    )(*s_parts, *carried, vm)


def sums_kernel(*refs):
    v_ref, out_ref = refs[NMOVE:]
    change = jnp.concatenate([jnp.transpose(ref[...]) for ref in refs[:NMOVE]], axis=0)
    n = refs[0].shape[1]
    for w in range(n // K):
        own = jnp.concatenate(
            [change[b * n + w * K : b * n + (w + 1) * K, :] for b in range(NMOVE)], axis=0
        )
        out_ref[w] = dot(own, v_ref[w])


def sums_call(changes, inverse):
    walkers, _, electrons = inverse.shape
    return pl.pallas_call(
        sums_kernel,
        name="sums",
        out_shape=jax.ShapeDtypeStruct((walkers, MOVED, electrons), F32),
        in_specs=[VMEM] * (NMOVE + 1),
        out_specs=VMEM,
        compiler_params=pltpu.CompilerParams(vmem_limit_bytes=LIMIT),
    )(*changes, inverse)


def update_kernel(v_ref, factor_ref, sums_ref, out_ref):
    out_ref[0] = v_ref[0] - dot(factor_ref[0], sums_ref[0])


def update_call(inverse, factor, sums):
    walkers, orbitals, electrons = inverse.shape
    return pl.pallas_call(
        update_kernel,
        name="update",
        grid=(walkers,),
        out_shape=jax.ShapeDtypeStruct(inverse.shape, F32),
        in_specs=[
            pl.BlockSpec((1, orbitals, electrons), lambda w: (w, 0, 0)),
            pl.BlockSpec((1, orbitals, MOVED), lambda w: (w, 0, 0)),
            pl.BlockSpec((1, MOVED, electrons), lambda w: (w, 0, 0)),
        ],
        out_specs=pl.BlockSpec((1, orbitals, electrons), lambda w: (w, 0, 0)),
        compiler_params=pltpu.CompilerParams(vmem_limit_bytes=LIMIT),
    )(inverse, factor, sums)


def exchange(part, axis):
    size = lax.axis_size(axis)
    others = [
        lax.ppermute(part, axis, [(i, i ^ k) for i in range(size)]) for k in range(1, size)
    ]
    return [part, *others]


def routing(everyone, own_parent, width, myself):
    groups = everyone.shape[0] // width
    listing = everyone.reshape(groups, width)
    source = listing // width
    within = listing % width
    target = lax.broadcasted_iota(jnp.int32, (groups, width), 0)
    mine = jnp.logical_and(source == myself, target != myself)
    sending = jnp.sum(jnp.where(mine, within, 0), axis=1)
    anchor = own_parent // width
    picking = jnp.where(anchor == myself, own_parent % width, width + anchor)
    return sending, picking


def fetch(holding, sending, picking):
    outgoing = jnp.take(holding, sending, axis=0)
    received = lax.all_to_all(outgoing, "walker", split_axis=0, concat_axis=0, tiled=True)
    return jnp.take(jnp.concatenate([holding, received], axis=0), picking, axis=0)


def local(positions, inverse, spline_table, gaussian, accepted, block_order, parent):
    myself = lax.axis_index("walker")
    walkers, _, electrons = positions.shape
    orbitals = inverse.shape[1]
    n = walkers * K
    columns = (block_order[:NMOVE, None] * K + jnp.arange(K, dtype=jnp.int32)).reshape(MOVED)
    chosen = (
        columns[:, None] == lax.broadcasted_iota(jnp.int32, (MOVED, electrons), 1)
    ).astype(F32)

    moving = jnp.einsum("wdn,mn->wdm", positions, chosen, precision=HIGHEST)
    info = jnp.concatenate(
        [
            moving,
            gaussian,
            accepted.astype(F32)[:, None, :],
            jnp.broadcast_to(parent.astype(F32)[:, None, None], (walkers, 1, MOVED)),
        ],
        axis=1,
    )
    everyone = lax.all_gather(info, "walker", axis=0, tiled=True)
    sending, picking = routing(everyone[:, 7, 0].astype(jnp.int32), parent, walkers, myself)
    states = jnp.take(everyone, parent, axis=0)
    states = jnp.transpose(states.reshape(walkers, 8, NMOVE, K), (2, 1, 0, 3))
    states = states.reshape(NMOVE, 8, n)

    own_vm = jnp.einsum("mn,wjn->wmj", chosen, inverse, precision=HIGHEST)
    vm = fetch(own_vm, sending, picking).reshape(walkers * MOVED, orbitals)
    whole = fetch(inverse, sending, picking)
    all_positions = lax.all_gather(positions, "walker", axis=0, tiled=True)
    resting = jnp.take(all_positions, parent, axis=0)

    evals = [slopes_call(states[b], spline_table) for b in range(NMOVE)]
    s_parts = exchange(drift_call(True, vm, evals[0][1]), "orb")
    q_parts = [[]] + [
        exchange(drift_call(False, vm, evals[b][1]), "orb") for b in range(1, NMOVE)
    ]
    carried = []
    moved = []
    changes = []
    for b in range(NMOVE):
        s, new, change, *carried = step_call(
            b, s_parts, q_parts[b], carried, states[b], evals[b][0], vm, spline_table
        )
        moved.append(new[0:3].reshape(3, walkers, K))
        changes.append(change)
        s_parts = exchange(s, "orb")
    factor = last_call(s_parts, carried, vm)
    sums = lax.psum(sums_call(changes, whole), "orb")
    new_inverse = update_call(whole, factor, sums)

    fresh = jnp.transpose(jnp.stack(moved), (2, 1, 0, 3)).reshape(walkers, 3, MOVED)
    placed = jnp.einsum("wdm,mn->wdn", fresh, chosen, precision=HIGHEST)
    touched = jnp.sum(chosen, axis=0) > 0.0
    return jnp.where(touched, placed, resting), new_inverse


def solution(mesh):
    return jax.shard_map(
        local,
        mesh=mesh,
        in_specs=(
            P("walker", None, None),
            P("walker", "orb", None),
            P("orb", None),
            P("walker", None, None),
            P("walker", None),
            P(),
            P("walker"),
        ),
        out_specs=(P("walker", None, None), P("walker", "orb", None)),
        check_vma=False,
    )
```

```python
import functools

import jax
import jax.numpy as jnp
from jax import lax
from jax.experimental import pallas as pl
from jax.experimental.pallas import tpu as pltpu
from jax.sharding import PartitionSpec as P

GRID = 24
PLANE = GRID * GRID
WIDE = 640
UNROLL = 4
K = 16
NMOVE = 4
MOVED = K * NMOVE
CAP = 1
TAU = 0.25
ROOT_TAU = 0.5
F32 = jnp.float32
BF16 = jnp.bfloat16
LEVELS = 32767.0
HIGHEST = lax.Precision.HIGHEST
VMEM = pl.BlockSpec(memory_space=pltpu.VMEM)
SMEM = pl.BlockSpec(memory_space=pltpu.SMEM)
LIMIT = 16 * 2**20


def axis_weights(u, with_slopes):
    floors = jnp.floor(u)
    t = u - floors
    remain = 1.0 - t
    square = t * t
    cubed = square * t
    values = (
        remain * remain * remain / 6.0,
        (3.0 * cubed - 6.0 * square + 4.0) / 6.0,
        (-3.0 * cubed + 3.0 * square + 3.0 * t + 1.0) / 6.0,
        cubed / 6.0,
    )
    lanes = u.shape[1]
    line = lax.broadcasted_iota(jnp.int32, (GRID, lanes), 0)
    step = line - (floors.astype(jnp.int32) - 1)
    step = jnp.where(step < 0, step + GRID, step)
    step = jnp.where(step < 0, step + GRID, step)
    step = jnp.where(step >= GRID, step - GRID, step)

    def spread(weights):
        out = jnp.zeros((GRID, lanes), F32)
        for a in range(4):
            out = jnp.where(step == a, jnp.broadcast_to(weights[a], (GRID, lanes)), out)
        return out

    if not with_slopes:
        return spread(values), None
    slopes = (
        -0.5 * remain * remain,
        1.5 * square - 2.0 * t,
        -1.5 * square + t + 0.5,
        0.5 * square,
    )
    return spread(values), spread(slopes)


def halves(first, second):
    product = jnp.concatenate([first[y : y + 1, :] * second for y in range(GRID)], axis=0)
    high = product.astype(BF16)
    return [high, (product - high.astype(F32)).astype(BF16)]


def fill(even_ref, odd_ref, pieces):
    lanes = pieces[0].shape[1]
    pad = jnp.zeros((WIDE - PLANE, lanes), BF16)
    for i, piece in enumerate(pieces):
        at = slice(i * lanes, (i + 1) * lanes)
        even_ref[0:PLANE, at] = piece
        even_ref[PLANE:WIDE, at] = pad
        odd_ref[0 : WIDE - PLANE, at] = pad
        odd_ref[WIDE - PLANE : WIDE, at] = piece


def plane_pair(table_ref, pair, even_ref, odd_ref):
    start = pl.multiple_of(pair * 2 * PLANE, 128)
    even = table_ref[:, pl.ds(start, WIDE)]
    start = pl.multiple_of(pair * 2 * PLANE + 2 * PLANE - WIDE, 128)
    odd = table_ref[:, pl.ds(start, WIDE)]
    return (
        jnp.dot(even, even_ref[...], preferred_element_type=F32),
        jnp.dot(odd, odd_ref[...], preferred_element_type=F32),
    )


def slopes_kernel(state_ref, table_ref, phi_ref, grad_ref, even_ref, odd_ref, wx_ref, sx_ref):
    n = state_ref.shape[1]
    wx, sx = axis_weights(state_ref[0:1, :], True)
    wy, sy = axis_weights(state_ref[1:2, :], True)
    wz, sz = axis_weights(state_ref[2:3, :], True)
    wx_ref[...] = wx
    sx_ref[...] = sx
    fill(even_ref, odd_ref, halves(wy, wz) + halves(sy, wz) + halves(wy, sz))
    phi_ref[...] = jnp.zeros_like(phi_ref)
    grad_ref[...] = jnp.zeros_like(grad_ref)

    def body(pair, carry):
        even, odd = plane_pair(table_ref, pair, even_ref, odd_ref)
        w0, w1 = wx_ref[pl.ds(2 * pair, 1), :], wx_ref[pl.ds(2 * pair + 1, 1), :]
        s0, s1 = sx_ref[pl.ds(2 * pair, 1), :], sx_ref[pl.ds(2 * pair + 1, 1), :]

        def both(i):
            at, to = slice(2 * i * n, (2 * i + 1) * n), slice((2 * i + 1) * n, (2 * i + 2) * n)
            return even[:, at] + even[:, to], odd[:, at] + odd[:, to]

        e, o = both(0)
        phi_ref[...] += w0 * e + w1 * o
        grad_ref[:, 0:n] += s0 * e + s1 * o
        for d in (1, 2):
            e, o = both(d)
            grad_ref[:, d * n : (d + 1) * n] += w0 * e + w1 * o
        return carry

    lax.fori_loop(0, GRID // 2, body, 0, unroll=UNROLL)


def slopes_call(state, table):
    orbitals = table.shape[0]
    n = state.shape[1]
    return pl.pallas_call(
        slopes_kernel,
        name="slopes",
        out_shape=(
            jax.ShapeDtypeStruct((orbitals, n), F32),
            jax.ShapeDtypeStruct((orbitals, 3 * n), F32),
        ),
        in_specs=[VMEM, VMEM],
        out_specs=(VMEM, VMEM),
        scratch_shapes=[
            pltpu.VMEM((WIDE, 6 * n), BF16),
            pltpu.VMEM((WIDE, 6 * n), BF16),
            pltpu.VMEM((GRID, n), F32),
            pltpu.VMEM((GRID, n), F32),
        ],
        compiler_params=pltpu.CompilerParams(vmem_limit_bytes=LIMIT),
    )(state, table)


def dot(a, b):
    return jnp.dot(a, b, precision=HIGHEST, preferred_element_type=F32)


def dot_nt(a, b):
    return lax.dot_general(
        a, b, (((1,), (1,)), ((), ())), precision=HIGHEST, preferred_element_type=F32
    )


def own_lanes(n, walker):
    lane = lax.broadcasted_iota(jnp.int32, (MOVED, n), 1)
    return jnp.logical_and(lane >= walker * K, lane < (walker + 1) * K)


def fold(big):
    n = big.shape[1]
    total = jnp.zeros((MOVED, n), F32)
    for w in range(n // K):
        total = jnp.where(own_lanes(n, w), big[w * MOVED : (w + 1) * MOVED, :], total)
    return total


def unit(block, n):
    row = lax.broadcasted_iota(jnp.int32, (MOVED, n), 0)
    lane = lax.broadcasted_iota(jnp.int32, (MOVED, n), 1)
    return jnp.where(row - block * K == lane % K, 1.0, 0.0).astype(F32)


def tree(parts):
    while len(parts) > 1:
        parts = [parts[i] + parts[i + 1] for i in range(0, len(parts), 2)]
    return parts[0]


def total(refs):
    return tree([ref[...] for ref in refs])


def params(limit=LIMIT):
    return pltpu.CompilerParams(vmem_limit_bytes=limit)


def parent_of(meta_ref, walkers, w):
    parent = meta_ref[w]
    group = parent // walkers
    here = group == meta_ref[walkers + NMOVE]
    return here, jnp.where(here, parent % walkers, 0), jnp.where(here, 0, group)


def block_lanes(x, block):
    lane = lax.broadcasted_iota(jnp.int32, x.shape, 1)
    kept = jnp.where(lane // K == block, x, 0.0)
    return tree([kept[:, i : i + 128] for i in range(0, x.shape[1], 128)])


def roll(x, shift):
    if isinstance(shift, int):
        shift = shift % 128
        return x if shift == 0 else pltpu.roll(x, shift, 1)
    return pltpu.roll(x, lax.rem(shift + 1024, 128), 1)


def pack_kernel(meta_ref, pos_ref, gauss_ref, acc_ref, out_ref):
    walkers = pos_ref.shape[0]
    half = jnp.zeros((3, MOVED), F32)
    lane = lax.broadcasted_iota(jnp.int32, (1, 128), 1)
    for w in range(walkers):
        line = jnp.concatenate([half, gauss_ref[w]], axis=1)
        for b in range(NMOVE):
            block = meta_ref[walkers + b]
            line = line + roll(block_lanes(pos_ref[w], block), (b - block) * K)
        decided = acc_ref[w : w + 1, :].astype(F32)
        decided = jnp.concatenate([decided, jnp.zeros((1, 128 - MOVED), F32)], axis=1)
        decided = jnp.where(lane < MOVED, decided, meta_ref[w].astype(F32))
        for g in range(out_ref.shape[0]):
            out_ref[g, 4 * w : 4 * w + 3, :] = line
            out_ref[g, 4 * w + 3 : 4 * w + 4, :] = decided


def pack_call(meta, positions, gaussian, accepted, groups):
    walkers = positions.shape[0]
    return pl.pallas_call(
        pack_kernel,
        name="pack",
        out_shape=jax.ShapeDtypeStruct((groups, 4 * walkers, 128), F32),
        in_specs=[SMEM, VMEM, VMEM, VMEM],
        out_specs=VMEM,
        compiler_params=params(),
    )(meta, positions, gaussian, accepted)


def columns_kernel(meta_ref, v_ref, pos_ref, out_ref, code_ref):
    walkers = meta_ref.shape[0] - NMOVE - 1
    v = v_ref[0]
    orbitals, electrons = v.shape
    row = lax.broadcasted_iota(jnp.int32, (K, electrons), 0)
    column = lax.broadcasted_iota(jnp.int32, (K, electrons), 1)
    chosen = jnp.concatenate(
        [
            jnp.where(column - meta_ref[walkers + b] * K == row, 1.0, 0.0).astype(F32)
            for b in range(NMOVE)
        ],
        axis=0,
    )
    out_ref[0, 0:MOVED, :] = dot_nt(chosen, v)
    size = jnp.abs(v)
    scale = jnp.max(size, axis=0, keepdims=True)
    at = MOVED
    for line in [scale] + [pos_ref[0, d : d + 1, :] for d in range(3)]:
        for i in range(0, electrons, orbitals):
            out_ref[0, at : at + 1, :] = line[:, i : i + orbitals]
            at += 1
    step = jnp.where(scale > 0.0, LEVELS / jnp.sqrt(jnp.where(scale > 0.0, scale, 1.0)), 0.0)
    level = jnp.minimum(jnp.floor(jnp.sqrt(size) * step + 0.5), LEVELS)
    code_ref[0] = jnp.where(v < 0.0, -level, level).astype(jnp.int32).astype(jnp.int16)


def payload_rows(orbitals, electrons):
    return MOVED + 4 * electrons // orbitals


def columns_call(meta, inverse, positions):
    walkers, orbitals, electrons = inverse.shape
    rows = payload_rows(orbitals, electrons)
    return pl.pallas_call(
        columns_kernel,
        name="columns",
        grid_spec=pltpu.PrefetchScalarGridSpec(
            num_scalar_prefetch=1,
            grid=(walkers,),
            in_specs=[
                pl.BlockSpec((1, orbitals, electrons), lambda w, m: (w, 0, 0)),
                pl.BlockSpec((1, 3, electrons), lambda w, m: (w, 0, 0)),
            ],
            out_specs=(
                pl.BlockSpec((1, rows, orbitals), lambda w, m: (w, 0, 0)),
                pl.BlockSpec((1, orbitals, electrons), lambda w, m: (w, 0, 0)),
            ),
        ),
        out_shape=(
            jax.ShapeDtypeStruct((walkers, rows, orbitals), F32),
            jax.ShapeDtypeStruct(inverse.shape, jnp.int16),
        ),
        compiler_params=params(),
    )(meta, inverse, positions)


def route_kernel(meta_ref, info_ref, own_ref, states_ref, out_ref, sending_ref):
    walkers = own_ref.shape[0]
    groups = out_ref.shape[0]
    me = meta_ref[walkers + NMOVE]
    lane = lax.broadcasted_iota(jnp.int32, (4, 128), 1)
    lines = [info_ref[pl.ds(4 * meta_ref[w], 4), :] for w in range(walkers)]
    for b in range(NMOVE):
        for half in range(2):
            total = jnp.zeros((4, 128), F32)
            for w in range(walkers):
                moved = roll(lines[w], (w - b) * K - half * MOVED)
                total = jnp.where(lane // K == w, moved, total)
            states_ref[b, 4 * half : 4 * half + 4, :] = total
    for g in range(groups):
        wanted = jnp.zeros((1, 128), jnp.int32)
        for s in range(walkers):
            row = 4 * (g * walkers + s) + 3
            parent = info_ref[row : row + 1, :].astype(jnp.int32)
            parent = jnp.where(lane[0:1] < MOVED, pltpu.roll(parent, 128 - MOVED, 1), parent)
            within = parent - me * walkers
            wanted = jnp.where(
                jnp.logical_and(within >= 0, within < walkers), within, wanted
            )
        wanted = jnp.where(me == g, 0, wanted)
        sending_ref[g : g + 1, :] = wanted
        picked = wanted[:, 0 : own_ref.shape[2]]
        total = own_ref[0]
        for w in range(1, walkers):
            total = jnp.where(picked == w, own_ref[w], total)
        out_ref[g] = total


def route_call(meta, info, own):
    walkers, rows, orbitals = own.shape
    groups = info.shape[0] // (4 * walkers)
    return pl.pallas_call(
        route_kernel,
        name="route",
        out_shape=(
            jax.ShapeDtypeStruct((NMOVE, 8, 128), F32),
            jax.ShapeDtypeStruct((groups, rows, orbitals), F32),
            jax.ShapeDtypeStruct((groups, 128), jnp.int32),
        ),
        in_specs=[SMEM, VMEM, VMEM],
        out_specs=(VMEM, VMEM, VMEM),
        compiler_params=params(),
    )(meta, info, own)


def select_kernel(meta_ref, own_ref, got_ref, grad_ref, vm_ref, out_ref):
    walkers = own_ref.shape[0]
    for w in range(walkers):
        here, place, group = parent_of(meta_ref, walkers, w)
        vm_ref[w * MOVED : (w + 1) * MOVED, :] = jnp.where(
            here, own_ref[place, 0:MOVED, :], got_ref[group, 0:MOVED, :]
        )
    n = grad_ref.shape[1] // 3
    for d in range(3):
        q = fold(dot(vm_ref[...], grad_ref[:, d * n : (d + 1) * n]))
        out_ref[d : d + 1, :] = jnp.sum(q * unit(0, n), axis=0, keepdims=True)
    out_ref[3:8, :] = jnp.zeros((5, n), F32)


def select_call(meta, own, got, grad):
    walkers, _, orbitals = own.shape
    n = grad.shape[1] // 3
    return pl.pallas_call(
        select_kernel,
        name="select",
        out_shape=(
            jax.ShapeDtypeStruct((walkers * MOVED, orbitals), F32),
            jax.ShapeDtypeStruct((8, n), F32),
        ),
        in_specs=[SMEM, VMEM, VMEM, VMEM],
        out_specs=(VMEM, VMEM),
        compiler_params=params(),
    )(meta, own, got, grad)


def drift_kernel(vm_ref, grad_ref, out_ref):
    n = grad_ref.shape[1] // 3
    rows = out_ref.shape[0] // 3
    for d in range(3):
        q = fold(dot(vm_ref[...], grad_ref[:, d * n : (d + 1) * n]))
        out_ref[d * rows : (d + 1) * rows, :] = q[0:rows, :]


def drift_call(block, vm, grad):
    n = grad.shape[1] // 3
    return pl.pallas_call(
        drift_kernel,
        name="drift",
        out_shape=jax.ShapeDtypeStruct((3 * (block + 1) * K, n), F32),
        in_specs=[VMEM, VMEM],
        out_specs=VMEM,
        compiler_params=params(),
    )(vm, grad)


def spread(x):
    n = x.shape[1]
    return jnp.concatenate([jnp.where(own_lanes(n, w), x, 0.0) for w in range(n // K)], axis=0)


def step_kernel(block, shards, *refs):
    refs = list(refs)
    s_parts = [refs.pop(0) for _ in range(shards)]
    if block:
        q_parts = [refs.pop(0) for _ in range(shards)]
        t_before = refs.pop(0)
    if block > 1:
        y_before = refs.pop(0)
    states_ref, phi_ref, vm_ref, table_ref = [refs.pop(0) for _ in range(4)]
    s_ref, moved_ref, d_ref, t_ref = [refs.pop(0) for _ in range(4)]
    y_ref = refs.pop(0) if block else None
    sum_ref, big_ref, even_ref, odd_ref, wx_ref = refs
    n = phi_ref.shape[1]
    state = states_ref[block]
    if block == 0:
        drifts = total(s_parts)[0:3, :]
        t_ref[...] = unit(0, n)
    else:
        s = total(s_parts)
        if block > 1:
            s_ref[...] = s
            big_ref[...] = dot(y_before[...], s_ref[...])
            s = s - fold(big_ref[...])
        s_ref[...] = s
        y_all = dot_nt(spread(s_ref[...]), t_before[...])
        if block > 1:
            y_all = y_all + y_before[...]
        y_ref[...] = y_all
        rows = jnp.concatenate(
            [
                y_ref[w * MOVED + block * K : w * MOVED + (block + 1) * K, :]
                for w in range(n // K)
            ],
            axis=0,
        )
        t_ref[...] = unit(block, n) - jnp.transpose(rows)
        t = t_ref[...]
        q = total(q_parts)
        size = q.shape[0] // 3
        drifts = jnp.concatenate(
            [
                jnp.sum(q[d * size : (d + 1) * size, :] * t[0:size, :], axis=0, keepdims=True)
                for d in range(3)
            ],
            axis=0,
        )
    speeds = jnp.sum(drifts * drifts, axis=0, keepdims=True)
    capped = drifts / jnp.sqrt(1.0 + TAU * speeds)
    moved = state[0:3, :] + state[3:4, :] * (TAU * capped + ROOT_TAU * state[4:7, :])
    moved_ref[0:3, :] = moved
    moved_ref[3:8, :] = jnp.zeros((5, n), F32)
    wx, _ = axis_weights(moved[0:1, :], False)
    wy, _ = axis_weights(moved[1:2, :], False)
    wz, _ = axis_weights(moved[2:3, :], False)
    wx_ref[...] = wx
    fill(even_ref, odd_ref, halves(wy, wz))
    sum_ref[...] = jnp.zeros_like(sum_ref)

    def body(pair, carry):
        even, odd = plane_pair(table_ref, pair, even_ref, odd_ref)
        w0, w1 = wx_ref[pl.ds(2 * pair, 1), :], wx_ref[pl.ds(2 * pair + 1, 1), :]
        sum_ref[...] += w0 * (even[:, 0:n] + even[:, n:]) + w1 * (odd[:, 0:n] + odd[:, n:])
        return carry

    lax.fori_loop(0, GRID // 2, body, 0, unroll=UNROLL)
    change = sum_ref[...] - phi_ref[...]
    d_ref[...] = jnp.transpose(change)
    s_ref[...] = fold(dot(vm_ref[...], change))


def step_call(block, s_parts, q_parts, carried, states, phi, vm, table):
    orbitals, n = phi.shape
    rows = vm.shape[0]
    operands = [*s_parts, *q_parts, *carried, states, phi, vm, table]
    shapes = [(MOVED, n), (8, n), (n, orbitals), (MOVED, n)] + [(rows, MOVED)] * (block > 0)
    return pl.pallas_call(
        functools.partial(step_kernel, block, len(s_parts)),
        name="step",
        out_shape=tuple(jax.ShapeDtypeStruct(shape, F32) for shape in shapes),
        in_specs=[VMEM] * len(operands),
        out_specs=(VMEM,) * len(shapes),
        scratch_shapes=[
            pltpu.VMEM((orbitals, n), F32),
            pltpu.VMEM((rows, n), F32),
            pltpu.VMEM((WIDE, 2 * n), BF16),
            pltpu.VMEM((WIDE, 2 * n), BF16),
            pltpu.VMEM((GRID, n), F32),
        ],
        compiler_params=params(),
    )(*operands)


def last_kernel(shards, *refs):
    l_all = None
    for block in range(NMOVE):
        t = refs[NMOVE * shards + block][...]
        r = unit(block, t.shape[1])
        if block:
            r = r - fold(dot(l_all, total(refs[block * shards : (block + 1) * shards])))
        more = dot_nt(spread(r), t)
        l_all = l_all + more if block else more
    vm_ref, out_ref = refs[NMOVE * (shards + 1) :]
    for w in range(out_ref.shape[0]):
        at = slice(w * MOVED, (w + 1) * MOVED)
        out_ref[w] = jnp.transpose(dot(l_all[at, :], vm_ref[at, :]))


def last_call(s_parts, ts, vm):
    rows, orbitals = vm.shape
    operands = [part for parts in s_parts for part in parts] + list(ts) + [vm]
    return pl.pallas_call(
        functools.partial(last_kernel, len(s_parts[0])),
        name="last",
        out_shape=jax.ShapeDtypeStruct((rows // MOVED, orbitals, MOVED), F32),
        in_specs=[VMEM] * len(operands),
        out_specs=VMEM,
        compiler_params=params(),
    )(*operands)


def assemble_kernel(meta_ref, own_ref, code_ref, got_ref, *refs):
    v_ref, out_ref = refs[NMOVE - 1 :]
    walkers = meta_ref.shape[0] - NMOVE - 1
    here, _, _ = parent_of(meta_ref, walkers, pl.program_id(0))
    _, orbitals, electrons = own_ref.shape
    scale = jnp.concatenate(
        [got_ref[0, MOVED + i : MOVED + i + 1, :] for i in range(electrons // orbitals)], axis=1
    )
    level = code_ref[0].astype(jnp.int32).astype(F32) * (1.0 / LEVELS)
    v = jnp.where(here, own_ref[0], level * jnp.abs(level) * scale)
    v_ref[0] = v
    change = jnp.concatenate([ref[...] for ref in refs[: NMOVE - 1]], axis=0)
    out_ref[0] = dot(change, v)


def assemble_call(meta, inverse, code, got, changes):
    walkers, orbitals, electrons = inverse.shape
    rows = got.shape[1]

    def near(w, m):
        return parent_of(m, walkers, w)[1], 0, 0

    def far(w, m):
        return parent_of(m, walkers, w)[2], 0, 0

    return pl.pallas_call(
        assemble_kernel,
        name="assemble",
        grid_spec=pltpu.PrefetchScalarGridSpec(
            num_scalar_prefetch=1,
            grid=(walkers,),
            in_specs=[
                pl.BlockSpec((1, orbitals, electrons), near),
                pl.BlockSpec((1, orbitals, electrons), far),
                pl.BlockSpec((1, rows, orbitals), far),
            ]
            + [pl.BlockSpec((K, orbitals), lambda w, m: (w, 0))] * (NMOVE - 1),
            out_specs=(
                pl.BlockSpec((1, orbitals, electrons), lambda w, m: (w, 0, 0)),
                pl.BlockSpec((1, (NMOVE - 1) * K, electrons), lambda w, m: (w, 0, 0)),
            ),
        ),
        out_shape=(
            jax.ShapeDtypeStruct(inverse.shape, F32),
            jax.ShapeDtypeStruct((walkers, (NMOVE - 1) * K, electrons), F32),
        ),
        compiler_params=params(),
    )(meta, inverse, code, got, *changes)


def sums_kernel(v_ref, change_ref, out_ref):
    out_ref[0] = dot(change_ref[...], v_ref[0])


def sums_call(inverse, change):
    walkers, orbitals, electrons = inverse.shape
    return pl.pallas_call(
        sums_kernel,
        name="sums",
        grid=(walkers,),
        out_shape=jax.ShapeDtypeStruct((walkers, K, electrons), F32),
        in_specs=[
            pl.BlockSpec((1, orbitals, electrons), lambda w: (w, 0, 0)),
            pl.BlockSpec((K, orbitals), lambda w: (w, 0)),
        ],
        out_specs=pl.BlockSpec((1, K, electrons), lambda w: (w, 0, 0)),
        compiler_params=params(),
    )(inverse, change)


def update_kernel(v_ref, factor_ref, first_ref, second_ref, out_ref):
    sums = jnp.concatenate([first_ref[0], second_ref[0]], axis=0)
    out_ref[0] = v_ref[0] - dot(factor_ref[0], sums)


def update_call(inverse, factor, first, second):
    walkers, orbitals, electrons = inverse.shape

    def per_walker(shape):
        return pl.BlockSpec((1, *shape[1:]), lambda w: (w, 0, 0))

    return pl.pallas_call(
        update_kernel,
        name="update",
        grid=(walkers,),
        out_shape=jax.ShapeDtypeStruct(inverse.shape, F32),
        in_specs=[per_walker(x.shape) for x in (inverse, factor, first, second)],
        out_specs=per_walker(inverse.shape),
        compiler_params=params(),
    )(inverse, factor, first, second)


def place_kernel(meta_ref, own_ref, got_ref, *refs):
    out_ref = refs[NMOVE]
    walkers, _, electrons = own_ref.shape
    width = got_ref.shape[2]
    parts = electrons // width
    lane = lax.broadcasted_iota(jnp.int32, (1, electrons), 1)
    for w in range(walkers):
        here, place, group = parent_of(meta_ref, walkers, w)
        lines = []
        for d in range(3):
            at = MOVED + (d + 1) * parts
            lines.append(
                jnp.concatenate(
                    [got_ref[group, at + i : at + i + 1, :] for i in range(parts)], axis=1
                )
            )
        line = jnp.where(here, own_ref[place], jnp.concatenate(lines, axis=0))
        for b in range(NMOVE):
            block = meta_ref[walkers + b]
            fresh = roll(refs[b][...], (block - w) * K)[0:3, :]
            fresh = jnp.concatenate([fresh] * (electrons // 128), axis=1)
            line = jnp.where(lane // K == block, fresh, line)
        out_ref[w] = line


def place_call(meta, positions, got, moved):
    return pl.pallas_call(
        place_kernel,
        name="place",
        out_shape=jax.ShapeDtypeStruct(positions.shape, F32),
        in_specs=[SMEM] + [VMEM] * (2 + NMOVE),
        out_specs=VMEM,
        compiler_params=params(),
    )(meta, positions, got, *moved)


def swap(x, axis, k):
    return lax.ppermute(x, axis, [(i, i ^ k) for i in range(lax.axis_size(axis))])


def exchange(part, axis):
    return [part] + [swap(part, axis, k) for k in range(1, lax.axis_size(axis))]


def add_up(part, axis):
    size = lax.axis_size(axis)
    half = part.shape[0] // 2
    low = lax.rem(lax.axis_index(axis), 2) == 0
    first, second = part[:half], part[half:]
    mine = jnp.where(low, first, second) + swap(jnp.where(low, second, first), axis, 1)
    k = 2
    while k < size:
        mine = mine + swap(mine, axis, k)
        k *= 2
    other = swap(mine, axis, 1)
    return jnp.concatenate([jnp.where(low, mine, other), jnp.where(low, other, mine)], axis=0)


def alltoall(x):
    return lax.all_to_all(x, "walker", split_axis=0, concat_axis=0, tiled=True)


def local(positions, inverse, spline_table, gaussian, accepted, block_order, parent):
    groups = lax.axis_size("walker")
    me = lax.axis_index("walker").astype(jnp.int32)
    meta = jnp.concatenate([parent, block_order[:NMOVE], me[None]])

    info = alltoall(pack_call(meta, positions, gaussian, accepted, groups))
    own, code = columns_call(meta, inverse, positions)
    states, outgoing, sending = route_call(meta, info.reshape(-1, 128), own)
    got = alltoall(outgoing)
    code = alltoall(code.at[sending[:, 0]].get(mode="promise_in_bounds"))

    evals = [slopes_call(states[b], spline_table) for b in range(NMOVE)]
    vm, first = select_call(meta, own, got, evals[0][1])
    s_parts = [exchange(first, "orb")]
    q_parts = [[]] + [
        exchange(drift_call(b, vm, evals[b][1]), "orb") for b in range(1, NMOVE)
    ]
    carried = []
    moved = []
    changes = []
    ts = []
    for b in range(NMOVE):
        s, new, change, t, *ys = step_call(
            b, s_parts[b], q_parts[b], carried, states, evals[b][0], vm, spline_table
        )
        carried = [t, *ys]
        ts.append(t)
        moved.append(new)
        changes.append(change)
        s_parts.append(exchange(s, "orb"))
        if b == NMOVE - 2:
            whole, sums = assemble_call(meta, inverse, code, got, changes)
            early = add_up(sums, "orb")
    late = add_up(sums_call(whole, changes[-1]), "orb")
    factor = last_call(s_parts[1:], ts, vm)
    return place_call(meta, positions, got, moved), update_call(whole, factor, early, late)


def solution(mesh):
    return jax.shard_map(
        local,
        mesh=mesh,
        in_specs=(
            P("walker", None, None),
            P("walker", "orb", None),
            P("orb", None),
            P("walker", None, None),
            P("walker", None),
            P(),
            P("walker"),
        ),
        out_specs=(P("walker", None, None), P("walker", "orb", None)),
        check_vma=False,
    )
```

```python
import functools

import jax
import jax.numpy as jnp
from jax import lax
from jax.experimental import pallas as pl
from jax.experimental.pallas import tpu as pltpu
from jax.sharding import PartitionSpec as P

GRID = 24
PLANE = GRID * GRID
WIDE = 640
UNROLL = 12
K = 16
NMOVE = 4
MOVED = K * NMOVE
CAP = 1
TAU = 0.25
ROOT_TAU = 0.5
F32 = jnp.float32
BF16 = jnp.bfloat16
LEVELS = 32767.0
HIGHEST = lax.Precision.HIGHEST
VMEM = pl.BlockSpec(memory_space=pltpu.VMEM)
SMEM = pl.BlockSpec(memory_space=pltpu.SMEM)
ANY = pl.BlockSpec(memory_space=pl.ANY)
LIMIT = 16 * 2**20


def axis_weights(u, with_slopes):
    floors = jnp.floor(u)
    t = u - floors
    remain = 1.0 - t
    square = t * t
    cubed = square * t
    values = (
        remain * remain * remain / 6.0,
        (3.0 * cubed - 6.0 * square + 4.0) / 6.0,
        (-3.0 * cubed + 3.0 * square + 3.0 * t + 1.0) / 6.0,
        cubed / 6.0,
    )
    lanes = u.shape[1]
    line = lax.broadcasted_iota(jnp.int32, (GRID, lanes), 0)
    step = line - (floors.astype(jnp.int32) - 1)
    step = jnp.where(step < 0, step + GRID, step)
    step = jnp.where(step < 0, step + GRID, step)
    step = jnp.where(step >= GRID, step - GRID, step)

    def spread(weights):
        out = jnp.zeros((GRID, lanes), F32)
        for a in range(4):
            out = jnp.where(step == a, jnp.broadcast_to(weights[a], (GRID, lanes)), out)
        return out

    if not with_slopes:
        return spread(values), None
    slopes = (
        -0.5 * remain * remain,
        1.5 * square - 2.0 * t,
        -1.5 * square + t + 0.5,
        0.5 * square,
    )
    return spread(values), spread(slopes)


def halves(first, second):
    product = jnp.concatenate([first[y : y + 1, :] * second for y in range(GRID)], axis=0)
    high = product.astype(BF16)
    return [high, (product - high.astype(F32)).astype(BF16)]


def fill(even_ref, odd_ref, pieces):
    lanes = pieces[0].shape[1]
    pad = jnp.zeros((WIDE - PLANE, lanes), BF16)
    for i, piece in enumerate(pieces):
        at = slice(i * lanes, (i + 1) * lanes)
        even_ref[0:PLANE, at] = piece
        even_ref[PLANE:WIDE, at] = pad
        odd_ref[0 : WIDE - PLANE, at] = pad
        odd_ref[WIDE - PLANE : WIDE, at] = piece


def plane_pair(table_ref, pair, even_ref, odd_ref):
    start = pl.multiple_of(pair * 2 * PLANE, 128)
    even = table_ref[:, pl.ds(start, WIDE)]
    start = pl.multiple_of(pair * 2 * PLANE + 2 * PLANE - WIDE, 128)
    odd = table_ref[:, pl.ds(start, WIDE)]
    return (
        jnp.dot(even, even_ref[...], preferred_element_type=F32),
        jnp.dot(odd, odd_ref[...], preferred_element_type=F32),
    )


def slopes_kernel(state_ref, table_ref, phi_ref, grad_ref, even_ref, odd_ref, wx_ref, sx_ref):
    n = state_ref.shape[2]
    wx, sx = axis_weights(state_ref[0, 0:1, :], True)
    wy, sy = axis_weights(state_ref[0, 1:2, :], True)
    wz, sz = axis_weights(state_ref[0, 2:3, :], True)
    wx_ref[...] = wx
    sx_ref[...] = sx
    fill(even_ref, odd_ref, halves(wy, wz) + halves(sy, wz) + halves(wy, sz))
    phi_ref[...] = jnp.zeros_like(phi_ref)
    grad_ref[...] = jnp.zeros_like(grad_ref)

    def body(pair, carry):
        even, odd = plane_pair(table_ref, pair, even_ref, odd_ref)
        w0, w1 = wx_ref[pl.ds(2 * pair, 1), :], wx_ref[pl.ds(2 * pair + 1, 1), :]
        s0, s1 = sx_ref[pl.ds(2 * pair, 1), :], sx_ref[pl.ds(2 * pair + 1, 1), :]

        def both(i):
            at, to = slice(2 * i * n, (2 * i + 1) * n), slice((2 * i + 1) * n, (2 * i + 2) * n)
            return even[:, at] + even[:, to], odd[:, at] + odd[:, to]

        e, o = both(0)
        phi_ref[...] += w0 * e + w1 * o
        grad_ref[:, 0:n] += s0 * e + s1 * o
        for d in (1, 2):
            e, o = both(d)
            grad_ref[:, d * n : (d + 1) * n] += w0 * e + w1 * o
        return carry

    lax.fori_loop(0, GRID // 2, body, 0, unroll=UNROLL)


def slopes_call(states, table, blocks):
    orbitals = table.shape[0]
    n = states.shape[2]
    return pl.pallas_call(
        slopes_kernel,
        name="slopes",
        grid=(blocks,),
        out_shape=(
            jax.ShapeDtypeStruct((blocks * orbitals, n), F32),
            jax.ShapeDtypeStruct((blocks * orbitals, 3 * n), F32),
        ),
        in_specs=[pl.BlockSpec((1, 8, n), lambda b: (b, 0, 0)), VMEM],
        out_specs=(
            pl.BlockSpec((orbitals, n), lambda b: (b, 0)),
            pl.BlockSpec((orbitals, 3 * n), lambda b: (b, 0)),
        ),
        scratch_shapes=slopes_scratch(n),
        compiler_params=params(),
        cost_estimate=lasting(5 * blocks),
    )(states, table)


def slopes_scratch(n):
    return [
        pltpu.VMEM((WIDE, 6 * n), BF16),
        pltpu.VMEM((WIDE, 6 * n), BF16),
        pltpu.VMEM((GRID, n), F32),
        pltpu.VMEM((GRID, n), F32),
    ]


def later_kernel(block, states_ref, table_ref, vm_ref, phi_ref, q_ref, grad_ref, *scratch):
    slopes_kernel(states_ref.at[block : block + 1], table_ref, phi_ref, grad_ref, *scratch)
    drift_rows(block, vm_ref, grad_ref, q_ref, 0)


def later_call(block, states, table, vm):
    orbitals = table.shape[0]
    n = states.shape[2]
    return pl.pallas_call(
        functools.partial(later_kernel, block),
        name="later",
        out_shape=(
            jax.ShapeDtypeStruct((orbitals, n), F32),
            jax.ShapeDtypeStruct((drift_size(block), n), F32),
        ),
        in_specs=[VMEM] * 3,
        out_specs=(VMEM, VMEM),
        scratch_shapes=[pltpu.VMEM((orbitals, 3 * n), F32)] + slopes_scratch(n),
        compiler_params=params(),
        cost_estimate=lasting(6),
    )(states, table, vm)


def split(x):
    high = x.astype(BF16)
    return high, (x - high.astype(F32)).astype(BF16)


def product(a, b, dims):
    (a0, a1), (b0, b1) = split(a), split(b)

    def one(x, y):
        return lax.dot_general(x, y, (dims, ((), ())), preferred_element_type=F32)

    return one(a0, b0) + (one(a0, b1) + one(a1, b0))


def dot(a, b):
    return product(a, b, ((1,), (0,)))


def dot_nt(a, b):
    return product(a, b, ((1,), (1,)))


def own_lanes(n, walker):
    lane = lax.broadcasted_iota(jnp.int32, (MOVED, n), 1)
    return jnp.logical_and(lane >= walker * K, lane < (walker + 1) * K)


def fold(big):
    n = big.shape[1]
    total = jnp.zeros((MOVED, n), F32)
    for w in range(n // K):
        total = jnp.where(own_lanes(n, w), big[w * MOVED : (w + 1) * MOVED, :], total)
    return total


def unit(block, n):
    row = lax.broadcasted_iota(jnp.int32, (MOVED, n), 0)
    lane = lax.broadcasted_iota(jnp.int32, (MOVED, n), 1)
    return jnp.where(row - block * K == lane % K, 1.0, 0.0).astype(F32)


def tree(parts):
    while len(parts) > 1:
        parts = [parts[i] + parts[i + 1] for i in range(0, len(parts), 2)]
    return parts[0]


def total(refs):
    return tree([ref[...] for ref in refs])


def params():
    return pltpu.CompilerParams(vmem_limit_bytes=LIMIT)


def lasting(us):
    return pl.CostEstimate(flops=int(us * 1e9), bytes_accessed=0, transcendentals=0)


def parent_of(meta_ref, walkers, w):
    parent = meta_ref[w]
    group = parent // walkers
    here = group == meta_ref[walkers + NMOVE]
    return here, jnp.where(here, parent % walkers, 0), jnp.where(here, 0, group)


def block_lanes(x, block):
    lane = lax.broadcasted_iota(jnp.int32, x.shape, 1)
    kept = jnp.where(lane // K == block, x, 0.0)
    return tree([kept[:, i : i + 128] for i in range(0, x.shape[1], 128)])


def roll(x, shift):
    if isinstance(shift, int):
        shift = shift % 128
        return x if shift == 0 else pltpu.roll(x, shift, 1)
    return pltpu.roll(x, lax.rem(shift + 1024, 128), 1)


def moved_lanes(x, meta_ref, walkers):
    line = jnp.zeros((x.shape[0], 128), F32)
    for b in range(NMOVE):
        block = meta_ref[walkers + b]
        line = line + roll(block_lanes(x, block), (b - block) * K)
    return line


def pack_kernel(meta_ref, pos_ref, gauss_ref, acc_ref, out_ref):
    walkers = pos_ref.shape[1]
    half = jnp.zeros((walkers, 128 - MOVED), F32)
    lane = lax.broadcasted_iota(jnp.int32, (walkers, 128), 1)
    row = lax.broadcasted_iota(jnp.int32, (walkers, 128), 0)
    lines = []
    for d in range(3):
        line = moved_lanes(pos_ref[d], meta_ref, walkers)
        lines.append(line + jnp.concatenate([half, gauss_ref[d]], axis=1))
    parents = jnp.zeros((walkers, 128), jnp.int32)
    for w in range(walkers):
        parents = jnp.where(row == w, meta_ref[w], parents)
    decided = jnp.concatenate([acc_ref[...].astype(F32), half], axis=1)
    lines.append(jnp.where(lane < MOVED, decided, parents.astype(F32)))
    for g in range(out_ref.shape[0]):
        for d in range(4):
            out_ref[g, pl.ds(d, walkers, stride=4), :] = lines[d]


def pack_call(meta, positions, gaussian, accepted, groups):
    walkers = positions.shape[1]
    return pl.pallas_call(
        pack_kernel,
        name="pack",
        out_shape=jax.ShapeDtypeStruct((groups, 4 * walkers, 128), F32),
        in_specs=[SMEM, VMEM, VMEM, VMEM],
        out_specs=VMEM,
        compiler_params=params(),
        cost_estimate=lasting(1),
    )(meta, positions, gaussian, accepted)


def columns_kernel(meta_ref, v_ref, pos_ref, out_ref, code_ref):
    walkers = pos_ref.shape[1]
    v = v_ref[0]
    orbitals, electrons = v.shape
    out_ref[0, 0:MOVED, :] = jnp.transpose(moved_lanes(v, meta_ref, walkers))[0:MOVED, :]
    size = jnp.abs(v)
    scale = jnp.max(size, axis=0, keepdims=True)
    at = MOVED
    own = pl.ds(pl.program_id(0), 1)
    for line in [scale] + [pos_ref[d, own, :] for d in range(3)]:
        for i in range(0, electrons, orbitals):
            out_ref[0, at : at + 1, :] = line[:, i : i + orbitals]
            at += 1
    step = jnp.where(scale > 0.0, LEVELS / jnp.sqrt(jnp.where(scale > 0.0, scale, 1.0)), 0.0)
    level = jnp.minimum(jnp.floor(jnp.sqrt(size) * step + 0.5), LEVELS)
    code_ref[0] = jnp.where(v < 0.0, -level, level).astype(jnp.int32).astype(jnp.int16)


def payload_rows(orbitals, electrons):
    return MOVED + 4 * electrons // orbitals


def columns_call(meta, inverse, positions):
    walkers, orbitals, electrons = inverse.shape
    rows = payload_rows(orbitals, electrons)
    return pl.pallas_call(
        columns_kernel,
        name="columns",
        grid_spec=pltpu.PrefetchScalarGridSpec(
            num_scalar_prefetch=1,
            grid=(walkers,),
            in_specs=[
                pl.BlockSpec((1, orbitals, electrons), lambda w, m: (w, 0, 0)),
                pl.BlockSpec(positions.shape, lambda w, m: (0, 0, 0)),
            ],
            out_specs=(
                pl.BlockSpec((1, rows, orbitals), lambda w, m: (w, 0, 0)),
                pl.BlockSpec((1, orbitals, electrons), lambda w, m: (w, 0, 0)),
            ),
        ),
        out_shape=(
            jax.ShapeDtypeStruct((walkers, rows, orbitals), F32),
            jax.ShapeDtypeStruct(inverse.shape, jnp.int16),
        ),
        compiler_params=params(),
        cost_estimate=lasting(3),
    )(meta, inverse, positions)


def route_kernel(meta_ref, info_ref, own_ref, states_ref, out_ref, sending_ref):
    walkers = own_ref.shape[0]
    groups = out_ref.shape[0]
    me = meta_ref[walkers + NMOVE]
    lane = lax.broadcasted_iota(jnp.int32, (8, 128), 1)
    tiles = []
    for w in range(walkers):
        line = info_ref[pl.ds(4 * meta_ref[w], 4), :]
        tiles.append(jnp.concatenate([line, roll(line, 128 - MOVED)], axis=0))
    for b in range(NMOVE):
        state = jnp.zeros((8, 128), F32)
        for w in range(walkers):
            state = jnp.where(lane // K == w, roll(tiles[w], (w - b) * K), state)
        states_ref[b] = state
    for g in range(groups):
        wanted = jnp.zeros((1, 128), jnp.int32)
        for s in range(walkers):
            row = 4 * (g * walkers + s) + 3
            parent = info_ref[row : row + 1, :].astype(jnp.int32)
            parent = jnp.where(lane[0:1] < MOVED, pltpu.roll(parent, 128 - MOVED, 1), parent)
            within = parent - me * walkers
            wanted = jnp.where(
                jnp.logical_and(within >= 0, within < walkers), within, wanted
            )
        wanted = jnp.where(me == g, 0, wanted)
        sending_ref[g : g + 1, :] = wanted
        picked = wanted[:, 0 : own_ref.shape[2]]
        total = own_ref[0]
        for w in range(1, walkers):
            total = jnp.where(picked == w, own_ref[w], total)
        out_ref[g] = total


def route_call(meta, info, own):
    walkers, rows, orbitals = own.shape
    groups = info.shape[0] // (4 * walkers)
    return pl.pallas_call(
        route_kernel,
        name="route",
        out_shape=(
            jax.ShapeDtypeStruct((NMOVE, 8, 128), F32),
            jax.ShapeDtypeStruct((groups, rows, orbitals), F32),
            jax.ShapeDtypeStruct((groups, 128), jnp.int32),
        ),
        in_specs=[SMEM, VMEM, VMEM],
        out_specs=(VMEM, VMEM, VMEM),
        compiler_params=params(),
        cost_estimate=lasting(2),
    )(meta, info, own)


def outcode_kernel(meta_ref, sending_ref, code_ref, *refs):
    out_refs, sem = refs[:-1], refs[-1]
    me = meta_ref[meta_ref.shape[0] - 2]
    copies = []
    for k, out_ref in enumerate(out_refs, start=1):
        source = sending_ref[jnp.bitwise_xor(me, k), 0]
        copies.append(pltpu.make_async_copy(code_ref.at[source], out_ref, sem.at[k - 1]))
    for copy in copies:
        copy.start()
    for copy in copies:
        copy.wait()


def outcode_call(meta, sending, code):
    others = sending.shape[0] - 1
    return pl.pallas_call(
        outcode_kernel,
        name="outcode",
        out_shape=tuple(jax.ShapeDtypeStruct(code.shape[1:], code.dtype) for _ in range(others)),
        in_specs=[SMEM, SMEM, ANY],
        out_specs=(ANY,) * others,
        scratch_shapes=[pltpu.SemaphoreType.DMA((others,))],
        compiler_params=params(),
        cost_estimate=lasting(1),
    )(meta, sending, code)


def select_kernel(meta_ref, own_ref, got_ref, grad_ref, vm_ref, out_ref):
    walkers = own_ref.shape[0]
    for w in range(walkers):
        here, place, group = parent_of(meta_ref, walkers, w)
        vm_ref[w * MOVED : (w + 1) * MOVED, :] = jnp.where(
            here, own_ref[place, 0:MOVED, :], got_ref[group, 0:MOVED, :]
        )
    orbitals = own_ref.shape[2]
    drift_rows(0, vm_ref, grad_ref.at[0:orbitals], out_ref, 0)
    drift_rows(1, vm_ref, grad_ref.at[orbitals:], out_ref, drift_size(0))


def drift_size(block):
    return 8 + 3 * K * block


def drift_rows(block, vm_ref, grad_ref, out_ref, at):
    n = grad_ref.shape[1] // 3
    size = K * block
    out_ref[at + 3 : at + 8, :] = jnp.zeros((5, n), F32)
    for d in range(3):
        q = fold(dot(vm_ref[...], grad_ref[:, d * n : (d + 1) * n]))
        out_ref[at + d : at + d + 1, :] = jnp.sum(q * unit(block, n), axis=0, keepdims=True)
        if block:
            out_ref[at + 8 + d * size : at + 8 + (d + 1) * size, :] = q[0:size, :]


def drift_of(block, q, t):
    size = K * block
    lines = [q[0:3, :]]
    if block:
        lines[0] += jnp.concatenate(
            [
                jnp.sum(q[8 + d * size : 8 + (d + 1) * size, :] * t[0:size, :], axis=0)[None]
                for d in range(3)
            ],
            axis=0,
        )
    return lines[0]


def select_call(meta, own, got, grad):
    walkers, _, orbitals = own.shape
    n = grad.shape[1] // 3
    return pl.pallas_call(
        select_kernel,
        name="select",
        out_shape=(
            jax.ShapeDtypeStruct((walkers * MOVED, orbitals), F32),
            jax.ShapeDtypeStruct((drift_size(0) + drift_size(1), n), F32),
        ),
        in_specs=[SMEM, VMEM, VMEM, VMEM],
        out_specs=(VMEM, VMEM),
        compiler_params=params(),
        cost_estimate=lasting(2),
    )(meta, own, got, grad)


def spread(x):
    n = x.shape[1]
    return jnp.concatenate([jnp.where(own_lanes(n, w), x, 0.0) for w in range(n // K)], axis=0)


def step_kernel(block, shards, *refs):
    refs = list(refs)
    first_parts = [refs.pop(0) for _ in range(shards)] if block < 2 else []
    if block:
        s_parts = [refs.pop(0) for _ in range(shards)]
        t_before = refs.pop(0)
    if block > 1:
        q_parts = [refs.pop(0) for _ in range(shards)]
        y_before = refs.pop(0)
    states_ref, phi_ref, vm_ref, table_ref = [refs.pop(0) for _ in range(4)]
    s_ref, moved_ref, d_ref, t_ref = [refs.pop(0) for _ in range(4)]
    y_ref = refs.pop(0) if block else None
    sum_ref, big_ref, even_ref, odd_ref, wx_ref = refs
    orbitals, n = sum_ref.shape
    state = states_ref[block]
    if block == 0:
        t_ref[...] = unit(0, n)
        drifts = drift_of(0, tree([ref[0:8, :] for ref in first_parts]), None)
    else:
        s = total(s_parts)
        if block > 1:
            s_ref[...] = s
            big_ref[...] = dot(y_before[...], s_ref[...])
            s = s - fold(big_ref[...])
        s_ref[...] = s
        y_all = dot_nt(spread(s_ref[...]), t_before[...])
        if block > 1:
            y_all = y_all + y_before[...]
        y_ref[...] = y_all
        rows = jnp.concatenate(
            [
                y_ref[w * MOVED + block * K : w * MOVED + (block + 1) * K, :]
                for w in range(n // K)
            ],
            axis=0,
        )
        t_ref[...] = unit(block, n) - jnp.transpose(rows)
        if block == 1:
            q = tree([ref[drift_size(0) :, :] for ref in first_parts])
        else:
            q = total(q_parts)
        drifts = drift_of(block, q, t_ref[...])
    speeds = jnp.sum(drifts * drifts, axis=0, keepdims=True)
    capped = drifts / jnp.sqrt(1.0 + TAU * speeds)
    moved = state[0:3, :] + state[3:4, :] * (TAU * capped + ROOT_TAU * state[4:7, :])
    moved_ref[0:3, :] = moved
    moved_ref[3:8, :] = jnp.zeros((5, n), F32)
    wx, _ = axis_weights(moved[0:1, :], False)
    wy, _ = axis_weights(moved[1:2, :], False)
    wz, _ = axis_weights(moved[2:3, :], False)
    wx_ref[...] = wx
    fill(even_ref, odd_ref, halves(wy, wz))
    sum_ref[...] = jnp.zeros_like(sum_ref)

    def body(pair, carry):
        even, odd = plane_pair(table_ref, pair, even_ref, odd_ref)
        w0, w1 = wx_ref[pl.ds(2 * pair, 1), :], wx_ref[pl.ds(2 * pair + 1, 1), :]
        sum_ref[...] += w0 * (even[:, 0:n] + even[:, n:]) + w1 * (odd[:, 0:n] + odd[:, n:])
        return carry

    lax.fori_loop(0, GRID // 2, body, 0, unroll=UNROLL)
    at = block * orbitals if block < 2 else 0
    change = sum_ref[...] - phi_ref[at : at + orbitals, :]
    d_ref[...] = jnp.transpose(change)
    s_ref[...] = fold(dot(vm_ref[...], change))


def step_call(block, operands, states, phi, vm, table):
    orbitals, n = table.shape[0], states.shape[2]
    shards = lax.axis_size("orb")
    rows = vm.shape[0]
    operands = [*operands, states, phi, vm, table]
    shapes = [(MOVED, n), (8, n), (n, orbitals), (MOVED, n)] + [(rows, MOVED)] * (block > 0)
    return pl.pallas_call(
        functools.partial(step_kernel, block, shards),
        name="step",
        out_shape=tuple(jax.ShapeDtypeStruct(shape, F32) for shape in shapes),
        in_specs=[VMEM] * len(operands),
        out_specs=(VMEM,) * len(shapes),
        scratch_shapes=[
            pltpu.VMEM((orbitals, n), F32),
            pltpu.VMEM((rows, n), F32),
            pltpu.VMEM((WIDE, 2 * n), BF16),
            pltpu.VMEM((WIDE, 2 * n), BF16),
            pltpu.VMEM((GRID, n), F32),
        ],
        compiler_params=params(),
        cost_estimate=lasting(4),
    )(*operands)


def last_kernel(shards, *refs):
    l_all = None
    for block in range(NMOVE):
        t = refs[NMOVE * shards + block][...]
        r = unit(block, t.shape[1])
        if block:
            r = r - fold(dot(l_all, total(refs[block * shards : (block + 1) * shards])))
        more = dot_nt(spread(r), t)
        l_all = l_all + more if block else more
    vm_ref, out_ref = refs[NMOVE * (shards + 1) :]
    for w in range(out_ref.shape[0]):
        at = slice(w * MOVED, (w + 1) * MOVED)
        out_ref[w] = jnp.transpose(dot(l_all[at, :], vm_ref[at, :]))


def last_call(s_parts, ts, vm):
    rows, orbitals = vm.shape
    operands = [part for parts in s_parts for part in parts] + list(ts) + [vm]
    return pl.pallas_call(
        functools.partial(last_kernel, len(s_parts[0])),
        name="last",
        out_shape=jax.ShapeDtypeStruct((rows // MOVED, orbitals, MOVED), F32),
        in_specs=[VMEM] * len(operands),
        out_specs=VMEM,
        compiler_params=params(),
        cost_estimate=lasting(3),
    )(*operands)


def both_halves(meta_ref, walkers, i):
    parity = meta_ref[meta_ref.shape[0] - 1]
    half = walkers // 2
    return i + half * parity, i + half * (1 - parity)


def assemble_kernel(others, meta_ref, own_ref, got_ref, *refs):
    code_refs, change_refs = refs[:others], refs[others : others + NMOVE - 1]
    v_ref, mine_ref, give_ref, held_ref, sem = refs[others + NMOVE - 1 :]
    walkers, orbitals, electrons = own_ref.shape
    me = meta_ref[walkers + NMOVE]
    copies = [
        pltpu.make_async_copy(ref, held_ref.at[k], sem.at[k]) for k, ref in enumerate(code_refs)
    ]
    for copy in copies:
        copy.start()
    for copy in copies:
        copy.wait()

    def body(i, carry):
        for w, out_ref in zip(both_halves(meta_ref, walkers, i), (mine_ref, give_ref)):
            here, place, group = parent_of(meta_ref, walkers, w)
            scale = jnp.concatenate(
                [
                    got_ref[group, MOVED + j : MOVED + j + 1, :]
                    for j in range(electrons // orbitals)
                ],
                axis=1,
            )
            slot = jnp.where(here, 0, jnp.bitwise_xor(group, me) - 1)
            level = held_ref[slot].astype(jnp.int32).astype(F32) * (1.0 / LEVELS)
            v = jnp.where(here, own_ref[place], level * jnp.abs(level) * scale)
            v_ref[w] = v
            at = pl.ds(pl.multiple_of(w * K, K), K)
            change = jnp.concatenate([ref[at, :] for ref in change_refs], axis=0)
            out_ref[i] = dot(change, v)
        return carry

    lax.fori_loop(0, walkers // 2, body, 0)


def assemble_call(meta, inverse, got, codes, changes):
    walkers, orbitals, electrons = inverse.shape
    half = (walkers // 2, (NMOVE - 1) * K, electrons)
    return pl.pallas_call(
        functools.partial(assemble_kernel, len(codes)),
        name="assemble",
        out_shape=(
            jax.ShapeDtypeStruct(inverse.shape, F32),
            jax.ShapeDtypeStruct(half, F32),
            jax.ShapeDtypeStruct(half, F32),
        ),
        in_specs=[SMEM, VMEM, VMEM] + [ANY] * len(codes) + [VMEM] * len(changes),
        out_specs=(VMEM,) * 3,
        scratch_shapes=[
            pltpu.VMEM((len(codes), orbitals, electrons), jnp.int16),
            pltpu.SemaphoreType.DMA((len(codes),)),
        ],
        compiler_params=params(),
        cost_estimate=lasting(4),
    )(meta, inverse, got, *codes, *changes)


def sums_kernel(meta_ref, v_ref, change_ref, mine_ref, give_ref):
    walkers = v_ref.shape[0]

    def body(i, carry):
        for w, out_ref in zip(both_halves(meta_ref, walkers, i), (mine_ref, give_ref)):
            at = pl.ds(pl.multiple_of(w * K, K), K)
            out_ref[i] = dot(change_ref[at, :], v_ref[w])
        return carry

    lax.fori_loop(0, walkers // 2, body, 0)


def sums_call(meta, inverse, change):
    walkers, _, electrons = inverse.shape
    half = jax.ShapeDtypeStruct((walkers // 2, K, electrons), F32)
    return pl.pallas_call(
        sums_kernel,
        name="sums",
        out_shape=(half, half),
        in_specs=[SMEM, VMEM, VMEM],
        out_specs=(VMEM, VMEM),
        compiler_params=params(),
        cost_estimate=lasting(1),
    )(meta, inverse, change)


def update_kernel(meta_ref, v_ref, factor_ref, *refs):
    out_ref = refs[4]
    parity = meta_ref[meta_ref.shape[0] - 1]
    for half in range(2):
        own = parity == half
        sums = jnp.concatenate(
            [jnp.where(own, refs[i][0], refs[i + 1][0]) for i in (0, 2)], axis=0
        )
        out_ref[half, 0] = v_ref[half, 0] - dot(factor_ref[half, 0], sums)


def update_call(meta, inverse, factor, early, late):
    shape = inverse.shape
    half = shape[0] // 2

    def pair(x):
        return x.reshape(2, half, *x.shape[1:])

    def pair_spec(x):
        return pl.BlockSpec((2, 1, *x.shape[1:]), lambda i, m: (0, i, 0, 0))

    def half_spec(x):
        return pl.BlockSpec((1, *x.shape[1:]), lambda i, m: (i, 0, 0))

    sums = [*early, *late]
    return pl.pallas_call(
        update_kernel,
        name="update",
        grid_spec=pltpu.PrefetchScalarGridSpec(
            num_scalar_prefetch=1,
            grid=(half,),
            in_specs=[pair_spec(inverse), pair_spec(factor)] + [half_spec(x) for x in sums],
            out_specs=pair_spec(inverse),
        ),
        out_shape=jax.ShapeDtypeStruct((2, half, *shape[1:]), F32),
        compiler_params=params(),
        cost_estimate=lasting(3),
    )(meta, pair(inverse), pair(factor), *sums).reshape(shape)


def place_kernel(meta_ref, own_ref, got_ref, *refs):
    out_ref = refs[NMOVE]
    _, walkers, electrons = own_ref.shape
    parts = electrons // got_ref.shape[2]
    lane = lax.broadcasted_iota(jnp.int32, (1, electrons), 1)
    for w in range(walkers):
        here, place, group = parent_of(meta_ref, walkers, w)
        fresh = []
        for b in range(NMOVE):
            block = meta_ref[walkers + b]
            fresh.append((block, roll(refs[b][...], (block - w) * K)))
        for d in range(3):
            at = MOVED + (d + 1) * parts
            far = jnp.concatenate(
                [got_ref[group, at + i : at + i + 1, :] for i in range(parts)], axis=1
            )
            line = jnp.where(here, own_ref[d, pl.ds(place, 1), :], far)
            for block, moved in fresh:
                moved = jnp.concatenate([moved[d : d + 1, :]] * (electrons // 128), axis=1)
                line = jnp.where(lane // K == block, moved, line)
            out_ref[d, w : w + 1, :] = line


def place_call(meta, positions, got, moved):
    return pl.pallas_call(
        place_kernel,
        name="place",
        out_shape=jax.ShapeDtypeStruct(positions.shape, F32),
        in_specs=[SMEM] + [VMEM] * (2 + NMOVE),
        out_specs=VMEM,
        compiler_params=params(),
        cost_estimate=lasting(1),
    )(meta, positions, got, *moved)


def swap(x, axis, k):
    return lax.ppermute(x, axis, [(i, i ^ k) for i in range(lax.axis_size(axis))])


def exchange(part, axis):
    return [part] + [swap(part, axis, k) for k in range(1, lax.axis_size(axis))]


def add_up(mine, give, axis):
    size = lax.axis_size(axis)
    mine = mine + swap(give, axis, 1)
    k = 2
    while k < size:
        mine = mine + swap(mine, axis, k)
        k *= 2
    return mine, swap(mine, axis, 1)


def alltoall(x):
    return lax.all_to_all(x, "walker", split_axis=0, concat_axis=0, tiled=True)


def local(positions, inverse, spline_table, gaussian, accepted, block_order, parent):
    groups = lax.axis_size("walker")
    me = lax.axis_index("walker").astype(jnp.int32)
    parity = lax.rem(lax.axis_index("orb"), 2).astype(jnp.int32)
    meta = jnp.concatenate([parent, block_order[:NMOVE], me[None], parity[None]])
    positions = jnp.transpose(positions, (1, 0, 2))
    gaussian = jnp.transpose(gaussian, (1, 0, 2))

    info = alltoall(pack_call(meta, positions, gaussian, accepted, groups))
    own, code = columns_call(meta, inverse, positions)
    states, outgoing, sending = route_call(meta, info.reshape(-1, 128), own)
    got = alltoall(outgoing)
    codes = [
        swap(x, "walker", k + 1) for k, x in enumerate(outcode_call(meta, sending, code))
    ]
    phi, grad = slopes_call(states, spline_table, 2)
    vm, first = select_call(meta, own, got, grad)
    first = exchange(first, "orb")

    def step(b, operands, phi):
        return step_call(b, operands, states, phi, vm, spline_table)

    s0, new0, change0, t0 = step(0, first, phi)
    phi2, q2 = later_call(2, states, spline_table, vm)
    q2 = exchange(q2, "orb")
    s0 = exchange(s0, "orb")
    s1, new1, change1, t1, y = step(1, [*first, *s0, t0], phi)
    phi3, q3 = later_call(3, states, spline_table, vm)
    q3 = exchange(q3, "orb")
    s1 = exchange(s1, "orb")
    s2, new2, change2, t2, y = step(2, [*s1, t1, *q2, y], phi2)
    s2 = exchange(s2, "orb")
    whole, mine, give = assemble_call(meta, inverse, got, codes, [change0, change1, change2])
    early = add_up(mine, give, "orb")
    s3, new3, change3, t3, y = step(3, [*s2, t2, *q3, y], phi3)
    late = add_up(*sums_call(meta, whole, change3), "orb")
    s3 = exchange(s3, "orb")
    factor = last_call([s0, s1, s2, s3], [t0, t1, t2, t3], vm)
    new_positions = place_call(meta, positions, got, [new0, new1, new2, new3])
    new_inverse = update_call(meta, whole, factor, early, late)
    return jnp.transpose(new_positions, (1, 0, 2)), new_inverse


def solution(mesh):
    return jax.shard_map(
        local,
        mesh=mesh,
        in_specs=(
            P("walker", None, None),
            P("walker", "orb", None),
            P("orb", None),
            P("walker", None, None),
            P("walker", None),
            P(),
            P("walker"),
        ),
        out_specs=(P("walker", None, None), P("walker", "orb", None)),
        check_vma=False,
    )
```

```python
import functools

import jax
import jax.numpy as jnp
from jax import lax
from jax.experimental import pallas as pl
from jax.experimental.pallas import tpu as pltpu
from jax.sharding import PartitionSpec as P

GRID = 24
PLANE = GRID * GRID
WIDE = 640
UNROLL = 12
CHUNKS = (4, 4, 4)
K = 16
NMOVE = 4
MOVED = K * NMOVE
CAP = 1
TAU = 0.25
ROOT_TAU = 0.5
F32 = jnp.float32
BF16 = jnp.bfloat16
LEVELS = 32767.0
HIGHEST = lax.Precision.HIGHEST
VMEM = pl.BlockSpec(memory_space=pltpu.VMEM)
SMEM = pl.BlockSpec(memory_space=pltpu.SMEM)
ANY = pl.BlockSpec(memory_space=pl.ANY)
LIMIT = 16 * 2**20
WHOLE = 60 * 2**20
PART = 59500000


def axis_weights(u, with_slopes):
    floors = jnp.floor(u)
    t = u - floors
    remain = 1.0 - t
    square = t * t
    cubed = square * t
    values = (
        remain * remain * remain / 6.0,
        (3.0 * cubed - 6.0 * square + 4.0) / 6.0,
        (-3.0 * cubed + 3.0 * square + 3.0 * t + 1.0) / 6.0,
        cubed / 6.0,
    )
    lanes = u.shape[1]
    line = lax.broadcasted_iota(jnp.int32, (GRID, lanes), 0)
    step = line - (floors.astype(jnp.int32) - 1)
    step = jnp.where(step < 0, step + GRID, step)
    step = jnp.where(step < 0, step + GRID, step)
    step = jnp.where(step >= GRID, step - GRID, step)

    def spread(weights):
        out = jnp.zeros((GRID, lanes), F32)
        for a in range(4):
            out = jnp.where(step == a, jnp.broadcast_to(weights[a], (GRID, lanes)), out)
        return out

    if not with_slopes:
        return spread(values), None
    slopes = (
        -0.5 * remain * remain,
        1.5 * square - 2.0 * t,
        -1.5 * square + t + 0.5,
        0.5 * square,
    )
    return spread(values), spread(slopes)


def halves(first, second):
    product = jnp.concatenate([first[y : y + 1, :] * second for y in range(GRID)], axis=0)
    high = product.astype(BF16)
    return [high, (product - high.astype(F32)).astype(BF16)]


def fill(even_ref, odd_ref, pieces):
    lanes = pieces[0].shape[1]
    pad = jnp.zeros((WIDE - PLANE, lanes), BF16)
    for i, piece in enumerate(pieces):
        at = slice(i * lanes, (i + 1) * lanes)
        even_ref[0:PLANE, at] = piece
        even_ref[PLANE:WIDE, at] = pad
        odd_ref[0 : WIDE - PLANE, at] = pad
        odd_ref[WIDE - PLANE : WIDE, at] = piece


def plane_pair(table_ref, pair, even_ref, odd_ref):
    start = pl.multiple_of(pair * 2 * PLANE, 128)
    even = table_ref[:, pl.ds(start, WIDE)]
    start = pl.multiple_of(pair * 2 * PLANE + 2 * PLANE - WIDE, 128)
    odd = table_ref[:, pl.ds(start, WIDE)]
    return (
        jnp.dot(even, even_ref[...], preferred_element_type=F32),
        jnp.dot(odd, odd_ref[...], preferred_element_type=F32),
    )


def slopes_kernel(
    state_ref, table_ref, phi_ref, grad_ref, even_ref, odd_ref, wx_ref, sx_ref, loads=()
):
    n = state_ref.shape[2]
    wx, sx = axis_weights(state_ref[0, 0:1, :], True)
    wy, sy = axis_weights(state_ref[0, 1:2, :], True)
    wz, sz = axis_weights(state_ref[0, 2:3, :], True)
    wx_ref[...] = wx
    sx_ref[...] = sx
    fill(even_ref, odd_ref, halves(wy, wz) + halves(sy, wz) + halves(wy, sz))
    phi_ref[...] = jnp.zeros_like(phi_ref)
    grad_ref[...] = jnp.zeros_like(grad_ref)

    def body(pair, carry):
        even, odd = plane_pair(table_ref, pair, even_ref, odd_ref)
        w0, w1 = wx_ref[pl.ds(2 * pair, 1), :], wx_ref[pl.ds(2 * pair + 1, 1), :]
        s0, s1 = sx_ref[pl.ds(2 * pair, 1), :], sx_ref[pl.ds(2 * pair + 1, 1), :]

        def both(i):
            at, to = slice(2 * i * n, (2 * i + 1) * n), slice((2 * i + 1) * n, (2 * i + 2) * n)
            return even[:, at] + even[:, to], odd[:, at] + odd[:, to]

        e, o = both(0)
        phi_ref[...] += w0 * e + w1 * o
        grad_ref[:, 0:n] += s0 * e + s1 * o
        for d in (1, 2):
            e, o = both(d)
            grad_ref[:, d * n : (d + 1) * n] += w0 * e + w1 * o
        return carry

    pairs = GRID // 2
    if loads:
        start = 0
        for i, (load, size) in enumerate(zip(loads, CHUNKS)):
            load.wait()
            if i + 1 < len(loads):
                loads[i + 1].start()
            lax.fori_loop(start, start + size, body, 0, unroll=size)
            start += size
    else:
        lax.fori_loop(0, pairs, body, 0, unroll=UNROLL)


def first_kernel(states_ref, table_ref, phi_out, grad_out, held_ref, phi_ref, grad_ref, *refs):
    scratch, (in_sem, out_sem) = refs[:-2], refs[-2:]
    loads = []
    start = 0
    for i, pairs in enumerate(CHUNKS):
        at = pl.ds(start, 2 * PLANE * pairs)
        start += 2 * PLANE * pairs
        loads.append(
            pltpu.make_async_copy(table_ref.at[:, at], held_ref.at[:, at], in_sem.at[i])
        )
    loads[0].start()
    slopes_kernel(states_ref.at[0:1], held_ref, phi_ref, grad_ref, *scratch, loads=loads)
    stores = [
        pltpu.make_async_copy(phi_ref, phi_out, out_sem.at[0]),
        pltpu.make_async_copy(grad_ref, grad_out, out_sem.at[1]),
    ]
    for store in stores:
        store.start()
    for store in stores:
        store.wait()


def slopes_call(states, table):
    orbitals = table.shape[0]
    n = states.shape[2]
    shapes = [(orbitals, n), (orbitals, 3 * n)]
    return pl.pallas_call(
        first_kernel,
        name="slopes",
        out_shape=tuple(jax.ShapeDtypeStruct(shape, F32) for shape in shapes),
        in_specs=[VMEM, ANY],
        out_specs=(ANY, ANY),
        scratch_shapes=[pltpu.VMEM(table.shape, BF16)]
        + [pltpu.VMEM(shape, F32) for shape in shapes]
        + slopes_scratch(n)
        + [pltpu.SemaphoreType.DMA((len(CHUNKS),)), pltpu.SemaphoreType.DMA((2,))],
        compiler_params=params(WHOLE),
        cost_estimate=lasting(5),
    )(states, table)


def slopes_scratch(n):
    return [
        pltpu.VMEM((WIDE, 6 * n), BF16),
        pltpu.VMEM((WIDE, 6 * n), BF16),
        pltpu.VMEM((GRID, n), F32),
        pltpu.VMEM((GRID, n), F32),
    ]


def later_kernel(block, states_ref, table_ref, vm_ref, phi_ref, out_ref, grad_ref, *scratch):
    slopes_kernel(states_ref.at[block : block + 1], table_ref, phi_ref, grad_ref, *scratch)
    drift_rows(block, vm_ref, grad_ref, out_ref, 0)


def later_call(block, states, table, vm):
    orbitals = table.shape[0]
    n = states.shape[2]
    return pl.pallas_call(
        functools.partial(later_kernel, block),
        name="later",
        out_shape=(
            jax.ShapeDtypeStruct((orbitals, n), F32),
            jax.ShapeDtypeStruct((drift_size(block), n), F32),
        ),
        in_specs=[VMEM] * 3,
        out_specs=(VMEM, VMEM),
        scratch_shapes=[pltpu.VMEM((orbitals, 3 * n), F32)] + slopes_scratch(n),
        compiler_params=params(),
        cost_estimate=lasting(5),
    )(states, table, vm)


def split(x):
    high = x.astype(BF16)
    return high, (x - high.astype(F32)).astype(BF16)


def product(a, b, dims):
    (a0, a1), (b0, b1) = split(a), split(b)

    def one(x, y):
        return lax.dot_general(x, y, (dims, ((), ())), preferred_element_type=F32)

    return one(a0, b0) + (one(a0, b1) + one(a1, b0))


def dot(a, b):
    return product(a, b, ((1,), (0,)))


def dot_nt(a, b):
    return product(a, b, ((1,), (1,)))


def own_lanes(n, walker):
    lane = lax.broadcasted_iota(jnp.int32, (MOVED, n), 1)
    return jnp.logical_and(lane >= walker * K, lane < (walker + 1) * K)


def fold(big):
    n = big.shape[1]
    total = jnp.zeros((MOVED, n), F32)
    for w in range(n // K):
        total = jnp.where(own_lanes(n, w), big[w * MOVED : (w + 1) * MOVED, :], total)
    return total


def unit(block, n):
    row = lax.broadcasted_iota(jnp.int32, (MOVED, n), 0)
    lane = lax.broadcasted_iota(jnp.int32, (MOVED, n), 1)
    return jnp.where(row - block * K == lane % K, 1.0, 0.0).astype(F32)


def tree(parts):
    while len(parts) > 1:
        parts = [parts[i] + parts[i + 1] for i in range(0, len(parts), 2)]
    return parts[0]


def total(refs):
    return tree([ref[...] for ref in refs])


def params(limit=LIMIT):
    return pltpu.CompilerParams(vmem_limit_bytes=limit)


def lasting(us):
    return pl.CostEstimate(flops=int(us * 1e8), bytes_accessed=0, transcendentals=0)


def parent_of(meta_ref, walkers, w):
    parent = meta_ref[w]
    group = parent // walkers
    here = group == meta_ref[walkers + NMOVE]
    return here, jnp.where(here, parent % walkers, 0), jnp.where(here, 0, group)


def block_lanes(x, block):
    lane = lax.broadcasted_iota(jnp.int32, x.shape, 1)
    kept = jnp.where(lane // K == block, x, 0.0)
    return tree([kept[:, i : i + 128] for i in range(0, x.shape[1], 128)])


def roll(x, shift):
    if isinstance(shift, int):
        shift = shift % 128
        return x if shift == 0 else pltpu.roll(x, shift, 1)
    return pltpu.roll(x, lax.rem(shift + 1024, 128), 1)


def moved_lanes(x, order_ref):
    line = jnp.zeros((x.shape[0], 128), F32)
    for b in range(NMOVE):
        block = order_ref[b]
        line = line + roll(block_lanes(x, block), (b - block) * K)
    return line


def pack_kernel(parent_ref, order_ref, *refs):
    (out_ref, pos_ref, gauss_ref, acc_ref), sem = refs[3:-1], refs[-1]
    copies = [
        pltpu.make_async_copy(refs[i], refs[i + 4], sem.at[i]) for i in range(3)
    ]
    for copy in copies:
        copy.start()
    for copy in copies:
        copy.wait()
    walkers = pos_ref.shape[1]
    half = jnp.zeros((walkers, 128 - MOVED), F32)
    lane = lax.broadcasted_iota(jnp.int32, (walkers, 128), 1)
    row = lax.broadcasted_iota(jnp.int32, (walkers, 128), 0)
    lines = []
    for d in range(3):
        line = moved_lanes(pos_ref[d], order_ref)
        lines.append(line + jnp.concatenate([half, gauss_ref[d]], axis=1))
    parents = jnp.zeros((walkers, 128), jnp.int32)
    for w in range(walkers):
        parents = jnp.where(row == w, parent_ref[w], parents)
    decided = jnp.concatenate([acc_ref[...].astype(F32), half], axis=1)
    lines.append(jnp.where(lane < MOVED, decided, parents.astype(F32)))
    for g in range(out_ref.shape[0]):
        for d in range(4):
            out_ref[g, d * walkers : (d + 1) * walkers, :] = lines[d]


def pack_call(parent, order, positions, gaussian, accepted, groups):
    walkers = positions.shape[1]
    held = [positions, gaussian, accepted]
    return pl.pallas_call(
        pack_kernel,
        name="pack",
        out_shape=jax.ShapeDtypeStruct((groups, 4 * walkers, 128), F32),
        in_specs=[SMEM, SMEM, ANY, ANY, ANY],
        out_specs=VMEM,
        scratch_shapes=[pltpu.VMEM(x.shape, x.dtype) for x in held]
        + [pltpu.SemaphoreType.DMA((3,))],
        compiler_params=params(WHOLE),
        cost_estimate=lasting(1),
    )(parent, order, *held)


def columns_kernel(order_ref, v_in, pos_in, own_out, code_out, v_ref, pos_ref, own_ref, code_ref, sem):
    walkers, orbitals, electrons = v_ref.shape

    def load(w):
        return pltpu.make_async_copy(v_in.at[w], v_ref.at[w], sem.at[0, w])

    def store(w):
        return (
            pltpu.make_async_copy(own_ref.at[w], own_out.at[w], sem.at[1, w]),
            pltpu.make_async_copy(code_ref.at[w], code_out.at[w], sem.at[2, w]),
        )

    first = pltpu.make_async_copy(pos_in, pos_ref, sem.at[0, walkers])
    first.start()
    for w in range(walkers):
        load(w).start()
    first.wait()

    def body(w, carry):
        load(w).wait()
        v = v_ref[w]
        own_ref[w, 0:MOVED, :] = jnp.transpose(moved_lanes(v, order_ref))[0:MOVED, :]
        size = jnp.abs(v)
        scale = jnp.max(size, axis=0, keepdims=True)
        at = MOVED
        for line in [scale] + [pos_ref[d, pl.ds(w, 1), :] for d in range(3)]:
            for i in range(0, electrons, orbitals):
                own_ref[w, at : at + 1, :] = line[:, i : i + orbitals]
                at += 1
        some = scale > 0.0
        step = jnp.where(some, LEVELS / jnp.sqrt(jnp.where(some, scale, 1.0)), 0.0)
        level = jnp.minimum(jnp.floor(jnp.sqrt(size) * step + 0.5), LEVELS)
        code_ref[w] = jnp.where(v < 0.0, -level, level).astype(jnp.int32).astype(jnp.int16)
        for copy in store(w):
            copy.start()
        return carry

    lax.fori_loop(0, walkers, body, 0)
    for w in range(walkers):
        for copy in store(w):
            copy.wait()


def payload_rows(orbitals, electrons):
    return MOVED + 4 * electrons // orbitals


def columns_call(order, inverse, positions):
    walkers, orbitals, electrons = inverse.shape
    own = (walkers, payload_rows(orbitals, electrons), orbitals)
    return pl.pallas_call(
        columns_kernel,
        name="columns",
        out_shape=(
            jax.ShapeDtypeStruct(own, F32),
            jax.ShapeDtypeStruct(inverse.shape, jnp.int16),
        ),
        in_specs=[SMEM, ANY, ANY],
        out_specs=(ANY, ANY),
        scratch_shapes=[
            pltpu.VMEM(inverse.shape, F32),
            pltpu.VMEM(positions.shape, F32),
            pltpu.VMEM(own, F32),
            pltpu.VMEM(inverse.shape, jnp.int16),
            pltpu.SemaphoreType.DMA((3, walkers + 1)),
        ],
        compiler_params=params(WHOLE),
        cost_estimate=lasting(3),
    )(order, inverse, positions)


def route_kernel(meta_ref, info_in, own_in, code_in, states_ref, out_ref, outcode_ref, *refs):
    info_ref, own_ref, code_ref, parents_ref, sem, out_sem = refs
    walkers = own_ref.shape[0]
    groups = out_ref.shape[0]
    rows = 3 * walkers
    asked = []
    for g in range(groups):
        at = pl.ds(rows, walkers)
        asked.append(pltpu.make_async_copy(info_in.at[g, at], parents_ref.at[g], sem.at[3]))
    for each in asked:
        each.start()
    loads = [
        pltpu.make_async_copy(info_in, info_ref, sem.at[0]),
        pltpu.make_async_copy(own_in, own_ref, sem.at[1]),
        pltpu.make_async_copy(code_in, code_ref, sem.at[2]),
    ]
    for load in loads:
        load.start()
    for each in asked:
        each.wait()
    me = meta_ref[walkers + NMOVE]
    sending = []
    for g in range(groups):
        wanted = jnp.int32(0)
        for s in range(walkers):
            within = parents_ref[g, s, MOVED].astype(jnp.int32) - me * walkers
            mine = jnp.logical_and(within >= 0, within < walkers)
            wanted = jnp.where(mine, within, wanted)
        sending.append(jnp.where(me == g, 0, wanted))
    for load in loads[1:]:
        load.wait()
    stores = []
    for g in range(groups):
        source = sending[g]
        stores.append(pltpu.make_async_copy(own_ref.at[source], out_ref.at[g], out_sem.at[0, g]))
        stores.append(
            pltpu.make_async_copy(code_ref.at[source], outcode_ref.at[g], out_sem.at[1, g])
        )
    for store in stores:
        store.start()
    loads[0].wait()
    lane = lax.broadcasted_iota(jnp.int32, (8, 128), 1)
    tiles = []
    for w in range(walkers):
        group, place = meta_ref[w] // walkers, meta_ref[w] % walkers
        line = [info_ref[group, pl.ds(d * walkers + place, 1), :] for d in range(4)]
        line = jnp.concatenate(line, axis=0)
        tiles.append(jnp.concatenate([line, roll(line, 128 - MOVED)], axis=0))
    for b in range(NMOVE):
        state = jnp.zeros((8, 128), F32)
        for w in range(walkers):
            state = jnp.where(lane // K == w, roll(tiles[w], (w - b) * K), state)
        states_ref[b] = state
    for store in stores:
        store.wait()


def route_call(meta, info, own, code):
    groups = info.shape[0]
    shapes = [(groups, *own.shape[1:]), (groups, *code.shape[1:])]
    return pl.pallas_call(
        route_kernel,
        name="route",
        out_shape=(
            jax.ShapeDtypeStruct((NMOVE, 8, 128), F32),
            jax.ShapeDtypeStruct(shapes[0], F32),
            jax.ShapeDtypeStruct(shapes[1], code.dtype),
        ),
        in_specs=[SMEM, ANY, ANY, ANY],
        out_specs=(VMEM, ANY, ANY),
        scratch_shapes=[
            pltpu.VMEM(info.shape, F32),
            pltpu.VMEM(own.shape, F32),
            pltpu.VMEM(code.shape, code.dtype),
            pltpu.SMEM((groups, own.shape[0], 128), F32),
            pltpu.SemaphoreType.DMA((4,)),
            pltpu.SemaphoreType.DMA((2, groups)),
        ],
        compiler_params=params(WHOLE),
        cost_estimate=lasting(3),
    )(meta, info, own, code)


def select_kernel(meta_ref, own_ref, got_ref, grad_in, vm_ref, out_ref, grad_ref, sem):
    walkers = own_ref.shape[0]
    load = pltpu.make_async_copy(grad_in, grad_ref, sem.at[walkers])
    load.start()

    def copy(w, source):
        to = vm_ref.at[w * MOVED : (w + 1) * MOVED]
        return pltpu.make_async_copy(source.at[0:MOVED], to, sem.at[w])

    for w in range(walkers):
        here, place, group = parent_of(meta_ref, walkers, w)

        @pl.when(here)
        def _():
            copy(w, own_ref.at[place]).start()

        @pl.when(jnp.logical_not(here))
        def _():
            copy(w, got_ref.at[group]).start()

    for w in range(walkers):
        copy(w, own_ref.at[0]).wait()
    load.wait()
    drift_rows(0, vm_ref, grad_ref, out_ref, 0)


def drift_size(block):
    return 8 + 3 * K * block


def drift_rows(block, vm_ref, grad_ref, out_ref, at):
    n = grad_ref.shape[1] // 3
    size = K * block
    out_ref[at + 3 : at + 8, :] = jnp.zeros((5, n), F32)
    for d in range(3):
        q = fold(dot(vm_ref[...], grad_ref[:, d * n : (d + 1) * n]))
        out_ref[at + d : at + d + 1, :] = jnp.sum(q * unit(block, n), axis=0, keepdims=True)
        if block:
            out_ref[at + 8 + d * size : at + 8 + (d + 1) * size, :] = q[0:size, :]


def drift_of(block, q, t):
    size = K * block
    lines = [q[0:3, :]]
    if block:
        lines[0] += jnp.concatenate(
            [
                jnp.sum(q[8 + d * size : 8 + (d + 1) * size, :] * t[0:size, :], axis=0)[None]
                for d in range(3)
            ],
            axis=0,
        )
    return lines[0]


def select_call(meta, own, got, grad):
    walkers, _, orbitals = own.shape
    n = grad.shape[1] // 3
    return pl.pallas_call(
        select_kernel,
        name="select",
        out_shape=(
            jax.ShapeDtypeStruct((walkers * MOVED, orbitals), F32),
            jax.ShapeDtypeStruct((drift_size(0), n), F32),
        ),
        in_specs=[SMEM, ANY, ANY, ANY],
        out_specs=(VMEM, VMEM),
        scratch_shapes=[
            pltpu.VMEM(grad.shape, F32),
            pltpu.SemaphoreType.DMA((walkers + 1,)),
        ],
        compiler_params=params(PART),
        cost_estimate=lasting(2),
    )(meta, own, got, grad)


def spread(x):
    n = x.shape[1]
    return jnp.concatenate([jnp.where(own_lanes(n, w), x, 0.0) for w in range(n // K)], axis=0)


def step_kernel(block, count, *refs):
    refs = list(refs)
    parts = [refs.pop(0) for _ in range(count)]
    later_ref = refs.pop(0) if block < NMOVE - 1 else None
    if block:
        t_before = refs.pop(0)
    if block > 1:
        y_before = refs.pop(0)
    states_ref, phi_ref, vm_ref, table_ref = [refs.pop(0) for _ in range(4)]
    s_ref, moved_ref, d_ref, t_ref = [refs.pop(0) for _ in range(4)]
    y_ref = refs.pop(0) if block else None
    sum_ref, big_ref, even_ref, odd_ref, wx_ref = refs
    if later_ref is not None:
        s_ref[MOVED:, :] = later_ref[...]
    n = sum_ref.shape[1]
    state = states_ref[block]
    if block == 0:
        t_ref[...] = unit(0, n)
        drifts = drift_of(0, total(parts), None)
    else:
        s = tree([ref[0:MOVED, :] for ref in parts])
        if block > 1:
            s_ref[0:MOVED, :] = s
            big_ref[...] = dot(y_before[...], s_ref[0:MOVED, :])
            s = s - fold(big_ref[...])
        s_ref[0:MOVED, :] = s
        y_all = dot_nt(spread(s_ref[0:MOVED, :]), t_before[...])
        if block > 1:
            y_all = y_all + y_before[...]
        y_ref[...] = y_all
        rows = jnp.concatenate(
            [
                y_ref[w * MOVED + block * K : w * MOVED + (block + 1) * K, :]
                for w in range(n // K)
            ],
            axis=0,
        )
        t_ref[...] = unit(block, n) - jnp.transpose(rows)
        q = tree([ref[MOVED:, :] for ref in parts])
        drifts = drift_of(block, q, t_ref[...])
    speeds = jnp.sum(drifts * drifts, axis=0, keepdims=True)
    capped = drifts / jnp.sqrt(1.0 + TAU * speeds)
    moved = state[0:3, :] + state[3:4, :] * (TAU * capped + ROOT_TAU * state[4:7, :])
    moved_ref[0:3, :] = moved
    moved_ref[3:8, :] = jnp.zeros((5, n), F32)
    wx, _ = axis_weights(moved[0:1, :], False)
    wy, _ = axis_weights(moved[1:2, :], False)
    wz, _ = axis_weights(moved[2:3, :], False)
    wx_ref[...] = wx
    fill(even_ref, odd_ref, halves(wy, wz))
    sum_ref[...] = jnp.zeros_like(sum_ref)

    def body(pair, carry):
        even, odd = plane_pair(table_ref, pair, even_ref, odd_ref)
        w0, w1 = wx_ref[pl.ds(2 * pair, 1), :], wx_ref[pl.ds(2 * pair + 1, 1), :]
        sum_ref[...] += w0 * (even[:, 0:n] + even[:, n:]) + w1 * (odd[:, 0:n] + odd[:, n:])
        return carry

    lax.fori_loop(0, GRID // 2, body, 0, unroll=UNROLL)
    change = sum_ref[...] - phi_ref[...]
    d_ref[...] = jnp.transpose(change)
    s_ref[0:MOVED, :] = fold(dot(vm_ref[...], change))


def step_call(block, parts, later, carried, states, phi, vm, table):
    orbitals, n = table.shape[0], states.shape[2]
    rows = vm.shape[0]
    operands = [*parts, *later, *carried, states, phi, vm, table]
    sums = (MOVED + later[0].shape[0] if later else MOVED, n)
    shapes = [sums, (8, n), (n, orbitals), (MOVED, n)] + [(rows, MOVED)] * (block > 0)
    return pl.pallas_call(
        functools.partial(step_kernel, block, len(parts)),
        name="step",
        out_shape=tuple(jax.ShapeDtypeStruct(shape, F32) for shape in shapes),
        in_specs=[VMEM] * len(operands),
        out_specs=(VMEM,) * len(shapes),
        scratch_shapes=[
            pltpu.VMEM((orbitals, n), F32),
            pltpu.VMEM((rows, n), F32),
            pltpu.VMEM((WIDE, 2 * n), BF16),
            pltpu.VMEM((WIDE, 2 * n), BF16),
            pltpu.VMEM((GRID, n), F32),
        ],
        compiler_params=params(),
        cost_estimate=lasting(3),
    )(*operands)


def last_kernel(counts, *refs):
    refs = list(refs)
    sums = [[refs.pop(0) for _ in range(count)] for count in counts]
    ts = [refs.pop(0)[...] for _ in range(NMOVE)]
    vm_ref, out_ref, l_ref = refs
    for block in range(NMOVE - 1):
        r = unit(block, ts[block].shape[1])
        if block:
            sums_of = tree([ref[0:MOVED, :] for ref in sums[block - 1]])
            r = r - fold(dot(l_ref[...], sums_of))
        more = dot_nt(spread(r), ts[block])
        l_ref[...] = l_ref[...] + more if block else more
    t = jnp.transpose(ts[-1])
    for w in range(out_ref.shape[0]):
        at = slice(w * MOVED, (w + 1) * MOVED)
        early = l_ref[w * MOVED : (w + 1) * MOVED - K, :]
        factor = jnp.concatenate([early, t[w * K : (w + 1) * K, :]], axis=0)
        out_ref[w] = jnp.transpose(dot(factor, vm_ref[at, :]))


def last_call(s_parts, ts, vm):
    rows, orbitals = vm.shape
    operands = [part for parts in s_parts for part in parts] + list(ts) + [vm]
    return pl.pallas_call(
        functools.partial(last_kernel, [len(parts) for parts in s_parts]),
        name="last",
        out_shape=(
            jax.ShapeDtypeStruct((rows // MOVED, orbitals, MOVED), F32),
            jax.ShapeDtypeStruct((rows, MOVED), F32),
        ),
        in_specs=[VMEM] * len(operands),
        out_specs=(VMEM, VMEM),
        compiler_params=params(),
        cost_estimate=lasting(2),
    )(*operands)


def both_halves(meta_ref, walkers, i):
    parity = meta_ref[meta_ref.shape[0] - 1]
    half = walkers // 2
    return i + half * parity, i + half * (1 - parity)


def assemble_kernel(meta_ref, own_ref, got_ref, code_ref, *refs):
    change_refs = refs[: NMOVE - 1]
    v_ref, mine_ref, give_ref, held_ref, sem = refs[NMOVE - 1 :]
    walkers, orbitals, electrons = own_ref.shape
    load = pltpu.make_async_copy(code_ref, held_ref, sem)
    load.start()
    load.wait()

    def body(i, carry):
        for w, out_ref in zip(both_halves(meta_ref, walkers, i), (mine_ref, give_ref)):
            here, place, group = parent_of(meta_ref, walkers, w)
            scale = jnp.concatenate(
                [
                    got_ref[group, MOVED + j : MOVED + j + 1, :]
                    for j in range(electrons // orbitals)
                ],
                axis=1,
            )
            level = held_ref[group].astype(jnp.int32).astype(F32) * (1.0 / LEVELS)
            v = jnp.where(here, own_ref[place], level * jnp.abs(level) * scale)
            v_ref[w] = v
            at = pl.ds(pl.multiple_of(w * K, K), K)
            change = jnp.concatenate([ref[at, :] for ref in change_refs], axis=0)
            out_ref[i] = dot(change, v)
        return carry

    lax.fori_loop(0, walkers // 2, body, 0)


def assemble_call(meta, inverse, got, code, changes):
    walkers, orbitals, electrons = inverse.shape
    half = (walkers // 2, (NMOVE - 1) * K, electrons)
    return pl.pallas_call(
        assemble_kernel,
        name="assemble",
        out_shape=(
            jax.ShapeDtypeStruct(inverse.shape, F32),
            jax.ShapeDtypeStruct(half, F32),
            jax.ShapeDtypeStruct(half, F32),
        ),
        in_specs=[SMEM, VMEM, VMEM, ANY] + [VMEM] * len(changes),
        out_specs=(VMEM,) * 3,
        scratch_shapes=[
            pltpu.VMEM(code.shape, code.dtype),
            pltpu.SemaphoreType.DMA(()),
        ],
        compiler_params=params(),
        cost_estimate=lasting(4),
    )(meta, inverse, got, code, *changes)


def sums_kernel(meta_ref, v_ref, change_ref, mine_ref, give_ref):
    walkers = v_ref.shape[0]

    def body(i, carry):
        for w, out_ref in zip(both_halves(meta_ref, walkers, i), (mine_ref, give_ref)):
            at = pl.ds(pl.multiple_of(w * K, K), K)
            out_ref[i] = dot(change_ref[at, :], v_ref[w])
        return carry

    lax.fori_loop(0, walkers // 2, body, 0)


def sums_call(meta, inverse, change):
    walkers, _, electrons = inverse.shape
    half = jax.ShapeDtypeStruct((walkers // 2, K, electrons), F32)
    return pl.pallas_call(
        sums_kernel,
        name="sums",
        out_shape=(half, half),
        in_specs=[SMEM, VMEM, VMEM],
        out_specs=(VMEM, VMEM),
        compiler_params=params(),
        cost_estimate=lasting(1),
    )(meta, inverse, change)


def update_kernel(order_ref, meta_ref, v_ref, factor_ref, l_ref, *refs):
    sums_refs, (out_ref, new_ref, sem) = refs[:4], refs[4:]
    walkers = v_ref.shape[0]

    def store(w):
        return pltpu.make_async_copy(new_ref.at[w], out_ref.at[w], sem.at[w])

    half = walkers // 2
    own = [both_halves(meta_ref, walkers, i) for i in range(half)]
    places = [(own[i][h], i, sums_refs[2 * h : 2 * h + 2]) for i in range(half) for h in range(2)]
    lates = []
    for w, i, (early_ref, late_ref) in places:
        moved = moved_lanes(late_ref[i], order_ref)[:, 0:MOVED]
        rows = l_ref[pl.ds(pl.multiple_of(w * MOVED, MOVED), MOVED), :]
        lates.append(dot_nt(moved, rows)[:, 0 : MOVED - K])
    for n, (w, i, (early_ref, late_ref)) in enumerate(places):
        lates[n] = late_ref[i] - dot(lates[n], early_ref[i])
    for late, (w, i, (early_ref, _)) in zip(lates, places):
        sums = jnp.concatenate([early_ref[i], late], axis=0)
        new_ref[w] = v_ref[w] - dot(factor_ref[w], sums)
        store(w).start()
    for w in range(walkers):
        store(w).wait()


def update_call(order, meta, inverse, factor, rows, sums):
    return pl.pallas_call(
        update_kernel,
        name="update",
        out_shape=jax.ShapeDtypeStruct(inverse.shape, F32),
        in_specs=[SMEM] * 2 + [VMEM] * 7,
        out_specs=ANY,
        scratch_shapes=[
            pltpu.VMEM(inverse.shape, F32),
            pltpu.SemaphoreType.DMA((inverse.shape[0],)),
        ],
        compiler_params=params(),
        cost_estimate=lasting(2),
    )(order, meta, inverse, factor, rows, *sums)


def place_kernel(meta_ref, own_ref, got_ref, *refs):
    out_ref = refs[NMOVE]
    _, walkers, electrons = own_ref.shape
    parts = electrons // got_ref.shape[2]
    lane = lax.broadcasted_iota(jnp.int32, (1, electrons), 1)
    for w in range(walkers):
        here, place, group = parent_of(meta_ref, walkers, w)
        fresh = []
        for b in range(NMOVE):
            block = meta_ref[walkers + b]
            fresh.append((block, roll(refs[b][...], (block - w) * K)))
        for d in range(3):
            at = MOVED + (d + 1) * parts
            far = jnp.concatenate(
                [got_ref[group, at + i : at + i + 1, :] for i in range(parts)], axis=1
            )
            line = jnp.where(here, own_ref[d, pl.ds(place, 1), :], far)
            for block, moved in fresh:
                moved = jnp.concatenate([moved[d : d + 1, :]] * (electrons // 128), axis=1)
                line = jnp.where(lane // K == block, moved, line)
            out_ref[d, w : w + 1, :] = line


def place_call(meta, positions, got, moved):
    return pl.pallas_call(
        place_kernel,
        name="place",
        out_shape=jax.ShapeDtypeStruct(positions.shape, F32),
        in_specs=[SMEM] + [VMEM] * (2 + NMOVE),
        out_specs=VMEM,
        compiler_params=params(),
        cost_estimate=lasting(1),
    )(meta, positions, got, *moved)


def swap(x, axis, k):
    return lax.ppermute(x, axis, [(i, i ^ k) for i in range(lax.axis_size(axis))])


def exchange(part, axis):
    return [part] + [swap(part, axis, k) for k in range(1, lax.axis_size(axis))]


def add_up(mine, axis, done):
    k = 2
    while k < lax.axis_size(axis):
        *others, done = together(*[swap(x, axis, k) for x in mine], done)
        mine = [x + other for x, other in zip(mine, others)]
        k *= 2
    return [(x, swap(x, axis, 1)) for x in mine], done


def together(*values):
    return lax.optimization_barrier(values)


def alltoall(x):
    return lax.all_to_all(x, "walker", split_axis=0, concat_axis=0, tiled=True)


def local(positions, inverse, spline_table, gaussian, accepted, block_order, parent):
    groups = lax.axis_size("walker")
    me = lax.axis_index("walker").astype(jnp.int32)
    parity = lax.rem(lax.axis_index("orb"), 2).astype(jnp.int32)
    meta = jnp.concatenate([parent, block_order[:NMOVE], me[None], parity[None]])
    positions = jnp.transpose(positions, (1, 0, 2))
    gaussian = jnp.transpose(gaussian, (1, 0, 2))

    info = alltoall(pack_call(parent, block_order, positions, gaussian, accepted, groups))
    own, code = columns_call(block_order, inverse, positions)
    states, outgoing, code = route_call(meta, info, own, code)
    got = alltoall(outgoing)
    phi, grad = slopes_call(states, spline_table)
    got, code, phi, grad = together(got, code, phi, grad)
    code = alltoall(code)
    vm, first = select_call(meta, own, got, grad)
    p0 = exchange(first, "orb")

    def step(b, parts, later, carried, phi):
        return step_call(b, parts, later, carried, states, phi, vm, spline_table)

    phi1, later1 = later_call(1, states, spline_table, vm)
    p1, new0, change0, t0 = step(0, p0, [later1], [], phi)
    p1 = exchange(p1, "orb")
    phi2, later2 = later_call(2, states, spline_table, vm)
    p2, new1, change1, t1, y = step(1, p1, [later2], [t0], phi1)
    p2 = exchange(p2, "orb")
    phi3, later3 = later_call(3, states, spline_table, vm)
    p3, new2, change2, t2, y = step(2, p2, [later3], [t1, y], phi2)
    p3 = exchange(p3, "orb")
    whole, mine, give = assemble_call(meta, inverse, got, code, [change0, change1, change2])
    p3, mine, give = together(p3, mine, give)
    early = mine + swap(give, "orb", 1)
    _, new3, change3, t3, _ = step(3, p3, [], [t2, y], phi3)
    mine, give = sums_call(meta, whole, change3)
    late = mine + swap(give, "orb", 1)
    factor, rows = last_call([p2, p3], [t0, t1, t2, t3], vm)
    new_positions = place_call(meta, positions, got, [new0, new1, new2, new3])
    factor, new_positions = together(factor, new_positions)
    (early, late), factor = add_up([early, late], "orb", factor)
    new_inverse = update_call(block_order, meta, whole, factor, rows, [early[0], late[0], early[1], late[1]])
    return jnp.transpose(new_positions, (1, 0, 2)), new_inverse


def solution(mesh):
    return jax.shard_map(
        local,
        mesh=mesh,
        in_specs=(
            P("walker", None, None),
            P("walker", "orb", None),
            P("orb", None),
            P("walker", None, None),
            P("walker", None),
            P(),
            P("walker"),
        ),
        out_specs=(P("walker", None, None), P("walker", "orb", None)),
        check_vma=False,
    )
```

```python
import functools

import jax
import jax.numpy as jnp
from jax import lax
from jax.experimental import pallas as pl
from jax.experimental.pallas import tpu as pltpu
from jax.sharding import PartitionSpec as P

GRID = 24
PLANE = GRID * GRID
WIDE = 640
UNROLL = 12
CHUNKS = (4, 4, 4)
K = 16
NMOVE = 4
MOVED = K * NMOVE
CAP = 1
TAU = 0.25
ROOT_TAU = 0.5
F32 = jnp.float32
BF16 = jnp.bfloat16
LEVELS = 32767.0
HIGHEST = lax.Precision.HIGHEST
VMEM = pl.BlockSpec(memory_space=pltpu.VMEM)
SMEM = pl.BlockSpec(memory_space=pltpu.SMEM)
ANY = pl.BlockSpec(memory_space=pl.ANY)
LIMIT = 16 * 2**20
WHOLE = 60 * 2**20
PART = 59500000
ALMOST = 63300000


def axis_weights(u, with_slopes):
    floors = jnp.floor(u)
    t = u - floors
    remain = 1.0 - t
    square = t * t
    cubed = square * t
    values = (
        remain * remain * remain / 6.0,
        (3.0 * cubed - 6.0 * square + 4.0) / 6.0,
        (-3.0 * cubed + 3.0 * square + 3.0 * t + 1.0) / 6.0,
        cubed / 6.0,
    )
    lanes = u.shape[1]
    line = lax.broadcasted_iota(jnp.int32, (GRID, lanes), 0)
    step = line - (floors.astype(jnp.int32) - 1)
    step = jnp.where(step < 0, step + GRID, step)
    step = jnp.where(step < 0, step + GRID, step)
    step = jnp.where(step >= GRID, step - GRID, step)

    def spread(weights):
        out = jnp.zeros((GRID, lanes), F32)
        for a in range(4):
            out = jnp.where(step == a, jnp.broadcast_to(weights[a], (GRID, lanes)), out)
        return out

    if not with_slopes:
        return spread(values), None
    slopes = (
        -0.5 * remain * remain,
        1.5 * square - 2.0 * t,
        -1.5 * square + t + 0.5,
        0.5 * square,
    )
    return spread(values), spread(slopes)


def halves(first, second):
    product = jnp.concatenate([first[y : y + 1, :] * second for y in range(GRID)], axis=0)
    high = product.astype(BF16)
    return [high, (product - high.astype(F32)).astype(BF16)]


def fill(even_ref, odd_ref, pieces):
    lanes = pieces[0].shape[1]
    pad = jnp.zeros((WIDE - PLANE, lanes), BF16)
    for i, piece in enumerate(pieces):
        at = slice(i * lanes, (i + 1) * lanes)
        even_ref[0:PLANE, at] = piece
        even_ref[PLANE:WIDE, at] = pad
        odd_ref[0 : WIDE - PLANE, at] = pad
        odd_ref[WIDE - PLANE : WIDE, at] = piece


def plane_pair(table_ref, pair, even_ref, odd_ref):
    start = pl.multiple_of(pair * 2 * PLANE, 128)
    even = table_ref[:, pl.ds(start, WIDE)]
    start = pl.multiple_of(pair * 2 * PLANE + 2 * PLANE - WIDE, 128)
    odd = table_ref[:, pl.ds(start, WIDE)]
    return (
        jnp.dot(even, even_ref[...], preferred_element_type=F32),
        jnp.dot(odd, odd_ref[...], preferred_element_type=F32),
    )


def slopes_kernel(
    state_ref, table_ref, phi_ref, grad_ref, even_ref, odd_ref, wx_ref, sx_ref, loads=(), beside=()
):
    n = state_ref.shape[2]
    wx, sx = axis_weights(state_ref[0, 0:1, :], True)
    wy, sy = axis_weights(state_ref[0, 1:2, :], True)
    wz, sz = axis_weights(state_ref[0, 2:3, :], True)
    wx_ref[...] = wx
    sx_ref[...] = sx
    fill(even_ref, odd_ref, halves(wy, wz) + halves(sy, wz) + halves(wy, sz))
    phi_ref[...] = jnp.zeros_like(phi_ref)
    grad_ref[...] = jnp.zeros_like(grad_ref)

    def body(pair, carry):
        even, odd = plane_pair(table_ref, pair, even_ref, odd_ref)
        w0, w1 = wx_ref[pl.ds(2 * pair, 1), :], wx_ref[pl.ds(2 * pair + 1, 1), :]
        s0, s1 = sx_ref[pl.ds(2 * pair, 1), :], sx_ref[pl.ds(2 * pair + 1, 1), :]

        def both(i):
            at, to = slice(2 * i * n, (2 * i + 1) * n), slice((2 * i + 1) * n, (2 * i + 2) * n)
            return even[:, at] + even[:, to], odd[:, at] + odd[:, to]

        e, o = both(0)
        phi_ref[...] += w0 * e + w1 * o
        grad_ref[:, 0:n] += s0 * e + s1 * o
        for d in (1, 2):
            e, o = both(d)
            grad_ref[:, d * n : (d + 1) * n] += w0 * e + w1 * o
        return carry

    pairs = GRID // 2
    if loads:
        start = 0
        for i, (load, size) in enumerate(zip(loads, CHUNKS)):
            load.wait()
            if i + 1 < len(loads):
                loads[i + 1].start()
            if beside[i] is not None:
                beside[i]()
            lax.fori_loop(start, start + size, body, 0, unroll=size)
            start += size
    else:
        lax.fori_loop(0, pairs, body, 0, unroll=UNROLL)


def first_kernel(
    sending_ref, states_ref, table_ref, code_in, phi_out, grad_out, code_out, *refs
):
    held_ref, phi_ref, grad_ref, code_ref = refs[:4]
    scratch, (in_sem, out_sem, code_sem) = refs[4:-3], refs[-3:]
    groups = code_out.shape[0]
    loads = []
    start = 0
    for i, pairs in enumerate(CHUNKS):
        at = pl.ds(start, 2 * PLANE * pairs)
        start += 2 * PLANE * pairs
        loads.append(
            pltpu.make_async_copy(table_ref.at[:, at], held_ref.at[:, at], in_sem.at[i])
        )
    loads[0].start()
    codes = pltpu.make_async_copy(code_in, code_ref, code_sem.at[groups])
    picks = []
    for g in range(groups):
        source = code_ref.at[sending_ref[g]]
        picks.append(pltpu.make_async_copy(source, code_out.at[g], code_sem.at[g]))

    def pick():
        codes.wait()
        for copy in picks:
            copy.start()

    beside = (None, codes.start, pick)
    slopes_kernel(
        states_ref.at[0:1], held_ref, phi_ref, grad_ref, *scratch, loads=loads, beside=beside
    )
    stores = [
        pltpu.make_async_copy(phi_ref, phi_out, out_sem.at[0]),
        pltpu.make_async_copy(grad_ref, grad_out, out_sem.at[1]),
    ]
    for store in stores:
        store.start()
    for store in stores + picks:
        store.wait()


def slopes_call(sending, states, table, code):
    orbitals = table.shape[0]
    n = states.shape[2]
    groups = sending.shape[0]
    shapes = [(orbitals, n), (orbitals, 3 * n)]
    return pl.pallas_call(
        first_kernel,
        name="slopes",
        out_shape=tuple(jax.ShapeDtypeStruct(shape, F32) for shape in shapes)
        + (jax.ShapeDtypeStruct((groups, *code.shape[1:]), code.dtype),),
        in_specs=[SMEM, VMEM, ANY, ANY],
        out_specs=(ANY, ANY, ANY),
        scratch_shapes=[pltpu.VMEM(table.shape, BF16)]
        + [pltpu.VMEM(shape, F32) for shape in shapes]
        + [pltpu.VMEM(code.shape, code.dtype)]
        + slopes_scratch(n)
        + [
            pltpu.SemaphoreType.DMA((len(CHUNKS),)),
            pltpu.SemaphoreType.DMA((2,)),
            pltpu.SemaphoreType.DMA((groups + 1,)),
        ],
        compiler_params=params(WHOLE),
        cost_estimate=lasting(5),
    )(sending, states, table, code)


def slopes_scratch(n):
    return [
        pltpu.VMEM((WIDE, 6 * n), BF16),
        pltpu.VMEM((WIDE, 6 * n), BF16),
        pltpu.VMEM((GRID, n), F32),
        pltpu.VMEM((GRID, n), F32),
    ]


def later_kernel(block, states_ref, table_ref, vm_ref, out_ref, grad_ref, *scratch):
    orbitals = table_ref.shape[0]
    phi_ref = out_ref.at[0:orbitals]
    slopes_kernel(states_ref.at[block : block + 1], table_ref, phi_ref, grad_ref, *scratch)
    drift_rows(block, vm_ref, grad_ref, out_ref, orbitals)


def later_call(block, states, table, vm):
    orbitals = table.shape[0]
    n = states.shape[2]
    return pl.pallas_call(
        functools.partial(later_kernel, block),
        name="later",
        out_shape=jax.ShapeDtypeStruct((orbitals + drift_size(block), n), F32),
        in_specs=[VMEM] * 3,
        out_specs=VMEM,
        scratch_shapes=[pltpu.VMEM((orbitals, 3 * n), F32)] + slopes_scratch(n),
        compiler_params=params(),
        cost_estimate=lasting(5),
    )(states, table, vm)


def split(x):
    high = x.astype(BF16)
    return high, (x - high.astype(F32)).astype(BF16)


def product(a, b, dims):
    (a0, a1), (b0, b1) = split(a), split(b)

    def one(x, y):
        return lax.dot_general(x, y, (dims, ((), ())), preferred_element_type=F32)

    return one(a0, b0) + (one(a0, b1) + one(a1, b0))


def dot(a, b):
    return product(a, b, ((1,), (0,)))


def dot_nt(a, b):
    return product(a, b, ((1,), (1,)))


def own_lanes(n, walker):
    lane = lax.broadcasted_iota(jnp.int32, (MOVED, n), 1)
    return jnp.logical_and(lane >= walker * K, lane < (walker + 1) * K)


def fold(big):
    n = big.shape[1]
    total = jnp.zeros((MOVED, n), F32)
    for w in range(n // K):
        total = jnp.where(own_lanes(n, w), big[w * MOVED : (w + 1) * MOVED, :], total)
    return total


def unit(block, n):
    row = lax.broadcasted_iota(jnp.int32, (MOVED, n), 0)
    lane = lax.broadcasted_iota(jnp.int32, (MOVED, n), 1)
    return jnp.where(row - block * K == lane % K, 1.0, 0.0).astype(F32)


def tree(parts):
    while len(parts) > 1:
        parts = [parts[i] + parts[i + 1] for i in range(0, len(parts), 2)]
    return parts[0]


def total(refs):
    return tree([ref[...] for ref in refs])


def params(limit=LIMIT):
    return pltpu.CompilerParams(vmem_limit_bytes=limit)


def lasting(us):
    return pl.CostEstimate(flops=int(us * 1e8), bytes_accessed=0, transcendentals=0)


def parent_of(meta_ref, walkers, w):
    parent = meta_ref[w]
    group = parent // walkers
    here = group == meta_ref[walkers + NMOVE]
    return here, jnp.where(here, parent % walkers, 0), jnp.where(here, 0, group)


def block_lanes(x, block):
    lane = lax.broadcasted_iota(jnp.int32, x.shape, 1)
    kept = jnp.where(lane // K == block, x, 0.0)
    return tree([kept[:, i : i + 128] for i in range(0, x.shape[1], 128)])


def roll(x, shift):
    if isinstance(shift, int):
        shift = shift % 128
        return x if shift == 0 else pltpu.roll(x, shift, 1)
    return pltpu.roll(x, lax.rem(shift + 1024, 128), 1)


def moved_lanes(x, order_ref):
    line = jnp.zeros((x.shape[0], 128), F32)
    for b in range(NMOVE):
        block = order_ref[b]
        line = line + roll(block_lanes(x, block), (b - block) * K)
    return line


def pack_kernel(parent_ref, order_ref, *refs):
    (out_ref, pos_ref, gauss_ref, acc_ref), sem = refs[3:-1], refs[-1]
    copies = [
        pltpu.make_async_copy(refs[i], refs[i + 4], sem.at[i]) for i in range(3)
    ]
    for copy in copies:
        copy.start()
    for copy in copies:
        copy.wait()
    walkers = pos_ref.shape[1]
    half = jnp.zeros((walkers, 128 - MOVED), F32)
    lane = lax.broadcasted_iota(jnp.int32, (walkers, 128), 1)
    row = lax.broadcasted_iota(jnp.int32, (walkers, 128), 0)
    lines = []
    for d in range(3):
        line = moved_lanes(pos_ref[d], order_ref)
        lines.append(line + jnp.concatenate([half, gauss_ref[d]], axis=1))
    parents = jnp.zeros((walkers, 128), jnp.int32)
    for w in range(walkers):
        parents = jnp.where(row == w, parent_ref[w], parents)
    decided = jnp.concatenate([acc_ref[...].astype(F32), half], axis=1)
    lines.append(jnp.where(lane < MOVED, decided, parents.astype(F32)))
    for g in range(out_ref.shape[0]):
        for d in range(4):
            out_ref[g, d * walkers : (d + 1) * walkers, :] = lines[d]


def pack_call(parent, order, positions, gaussian, accepted, groups):
    walkers = positions.shape[1]
    held = [positions, gaussian, accepted]
    return pl.pallas_call(
        pack_kernel,
        name="pack",
        out_shape=jax.ShapeDtypeStruct((groups, 4 * walkers, 128), F32),
        in_specs=[SMEM, SMEM, ANY, ANY, ANY],
        out_specs=VMEM,
        scratch_shapes=[pltpu.VMEM(x.shape, x.dtype) for x in held]
        + [pltpu.SemaphoreType.DMA((3,))],
        compiler_params=params(WHOLE),
        cost_estimate=lasting(1),
    )(parent, order, *held)


def columns_kernel(order_ref, v_in, pos_in, own_out, code_out, v_ref, pos_ref, own_ref, code_ref, sem):
    walkers, orbitals, electrons = v_ref.shape

    def load(w):
        return pltpu.make_async_copy(v_in.at[w], v_ref.at[w], sem.at[0, w])

    def store(w):
        return (
            pltpu.make_async_copy(own_ref.at[w], own_out.at[w], sem.at[1, w]),
            pltpu.make_async_copy(code_ref.at[w], code_out.at[w], sem.at[2, w]),
        )

    first = pltpu.make_async_copy(pos_in, pos_ref, sem.at[0, walkers])
    first.start()
    for w in range(walkers):
        load(w).start()
    first.wait()

    def body(w, carry):
        load(w).wait()
        v = v_ref[w]
        own_ref[w, 0:MOVED, :] = jnp.transpose(moved_lanes(v, order_ref))[0:MOVED, :]
        size = jnp.abs(v)
        scale = jnp.max(size, axis=0, keepdims=True)
        at = MOVED
        for line in [scale] + [pos_ref[d, pl.ds(w, 1), :] for d in range(3)]:
            for i in range(0, electrons, orbitals):
                own_ref[w, at : at + 1, :] = line[:, i : i + orbitals]
                at += 1
        some = scale > 0.0
        step = jnp.where(some, LEVELS / jnp.sqrt(jnp.where(some, scale, 1.0)), 0.0)
        level = jnp.minimum(jnp.floor(jnp.sqrt(size) * step + 0.5), LEVELS)
        code_ref[w] = jnp.where(v < 0.0, -level, level).astype(jnp.int32).astype(jnp.int16)
        for copy in store(w):
            copy.start()
        return carry

    lax.fori_loop(0, walkers, body, 0)
    for w in range(walkers):
        for copy in store(w):
            copy.wait()


def payload_rows(orbitals, electrons):
    return MOVED + 4 * electrons // orbitals


def columns_call(order, inverse, positions):
    walkers, orbitals, electrons = inverse.shape
    own = (walkers, payload_rows(orbitals, electrons), orbitals)
    return pl.pallas_call(
        columns_kernel,
        name="columns",
        out_shape=(
            jax.ShapeDtypeStruct(own, F32),
            jax.ShapeDtypeStruct(inverse.shape, jnp.int16),
        ),
        in_specs=[SMEM, ANY, ANY],
        out_specs=(ANY, ANY),
        scratch_shapes=[
            pltpu.VMEM(inverse.shape, F32),
            pltpu.VMEM(positions.shape, F32),
            pltpu.VMEM(own, F32),
            pltpu.VMEM(inverse.shape, jnp.int16),
            pltpu.SemaphoreType.DMA((3, walkers + 1)),
        ],
        compiler_params=params(WHOLE),
        cost_estimate=lasting(3),
    )(order, inverse, positions)


def route_kernel(meta_ref, info_in, own_in, states_ref, out_ref, sending_ref, *refs):
    info_ref, own_ref, parents_ref, sem, out_sem = refs
    walkers = own_ref.shape[0]
    groups = out_ref.shape[0]
    rows = 3 * walkers
    asked = []
    for g in range(groups):
        at = pl.ds(rows, walkers)
        asked.append(pltpu.make_async_copy(info_in.at[g, at], parents_ref.at[g], sem.at[2]))
    for each in asked:
        each.start()
    loads = [
        pltpu.make_async_copy(info_in, info_ref, sem.at[0]),
        pltpu.make_async_copy(own_in, own_ref, sem.at[1]),
    ]
    for load in loads:
        load.start()
    for each in asked:
        each.wait()
    me = meta_ref[walkers + NMOVE]
    sending = []
    for g in range(groups):
        wanted = jnp.int32(0)
        for s in range(walkers):
            within = parents_ref[g, s, MOVED].astype(jnp.int32) - me * walkers
            mine = jnp.logical_and(within >= 0, within < walkers)
            wanted = jnp.where(mine, within, wanted)
        sending.append(jnp.where(me == g, 0, wanted))
        sending_ref[g] = sending[g]
    for load in loads[1:]:
        load.wait()
    stores = []
    for g in range(groups):
        source = sending[g]
        stores.append(pltpu.make_async_copy(own_ref.at[source], out_ref.at[g], out_sem.at[g]))
    for store in stores:
        store.start()
    loads[0].wait()
    lane = lax.broadcasted_iota(jnp.int32, (8, 128), 1)
    tiles = []
    for w in range(walkers):
        group, place = meta_ref[w] // walkers, meta_ref[w] % walkers
        line = [info_ref[group, pl.ds(d * walkers + place, 1), :] for d in range(4)]
        line = jnp.concatenate(line, axis=0)
        tiles.append(jnp.concatenate([line, roll(line, 128 - MOVED)], axis=0))
    for b in range(NMOVE):
        state = jnp.zeros((8, 128), F32)
        for w in range(walkers):
            state = jnp.where(lane // K == w, roll(tiles[w], (w - b) * K), state)
        states_ref[b] = state
    for store in stores:
        store.wait()


def route_call(meta, info, own):
    groups = info.shape[0]
    return pl.pallas_call(
        route_kernel,
        name="route",
        out_shape=(
            jax.ShapeDtypeStruct((NMOVE, 8, 128), F32),
            jax.ShapeDtypeStruct((groups, *own.shape[1:]), F32),
            jax.ShapeDtypeStruct((groups,), jnp.int32),
        ),
        in_specs=[SMEM, ANY, ANY],
        out_specs=(VMEM, ANY, SMEM),
        scratch_shapes=[
            pltpu.VMEM(info.shape, F32),
            pltpu.VMEM(own.shape, F32),
            pltpu.SMEM((groups, own.shape[0], 128), F32),
            pltpu.SemaphoreType.DMA((3,)),
            pltpu.SemaphoreType.DMA((groups,)),
        ],
        compiler_params=params(ALMOST),
        cost_estimate=lasting(3),
    )(meta, info, own)


def select_kernel(meta_ref, own_ref, got_ref, grad_in, vm_ref, out_ref, grad_ref, sem):
    walkers = own_ref.shape[0]
    load = pltpu.make_async_copy(grad_in, grad_ref, sem.at[walkers])
    load.start()

    def copy(w, source):
        to = vm_ref.at[w * MOVED : (w + 1) * MOVED]
        return pltpu.make_async_copy(source.at[0:MOVED], to, sem.at[w])

    for w in range(walkers):
        here, place, group = parent_of(meta_ref, walkers, w)

        @pl.when(here)
        def _():
            copy(w, own_ref.at[place]).start()

        @pl.when(jnp.logical_not(here))
        def _():
            copy(w, got_ref.at[group]).start()

    for w in range(walkers):
        copy(w, own_ref.at[0]).wait()
    load.wait()
    drift_rows(0, vm_ref, grad_ref, out_ref, 0)


def drift_size(block):
    return 8 + 3 * K * block


def drift_rows(block, vm_ref, grad_ref, out_ref, at):
    n = grad_ref.shape[1] // 3
    size = K * block
    out_ref[at + 3 : at + 8, :] = jnp.zeros((5, n), F32)
    for d in range(3):
        q = fold(dot(vm_ref[...], grad_ref[:, d * n : (d + 1) * n]))
        out_ref[at + d : at + d + 1, :] = jnp.sum(q * unit(block, n), axis=0, keepdims=True)
        if block:
            out_ref[at + 8 + d * size : at + 8 + (d + 1) * size, :] = q[0:size, :]


def drift_of(block, q, t):
    size = K * block
    lines = [q[0:3, :]]
    if block:
        lines[0] += jnp.concatenate(
            [
                jnp.sum(q[8 + d * size : 8 + (d + 1) * size, :] * t[0:size, :], axis=0)[None]
                for d in range(3)
            ],
            axis=0,
        )
    return lines[0]


def select_call(meta, own, got, grad):
    walkers, _, orbitals = own.shape
    n = grad.shape[1] // 3
    return pl.pallas_call(
        select_kernel,
        name="select",
        out_shape=(
            jax.ShapeDtypeStruct((walkers * MOVED, orbitals), F32),
            jax.ShapeDtypeStruct((drift_size(0), n), F32),
        ),
        in_specs=[SMEM, ANY, ANY, ANY],
        out_specs=(VMEM, VMEM),
        scratch_shapes=[
            pltpu.VMEM(grad.shape, F32),
            pltpu.SemaphoreType.DMA((walkers + 1,)),
        ],
        compiler_params=params(PART),
        cost_estimate=lasting(2),
    )(meta, own, got, grad)


def spread(x):
    n = x.shape[1]
    return jnp.concatenate([jnp.where(own_lanes(n, w), x, 0.0) for w in range(n // K)], axis=0)


BLOCK_ROWS = 8 + MOVED


def log_rows(block, n, kind):
    start = block * (BLOCK_ROWS + n)
    if kind == "moved":
        return slice(start, start + 8)
    if kind == "t":
        return slice(start + 8, start + BLOCK_ROWS)
    return slice(start + BLOCK_ROWS, start + BLOCK_ROWS + n)


def log_y(n):
    start = NMOVE * (BLOCK_ROWS + n)
    return slice(start, start + n // K * MOVED)


def step_kernel(block, count, *refs):
    refs = list(refs)
    last = block == NMOVE - 1
    parts = [refs.pop(0) for _ in range(count)]
    before_ref = refs.pop(0)
    if last:
        meta_ref, whole_ref = refs.pop(0), refs.pop(0)
    else:
        later_ref = refs.pop(0)
    states_ref, vm_ref, table_ref = [refs.pop(0) for _ in range(3)]
    if last:
        mine_ref, give_ref = refs.pop(0), refs.pop(0)
    else:
        s_ref = refs.pop(0)
    log_ref, sum_ref, big_ref, even_ref, odd_ref, wx_ref = refs
    orbitals, n = sum_ref.shape
    y_rows = log_y(n)
    phi_rows = slice(y_rows.stop, y_rows.stop + orbitals)
    if not last:
        s_ref[MOVED:, :] = later_ref[orbitals:, :]
        log_ref[phi_rows, :] = later_ref[0:orbitals, :]
    state = states_ref[block]
    if block == 0:
        phi_ref = before_ref
        t = unit(0, n)
        drifts = drift_of(0, total(parts), None)
    else:
        phi_ref = before_ref.at[phi_rows]
        done = slice(0, block * (BLOCK_ROWS + n))
        log_ref[done, :] = before_ref[done, :]
        t_before = before_ref[log_rows(block - 1, n, "t"), :]
        big_ref[0:MOVED, :] = tree([ref[0:MOVED, :] for ref in parts])
        if block > 1:
            y_before = before_ref[y_rows, 0:MOVED]
            big_ref[MOVED:, :] = dot(y_before, big_ref[0:MOVED, :])
            big_ref[0:MOVED, :] = big_ref[0:MOVED, :] - fold(big_ref[MOVED:, :])
        y_all = dot_nt(spread(big_ref[0:MOVED, :]), t_before)
        if block > 1:
            y_all = y_all + before_ref[y_rows, 0:MOVED]
        log_ref[y_rows, 0:MOVED] = y_all
        start = y_rows.start + block * K
        rows = jnp.concatenate(
            [
                log_ref[start + w * MOVED : start + w * MOVED + K, 0:MOVED]
                for w in range(n // K)
            ],
            axis=0,
        )
        log_ref[log_rows(block, n, "t"), :] = unit(block, n) - jnp.transpose(rows)
        t = log_ref[log_rows(block, n, "t"), :]
        q = tree([ref[MOVED:, :] for ref in parts])
        drifts = drift_of(block, q, t)
    if block == 0:
        log_ref[log_rows(0, n, "t"), :] = t
    speeds = jnp.sum(drifts * drifts, axis=0, keepdims=True)
    capped = drifts / jnp.sqrt(1.0 + TAU * speeds)
    moved = state[0:3, :] + state[3:4, :] * (TAU * capped + ROOT_TAU * state[4:7, :])
    moved_rows = log_rows(block, n, "moved")
    log_ref[moved_rows, :] = jnp.concatenate([moved, jnp.zeros((5, n), F32)], axis=0)
    wx, _ = axis_weights(moved[0:1, :], False)
    wy, _ = axis_weights(moved[1:2, :], False)
    wz, _ = axis_weights(moved[2:3, :], False)
    wx_ref[...] = wx
    fill(even_ref, odd_ref, halves(wy, wz))
    sum_ref[...] = jnp.zeros_like(sum_ref)

    def body(pair, carry):
        even, odd = plane_pair(table_ref, pair, even_ref, odd_ref)
        w0, w1 = wx_ref[pl.ds(2 * pair, 1), :], wx_ref[pl.ds(2 * pair + 1, 1), :]
        sum_ref[...] += w0 * (even[:, 0:n] + even[:, n:]) + w1 * (odd[:, 0:n] + odd[:, n:])
        return carry

    lax.fori_loop(0, GRID // 2, body, 0, unroll=UNROLL)
    change = sum_ref[...] - phi_ref[...]
    change_rows = log_rows(block, n, "change")
    log_ref[change_rows, 0:orbitals] = jnp.transpose(change)
    if not last:
        s_ref[0:MOVED, :] = fold(dot(vm_ref[...], change))
        return
    walkers = whole_ref.shape[0]
    for i in range(walkers // 2):
        for w, out_ref in zip(both_halves(meta_ref, walkers, i), (mine_ref, give_ref)):
            at = pl.ds(pl.multiple_of(change_rows.start + w * K, 8), K)
            out_ref[i] = dot(log_ref[at, 0:orbitals], whole_ref[w])


def step_call(block, parts, before, more, states, vm, table):
    orbitals, n = table.shape[0], states.shape[2]
    rows = vm.shape[0]
    operands = [*parts, before, *more, states, vm, table]
    specs = [VMEM] * len(operands)
    log = (log_y(n).stop + orbitals, 128)
    if block == NMOVE - 1:
        specs[len(parts) + 1] = SMEM
        walkers, _, electrons = more[1].shape
        shapes = [(walkers // 2, K, electrons)] * 2 + [log]
    else:
        shapes = [(MOVED + more[0].shape[0] - orbitals, n), log]
    return pl.pallas_call(
        functools.partial(step_kernel, block, len(parts)),
        name="step",
        out_shape=tuple(jax.ShapeDtypeStruct(shape, F32) for shape in shapes),
        in_specs=specs,
        out_specs=(VMEM,) * len(shapes),
        scratch_shapes=[
            pltpu.VMEM((orbitals, n), F32),
            pltpu.VMEM((MOVED + rows, n), F32),
            pltpu.VMEM((WIDE, 2 * n), BF16),
            pltpu.VMEM((WIDE, 2 * n), BF16),
            pltpu.VMEM((GRID, n), F32),
        ],
        compiler_params=params(),
        cost_estimate=lasting(3),
    )(*operands)


def last_kernel(counts, *refs):
    refs = list(refs)
    sums = [[refs.pop(0) for _ in range(count)] for count in counts]
    log_ref, vm_ref, out_ref, l_ref = refs
    n = log_ref.shape[1]
    ts = [log_ref[log_rows(block, n, "t"), :] for block in range(NMOVE)]
    for block in range(NMOVE - 1):
        r = unit(block, ts[block].shape[1])
        if block:
            sums_of = tree([ref[0:MOVED, :] for ref in sums[block - 1]])
            r = r - fold(dot(l_ref[...], sums_of))
        more = dot_nt(spread(r), ts[block])
        l_ref[...] = l_ref[...] + more if block else more
    t = jnp.transpose(ts[-1])
    for w in range(out_ref.shape[0]):
        at = slice(w * MOVED, (w + 1) * MOVED)
        early = l_ref[w * MOVED : (w + 1) * MOVED - K, :]
        factor = jnp.concatenate([early, t[w * K : (w + 1) * K, :]], axis=0)
        out_ref[w] = jnp.transpose(dot(factor, vm_ref[at, :]))


def last_call(s_parts, log, vm):
    rows, orbitals = vm.shape
    operands = [part for parts in s_parts for part in parts] + [log, vm]
    return pl.pallas_call(
        functools.partial(last_kernel, [len(parts) for parts in s_parts]),
        name="last",
        out_shape=(
            jax.ShapeDtypeStruct((rows // MOVED, orbitals, MOVED), F32),
            jax.ShapeDtypeStruct((rows, MOVED), F32),
        ),
        in_specs=[VMEM] * len(operands),
        out_specs=(VMEM, VMEM),
        compiler_params=params(),
        cost_estimate=lasting(2),
    )(*operands)


def both_halves(meta_ref, walkers, i):
    parity = meta_ref[meta_ref.shape[0] - 1]
    half = walkers // 2
    return i + half * parity, i + half * (1 - parity)


def assemble_kernel(meta_ref, own_ref, got_ref, code_ref, *refs):
    log_ref, v_ref, mine_ref, give_ref, held_ref, sem = refs
    n = log_ref.shape[1]
    walkers, orbitals, electrons = own_ref.shape
    load = pltpu.make_async_copy(code_ref, held_ref, sem)
    load.start()
    load.wait()

    def body(i, carry):
        for w, out_ref in zip(both_halves(meta_ref, walkers, i), (mine_ref, give_ref)):
            here, place, group = parent_of(meta_ref, walkers, w)
            scale = jnp.concatenate(
                [
                    got_ref[group, MOVED + j : MOVED + j + 1, :]
                    for j in range(electrons // orbitals)
                ],
                axis=1,
            )
            level = held_ref[group].astype(jnp.int32).astype(F32) * (1.0 / LEVELS)
            v = jnp.where(here, own_ref[place], level * jnp.abs(level) * scale)
            v_ref[w] = v
            change = []
            for b in range(NMOVE - 1):
                at = log_rows(b, n, "change").start + w * K
                change.append(log_ref[pl.ds(pl.multiple_of(at, 8), K), 0:orbitals])
            change = jnp.concatenate(change, axis=0)
            out_ref[i] = dot(change, v)
        return carry

    lax.fori_loop(0, walkers // 2, body, 0)


def assemble_call(meta, inverse, got, code, log):
    walkers, orbitals, electrons = inverse.shape
    half = (walkers // 2, (NMOVE - 1) * K, electrons)
    return pl.pallas_call(
        assemble_kernel,
        name="assemble",
        out_shape=(
            jax.ShapeDtypeStruct(inverse.shape, F32),
            jax.ShapeDtypeStruct(half, F32),
            jax.ShapeDtypeStruct(half, F32),
        ),
        in_specs=[SMEM, VMEM, VMEM, ANY, VMEM],
        out_specs=(VMEM,) * 3,
        scratch_shapes=[
            pltpu.VMEM(code.shape, code.dtype),
            pltpu.SemaphoreType.DMA(()),
        ],
        compiler_params=params(),
        cost_estimate=lasting(4),
    )(meta, inverse, got, code, log)


def update_kernel(order_ref, meta_ref, v_ref, factor_ref, l_ref, *refs):
    sums_refs, (out_ref, new_ref, sem) = refs[:4], refs[4:]
    walkers = v_ref.shape[0]

    def store(w):
        return pltpu.make_async_copy(new_ref.at[w], out_ref.at[w], sem.at[w])

    half = walkers // 2
    own = [both_halves(meta_ref, walkers, i) for i in range(half)]
    places = [(own[i][h], i, sums_refs[2 * h : 2 * h + 2]) for i in range(half) for h in range(2)]
    lates = []
    for w, i, (early_ref, late_ref) in places:
        moved = moved_lanes(late_ref[i], order_ref)[:, 0:MOVED]
        rows = l_ref[pl.ds(pl.multiple_of(w * MOVED, MOVED), MOVED), :]
        lates.append(dot_nt(moved, rows)[:, 0 : MOVED - K])
    for n, (w, i, (early_ref, late_ref)) in enumerate(places):
        lates[n] = late_ref[i] - dot(lates[n], early_ref[i])
    for late, (w, i, (early_ref, _)) in zip(lates, places):
        sums = jnp.concatenate([early_ref[i], late], axis=0)
        new_ref[w] = v_ref[w] - dot(factor_ref[w], sums)
        store(w).start()
    for w in range(walkers):
        store(w).wait()


def update_call(order, meta, inverse, factor, rows, sums):
    return pl.pallas_call(
        update_kernel,
        name="update",
        out_shape=jax.ShapeDtypeStruct(inverse.shape, F32),
        in_specs=[SMEM] * 2 + [VMEM] * 7,
        out_specs=ANY,
        scratch_shapes=[
            pltpu.VMEM(inverse.shape, F32),
            pltpu.SemaphoreType.DMA((inverse.shape[0],)),
        ],
        compiler_params=params(),
        cost_estimate=lasting(2),
    )(order, meta, inverse, factor, rows, *sums)


def place_kernel(meta_ref, own_ref, got_ref, log_ref, out_ref):
    _, walkers, electrons = own_ref.shape
    parts = electrons // got_ref.shape[2]
    lane = lax.broadcasted_iota(jnp.int32, (1, electrons), 1)
    for w in range(walkers):
        here, place, group = parent_of(meta_ref, walkers, w)
        fresh = []
        for b in range(NMOVE):
            block = meta_ref[walkers + b]
            moved = log_ref[log_rows(b, log_ref.shape[1], "moved"), :]
            fresh.append((block, roll(moved, (block - w) * K)))
        for d in range(3):
            at = MOVED + (d + 1) * parts
            far = jnp.concatenate(
                [got_ref[group, at + i : at + i + 1, :] for i in range(parts)], axis=1
            )
            line = jnp.where(here, own_ref[d, pl.ds(place, 1), :], far)
            for block, moved in fresh:
                moved = jnp.concatenate([moved[d : d + 1, :]] * (electrons // 128), axis=1)
                line = jnp.where(lane // K == block, moved, line)
            out_ref[d, w : w + 1, :] = line


def place_call(meta, positions, got, log):
    return pl.pallas_call(
        place_kernel,
        name="place",
        out_shape=jax.ShapeDtypeStruct(positions.shape, F32),
        in_specs=[SMEM] + [VMEM] * 3,
        out_specs=VMEM,
        compiler_params=params(),
        cost_estimate=lasting(1),
    )(meta, positions, got, log)


def swap(x, axis, k):
    return lax.ppermute(x, axis, [(i, i ^ k) for i in range(lax.axis_size(axis))])


def exchange(part, axis):
    return [part] + [swap(part, axis, k) for k in range(1, lax.axis_size(axis))]


def add_up(mine, axis, done):
    k = 2
    while k < lax.axis_size(axis):
        *others, done = together(*[swap(x, axis, k) for x in mine], done)
        mine = [x + other for x, other in zip(mine, others)]
        k *= 2
    return [(x, swap(x, axis, 1)) for x in mine], done


def together(*values):
    return lax.optimization_barrier(values)


def alltoall(x):
    return lax.all_to_all(x, "walker", split_axis=0, concat_axis=0, tiled=True)


def local(positions, inverse, spline_table, gaussian, accepted, block_order, parent):
    groups = lax.axis_size("walker")
    me = lax.axis_index("walker").astype(jnp.int32)
    parity = lax.rem(lax.axis_index("orb"), 2).astype(jnp.int32)
    meta = jnp.concatenate([parent, block_order[:NMOVE], me[None], parity[None]])
    positions = jnp.transpose(positions, (1, 0, 2))
    gaussian = jnp.transpose(gaussian, (1, 0, 2))

    info = alltoall(pack_call(parent, block_order, positions, gaussian, accepted, groups))
    own, code = columns_call(block_order, inverse, positions)
    states, outgoing, sending = route_call(meta, info, own)
    got = alltoall(outgoing)
    phi, grad, code = slopes_call(sending, states, spline_table, code)
    got, code, phi, grad = together(got, code, phi, grad)
    code = alltoall(code)
    vm, first = select_call(meta, own, got, grad)
    p0 = exchange(first, "orb")

    def step(b, parts, before, more):
        return step_call(b, parts, before, more, states, vm, spline_table)

    later = later_call(1, states, spline_table, vm)
    p1, log = step(0, p0, phi, [later])
    p1 = exchange(p1, "orb")
    later = later_call(2, states, spline_table, vm)
    p2, log = step(1, p1, log, [later])
    p2 = exchange(p2, "orb")
    held, code = together(states, code)
    later = later_call(3, held, spline_table, vm)
    p3, log = step(2, p2, log, [later])
    p3 = exchange(p3, "orb")
    whole, mine, give = assemble_call(meta, inverse, got, code, log)
    p3, mine, give = together(p3, mine, give)
    early = mine + swap(give, "orb", 1)
    mine, give, log = step(3, p3, log, [meta, whole])
    late = mine + swap(give, "orb", 1)
    factor, rows = last_call([p2, p3], log, vm)
    new_positions = place_call(meta, positions, got, log)
    factor, new_positions = together(factor, new_positions)
    (early, late), factor = add_up([early, late], "orb", factor)
    new_inverse = update_call(block_order, meta, whole, factor, rows, [early[0], late[0], early[1], late[1]])
    return jnp.transpose(new_positions, (1, 0, 2)), new_inverse


def solution(mesh):
    return jax.shard_map(
        local,
        mesh=mesh,
        in_specs=(
            P("walker", None, None),
            P("walker", "orb", None),
            P("orb", None),
            P("walker", None, None),
            P("walker", None),
            P(),
            P("walker"),
        ),
        out_specs=(P("walker", None, None), P("walker", "orb", None)),
        check_vma=False,
    )
```

```python
import functools

import jax
import jax.numpy as jnp
from jax import lax
from jax.experimental import pallas as pl
from jax.experimental.pallas import tpu as pltpu
from jax.sharding import PartitionSpec as P

GRID = 24
PLANE = GRID * GRID
MAIN = 512
EDGE = PLANE - MAIN
UNROLL = 12
CHUNKS = (4, 4, 4)
K = 16
NMOVE = 4
MOVED = K * NMOVE
CAP = 1
TAU = 0.25
ROOT_TAU = 0.5
F32 = jnp.float32
BF16 = jnp.bfloat16
LEVELS = 32767.0
LOG2_E = 1.4426950408889634
HIGHEST = lax.Precision.HIGHEST
VMEM = pl.BlockSpec(memory_space=pltpu.VMEM)
SMEM = pl.BlockSpec(memory_space=pltpu.SMEM)
ANY = pl.BlockSpec(memory_space=pl.ANY)
LIMIT = 16 * 2**20
WHOLE = 60 * 2**20
PART = 59500000
ALMOST = 63300000


def axis_weights(u, with_slopes):
    floors = jnp.floor(u)
    t = u - floors
    remain = 1.0 - t
    square = t * t
    cubed = square * t
    values = (
        remain * remain * remain / 6.0,
        (3.0 * cubed - 6.0 * square + 4.0) / 6.0,
        (-3.0 * cubed + 3.0 * square + 3.0 * t + 1.0) / 6.0,
        cubed / 6.0,
    )
    lanes = u.shape[1]
    line = lax.broadcasted_iota(jnp.int32, (GRID, lanes), 0)
    step = line - (floors.astype(jnp.int32) - 1)
    step = jnp.where(step < 0, step + GRID, step)
    step = jnp.where(step < 0, step + GRID, step)
    step = jnp.where(step >= GRID, step - GRID, step)

    def spread(weights):
        out = jnp.zeros((GRID, lanes), F32)
        for a in range(4):
            out = jnp.where(step == a, jnp.broadcast_to(weights[a], (GRID, lanes)), out)
        return out

    if not with_slopes:
        return spread(values), None
    slopes = (
        -0.5 * remain * remain,
        1.5 * square - 2.0 * t,
        -1.5 * square + t + 0.5,
        0.5 * square,
    )
    return spread(values), spread(slopes)


def products(first, second):
    return jnp.concatenate([first[y : y + 1, :] * second for y in range(GRID)], axis=0)


def fill(whole_ref, edge_ref, weights):
    n = edge_ref.shape[1]
    for i, weight in enumerate(weights):
        for j, piece in enumerate(split(weight)):
            whole_ref[:, (2 * i + j) * n : (2 * i + j + 1) * n] = piece
        edge_ref[2 * EDGE * i : 2 * EDGE * i + EDGE, :] = weight[MAIN:PLANE, :]
        edge_ref[2 * EDGE * i + EDGE : 2 * EDGE * (i + 1), :] = weight[0:EDGE, :]


def plane_pair(table_ref, pair, whole_ref):
    start = pl.multiple_of(pair * 2 * PLANE, 128)
    even = table_ref[:, pl.ds(start, MAIN)]
    start = pl.multiple_of(pair * 2 * PLANE + MAIN + 128, 128)
    odd = table_ref[:, pl.ds(start, MAIN)]
    return (
        jnp.dot(even, whole_ref[0:MAIN, :], preferred_element_type=F32),
        jnp.dot(odd, whole_ref[EDGE:PLANE, :], preferred_element_type=F32),
    )


def middle_weights(mid_ref, edge_ref, pair, terms):
    n = edge_ref.shape[1]
    at = pl.ds(pl.multiple_of(pair * 128, 128), 128)
    for i, (kind, w0, w1) in enumerate(terms):
        start = 2 * EDGE * kind
        part = jnp.concatenate(
            [
                w0 * edge_ref[start : start + EDGE, :],
                w1 * edge_ref[start + EDGE : start + 2 * EDGE, :],
            ],
            axis=0,
        )
        for j, piece in enumerate(split(part)):
            mid_ref[at, (2 * i + j) * n : (2 * i + j + 1) * n] = piece


def middle(table_ref, mid_ref):
    lanes = [
        table_ref[:, q * 2 * PLANE + MAIN : q * 2 * PLANE + MAIN + 128] for q in range(GRID // 2)
    ]
    lanes = jnp.concatenate(lanes, axis=1)
    return jnp.dot(lanes, mid_ref[...], preferred_element_type=F32)


def slopes_kernel(
    state_ref, table_ref, phi_ref, grad_ref, whole_ref, mid_ref, edge_ref, wx_ref, sx_ref,
    loads=(), beside=()
):
    n = state_ref.shape[2]
    wx, sx = axis_weights(state_ref[0, 0:1, :], True)
    wy, sy = axis_weights(state_ref[0, 1:2, :], True)
    wz, sz = axis_weights(state_ref[0, 2:3, :], True)
    wx_ref[...] = wx
    sx_ref[...] = sx
    fill(whole_ref, edge_ref, [products(wy, wz), products(sy, wz), products(wy, sz)])
    phi_ref[...] = jnp.zeros_like(phi_ref)
    grad_ref[...] = jnp.zeros_like(grad_ref)

    def body(pair, carry):
        even, odd = plane_pair(table_ref, pair, whole_ref)
        w0, w1 = wx_ref[pl.ds(2 * pair, 1), :], wx_ref[pl.ds(2 * pair + 1, 1), :]
        s0, s1 = sx_ref[pl.ds(2 * pair, 1), :], sx_ref[pl.ds(2 * pair + 1, 1), :]
        terms = [(0, w0, w1), (0, s0, s1), (1, w0, w1), (2, w0, w1)]
        middle_weights(mid_ref, edge_ref, pair, terms)

        def both(i):
            at, to = slice(2 * i * n, (2 * i + 1) * n), slice((2 * i + 1) * n, (2 * i + 2) * n)
            return even[:, at] + even[:, to], odd[:, at] + odd[:, to]

        e, o = both(0)
        phi_ref[...] += w0 * e + w1 * o
        grad_ref[:, 0:n] += s0 * e + s1 * o
        for d in (1, 2):
            e, o = both(d)
            grad_ref[:, d * n : (d + 1) * n] += w0 * e + w1 * o
        return carry

    pairs = GRID // 2
    if loads:
        start = 0
        for i, (load, size) in enumerate(zip(loads, CHUNKS)):
            load.wait()
            if i + 1 < len(loads):
                loads[i + 1].start()
            if beside[i] is not None:
                beside[i]()
            lax.fori_loop(start, start + size, body, 0, unroll=size)
            start += size
    else:
        lax.fori_loop(0, pairs, body, 0, unroll=UNROLL)
    rest = middle(table_ref, mid_ref)
    phi_ref[...] += rest[:, 0:n] + rest[:, n : 2 * n]
    for d in range(3):
        at = 2 * (d + 1) * n
        grad_ref[:, d * n : (d + 1) * n] += rest[:, at : at + n] + rest[:, at + n : at + 2 * n]


def first_kernel(
    sending_ref, states_ref, table_ref, code_in, phi_out, grad_out, code_out, *refs
):
    held_ref, phi_ref, grad_ref, code_ref = refs[:4]
    scratch, (in_sem, out_sem, code_sem) = refs[4:-3], refs[-3:]
    groups = code_out.shape[0]
    loads = []
    start = 0
    for i, pairs in enumerate(CHUNKS):
        at = pl.ds(start, 2 * PLANE * pairs)
        start += 2 * PLANE * pairs
        loads.append(
            pltpu.make_async_copy(table_ref.at[:, at], held_ref.at[:, at], in_sem.at[i])
        )
    loads[0].start()
    codes = pltpu.make_async_copy(code_in, code_ref, code_sem.at[groups])
    picks = []
    for g in range(groups):
        source = code_ref.at[sending_ref[g]]
        picks.append(pltpu.make_async_copy(source, code_out.at[g], code_sem.at[g]))

    def pick():
        codes.wait()
        for copy in picks:
            copy.start()

    beside = (None, codes.start, pick)
    slopes_kernel(
        states_ref.at[0:1], held_ref, phi_ref, grad_ref, *scratch, loads=loads, beside=beside
    )
    stores = [
        pltpu.make_async_copy(phi_ref, phi_out, out_sem.at[0]),
        pltpu.make_async_copy(grad_ref, grad_out, out_sem.at[1]),
    ]
    for store in stores:
        store.start()
    for store in stores + picks:
        store.wait()


def slopes_call(sending, states, table, code):
    orbitals = table.shape[0]
    n = states.shape[2]
    groups = sending.shape[0]
    shapes = [(orbitals, n), (orbitals, 3 * n)]
    return pl.pallas_call(
        first_kernel,
        name="slopes",
        out_shape=tuple(jax.ShapeDtypeStruct(shape, F32) for shape in shapes)
        + (jax.ShapeDtypeStruct((groups, *code.shape[1:]), code.dtype),),
        in_specs=[SMEM, VMEM, ANY, ANY],
        out_specs=(ANY, ANY, ANY),
        scratch_shapes=[pltpu.VMEM(table.shape, BF16)]
        + [pltpu.VMEM(shape, F32) for shape in shapes]
        + [pltpu.VMEM(code.shape, code.dtype)]
        + slopes_scratch(n)
        + [
            pltpu.SemaphoreType.DMA((len(CHUNKS),)),
            pltpu.SemaphoreType.DMA((2,)),
            pltpu.SemaphoreType.DMA((groups + 1,)),
        ],
        compiler_params=params(WHOLE),
        cost_estimate=lasting(5),
    )(sending, states, table, code)


def slopes_scratch(n):
    return weights_scratch(n, 3, 4) + [pltpu.VMEM((GRID, n), F32)]


def weights_scratch(n, kinds, terms):
    return [
        pltpu.VMEM((PLANE, 2 * kinds * n), BF16),
        pltpu.VMEM((GRID // 2 * 128, 2 * terms * n), BF16),
        pltpu.VMEM((2 * EDGE * kinds, n), F32),
        pltpu.VMEM((GRID, n), F32),
    ]


def later_kernel(block, states_ref, table_ref, vm_ref, out_ref, grad_ref, *scratch):
    orbitals = table_ref.shape[0]
    phi_ref = out_ref.at[0:orbitals]
    slopes_kernel(states_ref.at[block : block + 1], table_ref, phi_ref, grad_ref, *scratch)
    drift_rows(block, vm_ref, grad_ref, out_ref, orbitals)


def later_call(block, states, table, vm):
    orbitals = table.shape[0]
    n = states.shape[2]
    return pl.pallas_call(
        functools.partial(later_kernel, block),
        name="later",
        out_shape=jax.ShapeDtypeStruct((orbitals + drift_size(block), n), F32),
        in_specs=[VMEM] * 3,
        out_specs=VMEM,
        scratch_shapes=[pltpu.VMEM((orbitals, 3 * n), F32)] + slopes_scratch(n),
        compiler_params=params(),
        cost_estimate=lasting(5),
    )(states, table, vm)


def split(x):
    high = x.astype(BF16)
    return high, (x - high.astype(F32)).astype(BF16)


def product(a, b, dims):
    (a0, a1), (b0, b1) = split(a), split(b)

    def one(x, y):
        return lax.dot_general(x, y, (dims, ((), ())), preferred_element_type=F32)

    return one(a0, b0) + (one(a0, b1) + one(a1, b0))


def dot(a, b):
    return product(a, b, ((1,), (0,)))


def dot_nt(a, b):
    return product(a, b, ((1,), (1,)))


def own_lanes(rows, n, walker):
    lane = lax.broadcasted_iota(jnp.int32, (rows, n), 1)
    return jnp.logical_and(lane >= walker * K, lane < (walker + 1) * K)


def fold(big):
    n = big.shape[1]
    rows = big.shape[0] // (n // K)
    total = jnp.zeros((rows, n), F32)
    for w in range(n // K):
        total = jnp.where(own_lanes(rows, n, w), big[w * rows : (w + 1) * rows, :], total)
    return total


def unit(block, n):
    row = lax.broadcasted_iota(jnp.int32, (MOVED, n), 0)
    lane = lax.broadcasted_iota(jnp.int32, (MOVED, n), 1)
    return jnp.where(row - block * K == lane % K, 1.0, 0.0).astype(F32)


def tree(parts):
    while len(parts) > 1:
        parts = [parts[i] + parts[i + 1] for i in range(0, len(parts), 2)]
    return parts[0]


def total(refs):
    return tree([ref[...] for ref in refs])


def params(limit=LIMIT):
    return pltpu.CompilerParams(vmem_limit_bytes=limit)


def lasting(us):
    return pl.CostEstimate(flops=int(us * 1e8), bytes_accessed=0, transcendentals=0)


def parent_of(meta_ref, walkers, w):
    parent = meta_ref[w]
    group = parent // walkers
    here = group == meta_ref[walkers + NMOVE]
    return here, jnp.where(here, parent % walkers, 0), jnp.where(here, 0, group)


def block_lanes(x, block):
    lane = lax.broadcasted_iota(jnp.int32, x.shape, 1)
    kept = jnp.where(lane // K == block, x, 0.0)
    return tree([kept[:, i : i + 128] for i in range(0, x.shape[1], 128)])


def roll(x, shift):
    if isinstance(shift, int):
        shift = shift % 128
        return x if shift == 0 else pltpu.roll(x, shift, 1)
    return pltpu.roll(x, lax.rem(shift + 1024, 128), 1)


def moved_lanes(x, order_ref):
    line = jnp.zeros((x.shape[0], 128), F32)
    for b in range(NMOVE):
        block = order_ref[b]
        line = line + roll(block_lanes(x, block), (b - block) * K)
    return line


def pack_kernel(parent_ref, order_ref, *refs):
    (out_ref, pos_ref, gauss_ref, acc_ref), sem = refs[3:-1], refs[-1]
    copies = [
        pltpu.make_async_copy(refs[i], refs[i + 4], sem.at[i]) for i in range(3)
    ]
    for copy in copies:
        copy.start()
    for copy in copies:
        copy.wait()
    walkers = pos_ref.shape[1]
    half = jnp.zeros((walkers, 128 - MOVED), F32)
    lane = lax.broadcasted_iota(jnp.int32, (walkers, 128), 1)
    row = lax.broadcasted_iota(jnp.int32, (walkers, 128), 0)
    lines = []
    for d in range(3):
        line = moved_lanes(pos_ref[d], order_ref)
        lines.append(line + jnp.concatenate([half, gauss_ref[d]], axis=1))
    parents = jnp.zeros((walkers, 128), jnp.int32)
    for w in range(walkers):
        parents = jnp.where(row == w, parent_ref[w], parents)
    decided = jnp.concatenate([acc_ref[...].astype(F32), half], axis=1)
    lines.append(jnp.where(lane < MOVED, decided, parents.astype(F32)))
    for g in range(out_ref.shape[0]):
        for d in range(4):
            out_ref[g, d * walkers : (d + 1) * walkers, :] = lines[d]


def pack_call(parent, order, positions, gaussian, accepted, groups):
    walkers = positions.shape[1]
    held = [positions, gaussian, accepted]
    return pl.pallas_call(
        pack_kernel,
        name="pack",
        out_shape=jax.ShapeDtypeStruct((groups, 4 * walkers, 128), F32),
        in_specs=[SMEM, SMEM, ANY, ANY, ANY],
        out_specs=VMEM,
        scratch_shapes=[pltpu.VMEM(x.shape, x.dtype) for x in held]
        + [pltpu.SemaphoreType.DMA((3,))],
        compiler_params=params(WHOLE),
        cost_estimate=lasting(1),
    )(parent, order, *held)


def columns_kernel(order_ref, v_in, pos_in, own_out, code_out, v_ref, pos_ref, own_ref, code_ref, sem):
    walkers, orbitals, electrons = v_ref.shape

    def load(w):
        return pltpu.make_async_copy(v_in.at[w], v_ref.at[w], sem.at[0, w])

    def store(w):
        return (
            pltpu.make_async_copy(own_ref.at[w], own_out.at[w], sem.at[1, w]),
            pltpu.make_async_copy(code_ref.at[w], code_out.at[w], sem.at[2, w]),
        )

    first = pltpu.make_async_copy(pos_in, pos_ref, sem.at[0, walkers])
    first.start()
    for w in range(walkers):
        load(w).start()
    first.wait()

    def body(w, carry):
        load(w).wait()
        v = v_ref[w]
        own_ref[w, 0:MOVED, :] = jnp.transpose(moved_lanes(v, order_ref))[0:MOVED, :]
        size = jnp.abs(v)
        scale = jnp.max(size, axis=0, keepdims=True)
        at = MOVED
        for line in [scale] + [pos_ref[d, pl.ds(w, 1), :] for d in range(3)]:
            for i in range(0, electrons, orbitals):
                own_ref[w, at : at + 1, :] = line[:, i : i + orbitals]
                at += 1
        some = scale > 0.0
        step = jnp.where(some, LEVELS / jnp.sqrt(jnp.where(some, scale, 1.0)), 0.0)
        level = jnp.minimum(jnp.floor(jnp.sqrt(size) * step + 0.5), LEVELS)
        code_ref[w] = jnp.where(v < 0.0, -level, level).astype(jnp.int32).astype(jnp.int16)
        for copy in store(w):
            copy.start()
        return carry

    lax.fori_loop(0, walkers, body, 0)
    for w in range(walkers):
        for copy in store(w):
            copy.wait()


def payload_rows(orbitals, electrons):
    return MOVED + 4 * electrons // orbitals


def columns_call(order, inverse, positions):
    walkers, orbitals, electrons = inverse.shape
    own = (walkers, payload_rows(orbitals, electrons), orbitals)
    return pl.pallas_call(
        columns_kernel,
        name="columns",
        out_shape=(
            jax.ShapeDtypeStruct(own, F32),
            jax.ShapeDtypeStruct(inverse.shape, jnp.int16),
        ),
        in_specs=[SMEM, ANY, ANY],
        out_specs=(ANY, ANY),
        scratch_shapes=[
            pltpu.VMEM(inverse.shape, F32),
            pltpu.VMEM(positions.shape, F32),
            pltpu.VMEM(own, F32),
            pltpu.VMEM(inverse.shape, jnp.int16),
            pltpu.SemaphoreType.DMA((3, walkers + 1)),
        ],
        compiler_params=params(WHOLE),
        cost_estimate=lasting(3),
    )(order, inverse, positions)


def route_kernel(meta_ref, info_in, own_in, states_ref, out_ref, sending_ref, *refs):
    info_ref, own_ref, parents_ref, sem, out_sem = refs
    walkers = own_ref.shape[0]
    groups = out_ref.shape[0]
    rows = 3 * walkers
    asked = []
    for g in range(groups):
        at = pl.ds(rows, walkers)
        asked.append(pltpu.make_async_copy(info_in.at[g, at], parents_ref.at[g], sem.at[2]))
    for each in asked:
        each.start()
    loads = [
        pltpu.make_async_copy(info_in, info_ref, sem.at[0]),
        pltpu.make_async_copy(own_in, own_ref, sem.at[1]),
    ]
    for load in loads:
        load.start()
    for each in asked:
        each.wait()
    me = meta_ref[walkers + NMOVE]
    sending = []
    for g in range(groups):
        wanted = jnp.int32(0)
        for s in range(walkers):
            within = parents_ref[g, s, MOVED].astype(jnp.int32) - me * walkers
            mine = jnp.logical_and(within >= 0, within < walkers)
            wanted = jnp.where(mine, within, wanted)
        sending.append(jnp.where(me == g, 0, wanted))
        sending_ref[g] = sending[g]
    for load in loads[1:]:
        load.wait()
    stores = []
    for g in range(groups):
        source = sending[g]
        stores.append(pltpu.make_async_copy(own_ref.at[source], out_ref.at[g], out_sem.at[g]))
    for store in stores:
        store.start()
    loads[0].wait()
    lane = lax.broadcasted_iota(jnp.int32, (8, 128), 1)
    tiles = []
    for w in range(walkers):
        group, place = meta_ref[w] // walkers, meta_ref[w] % walkers
        line = [info_ref[group, pl.ds(d * walkers + place, 1), :] for d in range(4)]
        line = jnp.concatenate(line, axis=0)
        tiles.append(jnp.concatenate([line, roll(line, 128 - MOVED)], axis=0))
    for b in range(NMOVE):
        state = jnp.zeros((8, 128), F32)
        for w in range(walkers):
            state = jnp.where(lane // K == w, roll(tiles[w], (w - b) * K), state)
        states_ref[b] = state
    for store in stores:
        store.wait()


def route_call(meta, info, own):
    groups = info.shape[0]
    return pl.pallas_call(
        route_kernel,
        name="route",
        out_shape=(
            jax.ShapeDtypeStruct((NMOVE, 8, 128), F32),
            jax.ShapeDtypeStruct((groups, *own.shape[1:]), F32),
            jax.ShapeDtypeStruct((groups,), jnp.int32),
        ),
        in_specs=[SMEM, ANY, ANY],
        out_specs=(VMEM, ANY, SMEM),
        scratch_shapes=[
            pltpu.VMEM(info.shape, F32),
            pltpu.VMEM(own.shape, F32),
            pltpu.SMEM((groups, own.shape[0], 128), F32),
            pltpu.SemaphoreType.DMA((3,)),
            pltpu.SemaphoreType.DMA((groups,)),
        ],
        compiler_params=params(ALMOST),
        cost_estimate=lasting(3),
    )(meta, info, own)


def select_kernel(meta_ref, own_ref, got_ref, grad_in, vm_ref, out_ref, grad_ref, sem):
    walkers = own_ref.shape[0]
    load = pltpu.make_async_copy(grad_in, grad_ref, sem.at[walkers])
    load.start()

    def copy(w, source):
        to = vm_ref.at[w * MOVED : (w + 1) * MOVED]
        return pltpu.make_async_copy(source.at[0:MOVED], to, sem.at[w])

    for w in range(walkers):
        here, place, group = parent_of(meta_ref, walkers, w)

        @pl.when(here)
        def _():
            copy(w, own_ref.at[place]).start()

        @pl.when(jnp.logical_not(here))
        def _():
            copy(w, got_ref.at[group]).start()

    for w in range(walkers):
        copy(w, own_ref.at[0]).wait()
    load.wait()
    drift_rows(0, vm_ref, grad_ref, out_ref, 0)


def drift_size(block):
    return 8 + 3 * K * block


def drift_rows(block, vm_ref, grad_ref, out_ref, at):
    n = grad_ref.shape[1] // 3
    size = K * block
    used = size + K
    rows = [vm_ref[w * MOVED : w * MOVED + used, :] for w in range(n // K)]
    big = dot(jnp.concatenate(rows, axis=0), grad_ref[...])
    out_ref[at + 3 : at + 8, :] = jnp.zeros((5, n), F32)
    for d in range(3):
        q = fold(big[:, d * n : (d + 1) * n])
        own = q[size:used, :] * unit(0, n)[0:K, :]
        out_ref[at + d : at + d + 1, :] = jnp.sum(own, axis=0, keepdims=True)
        if block:
            out_ref[at + 8 + d * size : at + 8 + (d + 1) * size, :] = q[0:size, :]


def drift_of(block, q, t):
    size = K * block
    lines = [q[0:3, :]]
    if block:
        lines[0] += jnp.concatenate(
            [
                jnp.sum(q[8 + d * size : 8 + (d + 1) * size, :] * t[0:size, :], axis=0)[None]
                for d in range(3)
            ],
            axis=0,
        )
    return lines[0]


def select_call(meta, own, got, grad):
    walkers, _, orbitals = own.shape
    n = grad.shape[1] // 3
    return pl.pallas_call(
        select_kernel,
        name="select",
        out_shape=(
            jax.ShapeDtypeStruct((walkers * MOVED, orbitals), F32),
            jax.ShapeDtypeStruct((drift_size(0), n), F32),
        ),
        in_specs=[SMEM, ANY, ANY, ANY],
        out_specs=(VMEM, VMEM),
        scratch_shapes=[
            pltpu.VMEM(grad.shape, F32),
            pltpu.SemaphoreType.DMA((walkers + 1,)),
        ],
        compiler_params=params(PART),
        cost_estimate=lasting(2),
    )(meta, own, got, grad)


def spread(x):
    n = x.shape[1]
    return jnp.concatenate([jnp.where(own_lanes(x.shape[0], n, w), x, 0.0) for w in range(n // K)], axis=0)


BLOCK_ROWS = 8 + MOVED


def log_rows(block, n, kind):
    start = block * (BLOCK_ROWS + n)
    if kind == "moved":
        return slice(start, start + 8)
    if kind == "t":
        return slice(start + 8, start + BLOCK_ROWS)
    return slice(start + BLOCK_ROWS, start + BLOCK_ROWS + n)


def log_y(n):
    start = NMOVE * (BLOCK_ROWS + n)
    return slice(start, start + n // K * MOVED)


def step_kernel(block, count, *refs):
    refs = list(refs)
    last = block == NMOVE - 1
    parts = [refs.pop(0) for _ in range(count)]
    before_ref = refs.pop(0)
    if last:
        meta_ref, whole_ref = refs.pop(0), refs.pop(0)
    else:
        later_ref = refs.pop(0)
    states_ref, vm_ref, table_ref = [refs.pop(0) for _ in range(3)]
    if last:
        mine_ref, give_ref = refs.pop(0), refs.pop(0)
    else:
        s_ref = refs.pop(0)
    log_ref, sum_ref, big_ref, wide_ref, mid_ref, edge_ref, wx_ref = refs
    orbitals, n = sum_ref.shape
    y_rows = log_y(n)
    phi_rows = slice(y_rows.stop, y_rows.stop + orbitals)
    if not last:
        s_ref[MOVED:, :] = later_ref[orbitals:, :]
        log_ref[phi_rows, :] = later_ref[0:orbitals, :]
    state = states_ref[block]
    if block == 0:
        phi_ref = before_ref
        t = unit(0, n)
        drifts = drift_of(0, total(parts), None)
    else:
        phi_ref = before_ref.at[phi_rows]
        done = slice(0, block * (BLOCK_ROWS + n))
        log_ref[done, :] = before_ref[done, :]
        t_before = before_ref[log_rows(block - 1, n, "t"), :]
        big_ref[0:MOVED, :] = tree([ref[0:MOVED, :] for ref in parts])
        if block > 1:
            y_before = before_ref[y_rows, 0:MOVED]
            big_ref[MOVED:, :] = dot(y_before, big_ref[0:MOVED, :])
            big_ref[0:MOVED, :] = big_ref[0:MOVED, :] - fold(big_ref[MOVED:, :])
        y_all = dot_nt(spread(big_ref[0:MOVED, :]), t_before)
        if block > 1:
            y_all = y_all + before_ref[y_rows, 0:MOVED]
        log_ref[y_rows, 0:MOVED] = y_all
        start = y_rows.start + block * K
        rows = jnp.concatenate(
            [
                log_ref[start + w * MOVED : start + w * MOVED + K, 0:MOVED]
                for w in range(n // K)
            ],
            axis=0,
        )
        log_ref[log_rows(block, n, "t"), :] = unit(block, n) - jnp.transpose(rows)
        t = log_ref[log_rows(block, n, "t"), :]
        q = tree([ref[MOVED:, :] for ref in parts])
        drifts = drift_of(block, q, t)
    if block == 0:
        log_ref[log_rows(0, n, "t"), :] = t
    speeds = jnp.sum(drifts * drifts, axis=0, keepdims=True)
    capped = drifts / jnp.sqrt(1.0 + TAU * speeds)
    moved = state[0:3, :] + state[3:4, :] * (TAU * capped + ROOT_TAU * state[4:7, :])
    moved_rows = log_rows(block, n, "moved")
    log_ref[moved_rows, :] = jnp.concatenate([moved, jnp.zeros((5, n), F32)], axis=0)
    wx, _ = axis_weights(moved[0:1, :], False)
    wy, _ = axis_weights(moved[1:2, :], False)
    wz, _ = axis_weights(moved[2:3, :], False)
    wx_ref[...] = wx
    fill(wide_ref, edge_ref, [products(wy, wz)])
    sum_ref[...] = jnp.zeros_like(sum_ref)

    def body(pair, carry):
        even, odd = plane_pair(table_ref, pair, wide_ref)
        w0, w1 = wx_ref[pl.ds(2 * pair, 1), :], wx_ref[pl.ds(2 * pair + 1, 1), :]
        middle_weights(mid_ref, edge_ref, pair, [(0, w0, w1)])
        sum_ref[...] += w0 * (even[:, 0:n] + even[:, n:]) + w1 * (odd[:, 0:n] + odd[:, n:])
        return carry

    lax.fori_loop(0, GRID // 2, body, 0, unroll=UNROLL)
    rest = middle(table_ref, mid_ref)
    change = sum_ref[...] + (rest[:, 0:n] + rest[:, n:]) - phi_ref[...]
    change_rows = log_rows(block, n, "change")
    log_ref[change_rows, 0:orbitals] = jnp.transpose(change)
    if not last:
        s_ref[0:MOVED, :] = fold(dot(vm_ref[...], change))
        return
    walkers = whole_ref.shape[0]
    for i in range(walkers // 2):
        for w, out_ref in zip(both_halves(meta_ref, walkers, i), (mine_ref, give_ref)):
            at = pl.ds(pl.multiple_of(change_rows.start + w * K, 8), K)
            out_ref[i] = dot(log_ref[at, 0:orbitals], whole_ref[w])


def step_call(block, parts, before, more, states, vm, table):
    orbitals, n = table.shape[0], states.shape[2]
    rows = vm.shape[0]
    operands = [*parts, before, *more, states, vm, table]
    specs = [VMEM] * len(operands)
    log = (log_y(n).stop + orbitals, 128)
    if block == NMOVE - 1:
        specs[len(parts) + 1] = SMEM
        walkers, _, electrons = more[1].shape
        shapes = [(walkers // 2, K, electrons)] * 2 + [log]
    else:
        shapes = [(MOVED + more[0].shape[0] - orbitals, n), log]
    return pl.pallas_call(
        functools.partial(step_kernel, block, len(parts)),
        name="step",
        out_shape=tuple(jax.ShapeDtypeStruct(shape, F32) for shape in shapes),
        in_specs=specs,
        out_specs=(VMEM,) * len(shapes),
        scratch_shapes=[
            pltpu.VMEM((orbitals, n), F32),
            pltpu.VMEM((MOVED + rows, n), F32),
            *weights_scratch(n, 1, 1),
        ],
        compiler_params=params(),
        cost_estimate=lasting(3),
    )(*operands)


def last_kernel(counts, *refs):
    refs = list(refs)
    sums = [[refs.pop(0) for _ in range(count)] for count in counts]
    log_ref, vm_ref, out_ref, l_ref = refs
    n = log_ref.shape[1]
    ts = [log_ref[log_rows(block, n, "t"), :] for block in range(NMOVE)]
    for block in range(NMOVE - 1):
        r = unit(block, ts[block].shape[1])
        if block:
            sums_of = tree([ref[0:MOVED, :] for ref in sums[block - 1]])
            r = r - fold(dot(l_ref[...], sums_of))
        more = dot_nt(spread(r), ts[block])
        l_ref[...] = l_ref[...] + more if block else more
    t = jnp.transpose(ts[-1])
    for w in range(out_ref.shape[0]):
        at = slice(w * MOVED, (w + 1) * MOVED)
        early = l_ref[w * MOVED : (w + 1) * MOVED - K, :]
        factor = jnp.concatenate([early, t[w * K : (w + 1) * K, :]], axis=0)
        out_ref[w] = jnp.transpose(dot(factor, vm_ref[at, :]))


def last_call(s_parts, log, vm):
    rows, orbitals = vm.shape
    operands = [part for parts in s_parts for part in parts] + [log, vm]
    return pl.pallas_call(
        functools.partial(last_kernel, [len(parts) for parts in s_parts]),
        name="last",
        out_shape=(
            jax.ShapeDtypeStruct((rows // MOVED, orbitals, MOVED), F32),
            jax.ShapeDtypeStruct((rows, MOVED), F32),
        ),
        in_specs=[VMEM] * len(operands),
        out_specs=(VMEM, VMEM),
        compiler_params=params(),
        cost_estimate=lasting(2),
    )(*operands)


def both_halves(meta_ref, walkers, i):
    parity = meta_ref[meta_ref.shape[0] - 1]
    half = walkers // 2
    return i + half * parity, i + half * (1 - parity)


def assemble_kernel(meta_ref, own_ref, got_ref, code_ref, *refs):
    log_ref, v_ref, mine_ref, give_ref, held_ref, sem = refs
    n = log_ref.shape[1]
    walkers, orbitals, electrons = own_ref.shape
    load = pltpu.make_async_copy(code_ref, held_ref, sem)
    load.start()
    load.wait()

    def body(i, carry):
        for w, out_ref in zip(both_halves(meta_ref, walkers, i), (mine_ref, give_ref)):
            here, place, group = parent_of(meta_ref, walkers, w)
            scale = jnp.concatenate(
                [
                    got_ref[group, MOVED + j : MOVED + j + 1, :]
                    for j in range(electrons // orbitals)
                ],
                axis=1,
            )
            level = held_ref[group].astype(jnp.int32).astype(F32) * (1.0 / LEVELS)
            v = jnp.where(here, own_ref[place], level * jnp.abs(level) * scale)
            v_ref[w] = v
            change = []
            for b in range(NMOVE - 1):
                at = log_rows(b, n, "change").start + w * K
                change.append(log_ref[pl.ds(pl.multiple_of(at, 8), K), 0:orbitals])
            change = jnp.concatenate(change, axis=0)
            out_ref[i] = dot(change, v)
        return carry

    lax.fori_loop(0, walkers // 2, body, 0)


def assemble_call(meta, inverse, got, code, log):
    walkers, orbitals, electrons = inverse.shape
    half = (walkers // 2, (NMOVE - 1) * K, electrons)
    return pl.pallas_call(
        assemble_kernel,
        name="assemble",
        out_shape=(
            jax.ShapeDtypeStruct(inverse.shape, F32),
            jax.ShapeDtypeStruct(half, F32),
            jax.ShapeDtypeStruct(half, F32),
        ),
        in_specs=[SMEM, VMEM, VMEM, ANY, VMEM],
        out_specs=(VMEM,) * 3,
        scratch_shapes=[
            pltpu.VMEM(code.shape, code.dtype),
            pltpu.SemaphoreType.DMA(()),
        ],
        compiler_params=params(),
        cost_estimate=lasting(4),
    )(meta, inverse, got, code, log)


def join_kernel(mine_ref, got_ref, sum_ref, code_ref, power_ref):
    for i in range(mine_ref.shape[0]):
        x = mine_ref[i] + got_ref[i]
        sum_ref[i] = x
        size = jnp.abs(x)
        top = jnp.max(size, axis=0, keepdims=True)
        power = jnp.ceil(jnp.log(jnp.where(top > 0.0, top, 1.0)) * LOG2_E)
        power = jnp.where(top > 0.0, jnp.maximum(power, -126.0), 0.0)
        level = jnp.floor(jnp.sqrt(size) * (LEVELS * jnp.exp2(-0.5 * power)) + 0.5)
        level = jnp.minimum(level, LEVELS)
        code_ref[i] = jnp.where(x < 0.0, -level, level).astype(jnp.int32).astype(jnp.int16)
        power_ref[i : i + 1, :] = power


def join_call(mine, got):
    half, _, electrons = mine.shape
    return pl.pallas_call(
        join_kernel,
        name="join",
        out_shape=(
            jax.ShapeDtypeStruct(mine.shape, F32),
            jax.ShapeDtypeStruct(mine.shape, jnp.int16),
            jax.ShapeDtypeStruct((half, electrons), F32),
        ),
        in_specs=[VMEM, VMEM],
        out_specs=(VMEM,) * 3,
        compiler_params=params(),
        cost_estimate=lasting(1),
    )(mine, got)


def decode(code, power):
    root = jnp.exp2(0.5 * power[:, None, :]) * (1.0 / LEVELS)
    level = code.astype(F32)
    return (level * root) * (jnp.abs(level) * root)


def update_kernel(meta_ref, v_ref, factor_ref, l_ref, *refs):
    sums_refs, (out_ref, new_ref, sem) = refs[:4], refs[4:]
    walkers = v_ref.shape[0]

    def store(w):
        return pltpu.make_async_copy(new_ref.at[w], out_ref.at[w], sem.at[w])

    order = [meta_ref[walkers + b] for b in range(NMOVE)]
    half = walkers // 2
    own = [both_halves(meta_ref, walkers, i) for i in range(half)]
    places = [(own[i][h], i, sums_refs[2 * h : 2 * h + 2]) for i in range(half) for h in range(2)]
    lates = []
    for w, i, (early_ref, late_ref) in places:
        moved = moved_lanes(late_ref[i], order)[:, 0:MOVED]
        rows = l_ref[pl.ds(pl.multiple_of(w * MOVED, MOVED), MOVED), :]
        lates.append(dot_nt(moved, rows)[:, 0 : MOVED - K])
    for n, (w, i, (early_ref, late_ref)) in enumerate(places):
        lates[n] = late_ref[i] - dot(lates[n], early_ref[i])
    for late, (w, i, (early_ref, _)) in zip(lates, places):
        sums = jnp.concatenate([early_ref[i], late], axis=0)
        new_ref[w] = v_ref[w] - dot(factor_ref[w], sums)
        store(w).start()
    for w in range(walkers):
        store(w).wait()


def update_call(meta, inverse, factor, rows, sums):
    return pl.pallas_call(
        update_kernel,
        name="update",
        out_shape=jax.ShapeDtypeStruct(inverse.shape, F32),
        in_specs=[SMEM] + [VMEM] * 7,
        out_specs=ANY,
        scratch_shapes=[
            pltpu.VMEM(inverse.shape, F32),
            pltpu.SemaphoreType.DMA((inverse.shape[0],)),
        ],
        compiler_params=params(),
        cost_estimate=lasting(2),
    )(meta, inverse, factor, rows, *sums)


def place_kernel(meta_ref, own_ref, got_ref, log_ref, out_ref):
    _, walkers, electrons = own_ref.shape
    parts = electrons // got_ref.shape[2]
    lane = lax.broadcasted_iota(jnp.int32, (1, electrons), 1)
    for w in range(walkers):
        here, place, group = parent_of(meta_ref, walkers, w)
        fresh = []
        for b in range(NMOVE):
            block = meta_ref[walkers + b]
            moved = log_ref[log_rows(b, log_ref.shape[1], "moved"), :]
            fresh.append((block, roll(moved, (block - w) * K)))
        for d in range(3):
            at = MOVED + (d + 1) * parts
            far = jnp.concatenate(
                [got_ref[group, at + i : at + i + 1, :] for i in range(parts)], axis=1
            )
            line = jnp.where(here, own_ref[d, pl.ds(place, 1), :], far)
            for block, moved in fresh:
                moved = jnp.concatenate([moved[d : d + 1, :]] * (electrons // 128), axis=1)
                line = jnp.where(lane // K == block, moved, line)
            out_ref[d, w : w + 1, :] = line


def place_call(meta, positions, got, log):
    return pl.pallas_call(
        place_kernel,
        name="place",
        out_shape=jax.ShapeDtypeStruct(positions.shape, F32),
        in_specs=[SMEM] + [VMEM] * 3,
        out_specs=VMEM,
        compiler_params=params(),
        cost_estimate=lasting(1),
    )(meta, positions, got, log)


def swap(x, axis, k):
    return lax.ppermute(x, axis, [(i, i ^ k) for i in range(lax.axis_size(axis))])


def exchange(part, axis):
    return [part] + [swap(part, axis, k) for k in range(1, lax.axis_size(axis))]


def add_up(early, late, axis, done):
    parts = [early, late]
    k = 2
    size = lax.axis_size(axis)
    while k < size:
        got = [[swap(x, axis, k) for x in part[1:]] for part in parts]
        got, done = together(got, done)
        added = [decode(*x) for x in got]
        if 2 * k < size:
            parts = [join_call(part[0], x) for part, x in zip(parts, added)]
        else:
            parts = [[part[0] + x] for part, x in zip(parts, added)]
        k *= 2
    return [(x, swap(x, axis, 1)) for (x,) in parts], done


def together(*values):
    return lax.optimization_barrier(values)


def alltoall(x):
    return lax.all_to_all(x, "walker", split_axis=0, concat_axis=0, tiled=True)


def local(positions, inverse, spline_table, gaussian, accepted, block_order, parent):
    groups = lax.axis_size("walker")
    me = lax.axis_index("walker").astype(jnp.int32)
    parity = lax.rem(lax.axis_index("orb"), 2).astype(jnp.int32)
    meta = jnp.concatenate([parent, block_order[:NMOVE], me[None], parity[None]])
    positions = jnp.transpose(positions, (1, 0, 2))
    gaussian = jnp.transpose(gaussian, (1, 0, 2))

    info = alltoall(pack_call(parent, block_order, positions, gaussian, accepted, groups))
    own, code = columns_call(block_order, inverse, positions)
    states, outgoing, sending = route_call(meta, info, own)
    got = alltoall(outgoing)
    phi, grad, code = slopes_call(sending, states, spline_table, code)
    got, code, phi, grad = together(got, code, phi, grad)
    code = alltoall(code)
    vm, first = select_call(meta, own, got, grad)
    p0 = exchange(first, "orb")

    def step(b, parts, before, more):
        return step_call(b, parts, before, more, states, vm, spline_table)

    later = later_call(1, states, spline_table, vm)
    p1, log = step(0, p0, phi, [later])
    p1 = exchange(p1, "orb")
    later = later_call(2, states, spline_table, vm)
    p2, log = step(1, p1, log, [later])
    p2 = exchange(p2, "orb")
    held, code = together(states, code)
    later = later_call(3, held, spline_table, vm)
    p3, log = step(2, p2, log, [later])
    p3 = exchange(p3, "orb")
    whole, mine, give = assemble_call(meta, inverse, got, code, log)
    p3, mine, give = together(p3, mine, give)
    early = join_call(mine, swap(give, "orb", 1))
    mine, give, log = step(3, p3, log, [meta, whole])
    late = join_call(mine, swap(give, "orb", 1))
    factor, rows = last_call([p2, p3], log, vm)
    new_positions = place_call(meta, positions, got, log)
    factor, new_positions = together(factor, new_positions)
    (early, late), factor = add_up(early, late, "orb", factor)
    new_inverse = update_call(meta, whole, factor, rows, [early[0], late[0], early[1], late[1]])
    return jnp.transpose(new_positions, (1, 0, 2)), new_inverse


def solution(mesh):
    return jax.shard_map(
        local,
        mesh=mesh,
        in_specs=(
            P("walker", None, None),
            P("walker", "orb", None),
            P("orb", None),
            P("walker", None, None),
            P("walker", None),
            P(),
            P("walker"),
        ),
        out_specs=(P("walker", None, None), P("walker", "orb", None)),
        check_vma=False,
    )
```

```python
import functools

import jax
import jax.numpy as jnp
from jax import lax
from jax.experimental import pallas as pl
from jax.experimental.pallas import tpu as pltpu
from jax.sharding import PartitionSpec as P

GRID = 24
PLANE = GRID * GRID
MAIN = 512
EDGE = PLANE - MAIN
UNROLL = 12
CHUNKS = (4, 4, 4)
K = 16
NMOVE = 4
MOVED = K * NMOVE
CAP = 1
TAU = 0.25
ROOT_TAU = 0.5
F32 = jnp.float32
BF16 = jnp.bfloat16
LEVELS = 32767.0
LOG2_E = 1.4426950408889634
HIGHEST = lax.Precision.HIGHEST
VMEM = pl.BlockSpec(memory_space=pltpu.VMEM)
SMEM = pl.BlockSpec(memory_space=pltpu.SMEM)
ANY = pl.BlockSpec(memory_space=pl.ANY)
LIMIT = 16 * 2**20
WHOLE = 60 * 2**20
PART = 59500000
ALMOST = 63300000


def axis_weights(u, with_slopes):
    floors = jnp.floor(u)
    t = u - floors
    remain = 1.0 - t
    square = t * t
    cubed = square * t
    values = (
        remain * remain * remain / 6.0,
        (3.0 * cubed - 6.0 * square + 4.0) / 6.0,
        (-3.0 * cubed + 3.0 * square + 3.0 * t + 1.0) / 6.0,
        cubed / 6.0,
    )
    lanes = u.shape[1]
    line = lax.broadcasted_iota(jnp.int32, (GRID, lanes), 0)
    step = line - (floors.astype(jnp.int32) - 1)
    step = jnp.where(step < 0, step + GRID, step)
    step = jnp.where(step < 0, step + GRID, step)
    step = jnp.where(step >= GRID, step - GRID, step)

    def spread(weights):
        out = jnp.zeros((GRID, lanes), F32)
        for a in range(4):
            out = jnp.where(step == a, jnp.broadcast_to(weights[a], (GRID, lanes)), out)
        return out

    if not with_slopes:
        return spread(values), None
    slopes = (
        -0.5 * remain * remain,
        1.5 * square - 2.0 * t,
        -1.5 * square + t + 0.5,
        0.5 * square,
    )
    return spread(values), spread(slopes)


def products(first, second):
    return jnp.concatenate([first[y : y + 1, :] * second for y in range(GRID)], axis=0)


def fill(whole_ref, edge_ref, weights):
    n = edge_ref.shape[1]
    for i, weight in enumerate(weights):
        for j, piece in enumerate(split(weight)):
            whole_ref[:, (2 * i + j) * n : (2 * i + j + 1) * n] = piece
        edge_ref[2 * EDGE * i : 2 * EDGE * i + EDGE, :] = weight[MAIN:PLANE, :]
        edge_ref[2 * EDGE * i + EDGE : 2 * EDGE * (i + 1), :] = weight[0:EDGE, :]


def plane_pair(table_ref, pair, whole_ref):
    start = pl.multiple_of(pair * 2 * PLANE, 128)
    even = table_ref[:, pl.ds(start, MAIN)]
    start = pl.multiple_of(pair * 2 * PLANE + MAIN + 128, 128)
    odd = table_ref[:, pl.ds(start, MAIN)]
    return (
        jnp.dot(even, whole_ref[0:MAIN, :], preferred_element_type=F32),
        jnp.dot(odd, whole_ref[EDGE:PLANE, :], preferred_element_type=F32),
    )


def middle_weights(mid_ref, edge_ref, pair, terms):
    n = edge_ref.shape[1]
    at = pl.ds(pl.multiple_of(pair * 128, 128), 128)
    for i, (kind, w0, w1) in enumerate(terms):
        start = 2 * EDGE * kind
        part = jnp.concatenate(
            [
                w0 * edge_ref[start : start + EDGE, :],
                w1 * edge_ref[start + EDGE : start + 2 * EDGE, :],
            ],
            axis=0,
        )
        for j, piece in enumerate(split(part)):
            mid_ref[at, (2 * i + j) * n : (2 * i + j + 1) * n] = piece


def middle(table_ref, mid_ref):
    lanes = [
        table_ref[:, q * 2 * PLANE + MAIN : q * 2 * PLANE + MAIN + 128] for q in range(GRID // 2)
    ]
    lanes = jnp.concatenate(lanes, axis=1)
    return jnp.dot(lanes, mid_ref[...], preferred_element_type=F32)


def slopes_kernel(
    state_ref, table_ref, phi_ref, grad_ref, whole_ref, mid_ref, edge_ref, wx_ref, sx_ref,
    loads=(), beside=()
):
    n = state_ref.shape[2]
    wx, sx = axis_weights(state_ref[0, 0:1, :], True)
    wy, sy = axis_weights(state_ref[0, 1:2, :], True)
    wz, sz = axis_weights(state_ref[0, 2:3, :], True)
    wx_ref[...] = wx
    sx_ref[...] = sx
    fill(whole_ref, edge_ref, [products(wy, wz), products(sy, wz), products(wy, sz)])
    phi_ref[...] = jnp.zeros_like(phi_ref)
    grad_ref[...] = jnp.zeros_like(grad_ref)

    def body(pair, carry):
        even, odd = plane_pair(table_ref, pair, whole_ref)
        w0, w1 = wx_ref[pl.ds(2 * pair, 1), :], wx_ref[pl.ds(2 * pair + 1, 1), :]
        s0, s1 = sx_ref[pl.ds(2 * pair, 1), :], sx_ref[pl.ds(2 * pair + 1, 1), :]
        terms = [(0, w0, w1), (0, s0, s1), (1, w0, w1), (2, w0, w1)]
        middle_weights(mid_ref, edge_ref, pair, terms)

        def both(i):
            at, to = slice(2 * i * n, (2 * i + 1) * n), slice((2 * i + 1) * n, (2 * i + 2) * n)
            return even[:, at] + even[:, to], odd[:, at] + odd[:, to]

        e, o = both(0)
        phi_ref[...] += w0 * e + w1 * o
        grad_ref[:, 0:n] += s0 * e + s1 * o
        for d in (1, 2):
            e, o = both(d)
            grad_ref[:, d * n : (d + 1) * n] += w0 * e + w1 * o
        return carry

    pairs = GRID // 2
    if loads:
        start = 0
        for i, (load, size) in enumerate(zip(loads, CHUNKS)):
            load.wait()
            if i + 1 < len(loads):
                loads[i + 1].start()
            if beside[i] is not None:
                beside[i]()
            lax.fori_loop(start, start + size, body, 0, unroll=size)
            start += size
    else:
        lax.fori_loop(0, pairs, body, 0, unroll=UNROLL)
    rest = middle(table_ref, mid_ref)
    phi_ref[...] += rest[:, 0:n] + rest[:, n : 2 * n]
    for d in range(3):
        at = 2 * (d + 1) * n
        grad_ref[:, d * n : (d + 1) * n] += rest[:, at : at + n] + rest[:, at + n : at + 2 * n]


def first_kernel(
    sending_ref, states_ref, table_ref, code_in, phi_out, grad_out, code_out, *refs
):
    held_ref, phi_ref, grad_ref, code_ref = refs[:4]
    scratch, (in_sem, out_sem, code_sem) = refs[4:-3], refs[-3:]
    groups = code_out.shape[0]
    loads = []
    start = 0
    for i, pairs in enumerate(CHUNKS):
        at = pl.ds(start, 2 * PLANE * pairs)
        start += 2 * PLANE * pairs
        loads.append(
            pltpu.make_async_copy(table_ref.at[:, at], held_ref.at[:, at], in_sem.at[i])
        )
    loads[0].start()
    codes = pltpu.make_async_copy(code_in, code_ref, code_sem.at[groups])
    picks = []
    for g in range(groups):
        source = code_ref.at[sending_ref[g]]
        picks.append(pltpu.make_async_copy(source, code_out.at[g], code_sem.at[g]))

    def pick():
        codes.wait()
        for copy in picks:
            copy.start()

    beside = (None, codes.start, pick)
    slopes_kernel(
        states_ref.at[0:1], held_ref, phi_ref, grad_ref, *scratch, loads=loads, beside=beside
    )
    stores = [
        pltpu.make_async_copy(phi_ref, phi_out, out_sem.at[0]),
        pltpu.make_async_copy(grad_ref, grad_out, out_sem.at[1]),
    ]
    for store in stores:
        store.start()
    for store in stores + picks:
        store.wait()


def slopes_call(sending, states, table, code):
    orbitals = table.shape[0]
    n = states.shape[2]
    groups = sending.shape[0]
    shapes = [(orbitals, n), (orbitals, 3 * n)]
    return pl.pallas_call(
        first_kernel,
        name="slopes",
        out_shape=tuple(jax.ShapeDtypeStruct(shape, F32) for shape in shapes)
        + (jax.ShapeDtypeStruct((groups, *code.shape[1:]), code.dtype),),
        in_specs=[SMEM, VMEM, ANY, ANY],
        out_specs=(ANY, ANY, ANY),
        scratch_shapes=[pltpu.VMEM(table.shape, BF16)]
        + [pltpu.VMEM(shape, F32) for shape in shapes]
        + [pltpu.VMEM(code.shape, code.dtype)]
        + slopes_scratch(n)
        + [
            pltpu.SemaphoreType.DMA((len(CHUNKS),)),
            pltpu.SemaphoreType.DMA((2,)),
            pltpu.SemaphoreType.DMA((groups + 1,)),
        ],
        compiler_params=params(WHOLE),
        cost_estimate=lasting(5),
    )(sending, states, table, code)


def slopes_scratch(n):
    return weights_scratch(n, 3, 4) + [pltpu.VMEM((GRID, n), F32)]


def weights_scratch(n, kinds, terms):
    return [
        pltpu.VMEM((PLANE, 2 * kinds * n), BF16),
        pltpu.VMEM((GRID // 2 * 128, 2 * terms * n), BF16),
        pltpu.VMEM((2 * EDGE * kinds, n), F32),
        pltpu.VMEM((GRID, n), F32),
    ]


def later_kernel(block, states_ref, table_ref, vm_ref, out_ref, grad_ref, *scratch):
    orbitals = table_ref.shape[0]
    phi_ref = out_ref.at[0:orbitals]
    slopes_kernel(states_ref.at[block : block + 1], table_ref, phi_ref, grad_ref, *scratch)
    drift_rows(block, vm_ref, grad_ref, out_ref, orbitals)


def later_call(block, states, table, vm):
    orbitals = table.shape[0]
    n = states.shape[2]
    return pl.pallas_call(
        functools.partial(later_kernel, block),
        name="later",
        out_shape=jax.ShapeDtypeStruct((orbitals + drift_size(block), n), F32),
        in_specs=[VMEM] * 3,
        out_specs=VMEM,
        scratch_shapes=[pltpu.VMEM((orbitals, 3 * n), F32)] + slopes_scratch(n),
        compiler_params=params(),
        cost_estimate=lasting(5),
    )(states, table, vm)


def split(x):
    high = x.astype(BF16)
    return high, (x - high.astype(F32)).astype(BF16)


def product(a, b, dims):
    (a0, a1), (b0, b1) = split(a), split(b)

    def one(x, y):
        return lax.dot_general(x, y, (dims, ((), ())), preferred_element_type=F32)

    return one(a0, b0) + (one(a0, b1) + one(a1, b0))


def dot(a, b):
    return product(a, b, ((1,), (0,)))


def dot_nt(a, b):
    return product(a, b, ((1,), (1,)))


def own_lanes(rows, n, walker):
    lane = lax.broadcasted_iota(jnp.int32, (rows, n), 1)
    return jnp.logical_and(lane >= walker * K, lane < (walker + 1) * K)


def fold(big):
    n = big.shape[1]
    rows = big.shape[0] // (n // K)
    total = jnp.zeros((rows, n), F32)
    for w in range(n // K):
        total = jnp.where(own_lanes(rows, n, w), big[w * rows : (w + 1) * rows, :], total)
    return total


def unit(block, n):
    row = lax.broadcasted_iota(jnp.int32, (MOVED, n), 0)
    lane = lax.broadcasted_iota(jnp.int32, (MOVED, n), 1)
    return jnp.where(row - block * K == lane % K, 1.0, 0.0).astype(F32)


def tree(parts):
    while len(parts) > 1:
        parts = [parts[i] + parts[i + 1] for i in range(0, len(parts), 2)]
    return parts[0]


def total(refs):
    return tree([ref[...] for ref in refs])


def params(limit=LIMIT):
    return pltpu.CompilerParams(vmem_limit_bytes=limit)


def lasting(us):
    return pl.CostEstimate(flops=int(us * 1e9), bytes_accessed=0, transcendentals=0)


def parent_of(meta_ref, walkers, w):
    parent = meta_ref[w]
    group = parent // walkers
    here = group == meta_ref[walkers + NMOVE]
    return here, jnp.where(here, parent % walkers, 0), jnp.where(here, 0, group)


def block_lanes(x, block):
    lane = lax.broadcasted_iota(jnp.int32, x.shape, 1)
    kept = jnp.where(lane // K == block, x, 0.0)
    return tree([kept[:, i : i + 128] for i in range(0, x.shape[1], 128)])


def roll(x, shift):
    if isinstance(shift, int):
        shift = shift % 128
        return x if shift == 0 else pltpu.roll(x, shift, 1)
    return pltpu.roll(x, lax.rem(shift + 1024, 128), 1)


def moved_lanes(x, order_ref):
    line = jnp.zeros((x.shape[0], 128), F32)
    for b in range(NMOVE):
        block = order_ref[b]
        line = line + roll(block_lanes(x, block), (b - block) * K)
    return line


def pack_kernel(parent_ref, order_ref, *refs):
    (out_ref, pos_ref, gauss_ref, acc_ref), sem = refs[3:-1], refs[-1]
    copies = [
        pltpu.make_async_copy(refs[i], refs[i + 4], sem.at[i]) for i in range(3)
    ]
    for copy in copies:
        copy.start()
    for copy in copies:
        copy.wait()
    walkers = pos_ref.shape[1]
    half = jnp.zeros((walkers, 128 - MOVED), F32)
    lane = lax.broadcasted_iota(jnp.int32, (walkers, 128), 1)
    row = lax.broadcasted_iota(jnp.int32, (walkers, 128), 0)
    lines = []
    for d in range(3):
        line = moved_lanes(pos_ref[d], order_ref)
        lines.append(line + jnp.concatenate([half, gauss_ref[d]], axis=1))
    parents = jnp.zeros((walkers, 128), jnp.int32)
    for w in range(walkers):
        parents = jnp.where(row == w, parent_ref[w], parents)
    decided = jnp.concatenate([acc_ref[...].astype(F32), half], axis=1)
    lines.append(jnp.where(lane < MOVED, decided, parents.astype(F32)))
    for g in range(out_ref.shape[0]):
        for d in range(4):
            out_ref[g, d * walkers : (d + 1) * walkers, :] = lines[d]


def pack_call(parent, order, positions, gaussian, accepted, groups):
    walkers = positions.shape[1]
    held = [positions, gaussian, accepted]
    return pl.pallas_call(
        pack_kernel,
        name="pack",
        out_shape=jax.ShapeDtypeStruct((groups, 4 * walkers, 128), F32),
        in_specs=[SMEM, SMEM, ANY, ANY, ANY],
        out_specs=VMEM,
        scratch_shapes=[pltpu.VMEM(x.shape, x.dtype) for x in held]
        + [pltpu.SemaphoreType.DMA((3,))],
        compiler_params=params(WHOLE),
        cost_estimate=lasting(1),
    )(parent, order, *held)


def columns_kernel(order_ref, v_in, pos_in, own_out, code_out, v_ref, pos_ref, own_ref, code_ref, sem):
    walkers, orbitals, electrons = v_ref.shape

    def load(w):
        return pltpu.make_async_copy(v_in.at[w], v_ref.at[w], sem.at[0, w])

    def store(w):
        return (
            pltpu.make_async_copy(own_ref.at[w], own_out.at[w], sem.at[1, w]),
            pltpu.make_async_copy(code_ref.at[w], code_out.at[w], sem.at[2, w]),
        )

    first = pltpu.make_async_copy(pos_in, pos_ref, sem.at[0, walkers])
    first.start()
    for w in range(walkers):
        load(w).start()
    first.wait()

    def body(w, carry):
        load(w).wait()
        v = v_ref[w]
        own_ref[w, 0:MOVED, :] = jnp.transpose(moved_lanes(v, order_ref))[0:MOVED, :]
        size = jnp.abs(v)
        scale = jnp.max(size, axis=0, keepdims=True)
        at = MOVED
        for line in [scale] + [pos_ref[d, pl.ds(w, 1), :] for d in range(3)]:
            for i in range(0, electrons, orbitals):
                own_ref[w, at : at + 1, :] = line[:, i : i + orbitals]
                at += 1
        some = scale > 0.0
        step = jnp.where(some, LEVELS / jnp.sqrt(jnp.where(some, scale, 1.0)), 0.0)
        level = jnp.minimum(jnp.floor(jnp.sqrt(size) * step + 0.5), LEVELS)
        code_ref[w] = jnp.where(v < 0.0, -level, level).astype(jnp.int32).astype(jnp.int16)
        for copy in store(w):
            copy.start()
        return carry

    lax.fori_loop(0, walkers, body, 0)
    for w in range(walkers):
        for copy in store(w):
            copy.wait()


def payload_rows(orbitals, electrons):
    return MOVED + 4 * electrons // orbitals


def columns_call(order, inverse, positions):
    walkers, orbitals, electrons = inverse.shape
    own = (walkers, payload_rows(orbitals, electrons), orbitals)
    return pl.pallas_call(
        columns_kernel,
        name="columns",
        out_shape=(
            jax.ShapeDtypeStruct(own, F32),
            jax.ShapeDtypeStruct(inverse.shape, jnp.int16),
        ),
        in_specs=[SMEM, ANY, ANY],
        out_specs=(ANY, ANY),
        scratch_shapes=[
            pltpu.VMEM(inverse.shape, F32),
            pltpu.VMEM(positions.shape, F32),
            pltpu.VMEM(own, F32),
            pltpu.VMEM(inverse.shape, jnp.int16),
            pltpu.SemaphoreType.DMA((3, walkers + 1)),
        ],
        compiler_params=params(WHOLE),
        cost_estimate=lasting(3),
    )(order, inverse, positions)


def route_kernel(meta_ref, info_in, own_in, states_ref, out_ref, sending_ref, *refs):
    info_ref, own_ref, parents_ref, sem, out_sem = refs
    walkers = own_ref.shape[0]
    groups = out_ref.shape[0]
    rows = 3 * walkers
    asked = []
    for g in range(groups):
        at = pl.ds(rows, walkers)
        asked.append(pltpu.make_async_copy(info_in.at[g, at], parents_ref.at[g], sem.at[2]))
    for each in asked:
        each.start()
    loads = [
        pltpu.make_async_copy(info_in, info_ref, sem.at[0]),
        pltpu.make_async_copy(own_in, own_ref, sem.at[1]),
    ]
    for load in loads:
        load.start()
    for each in asked:
        each.wait()
    me = meta_ref[walkers + NMOVE]
    sending = []
    for g in range(groups):
        wanted = jnp.int32(0)
        for s in range(walkers):
            within = parents_ref[g, s, MOVED].astype(jnp.int32) - me * walkers
            mine = jnp.logical_and(within >= 0, within < walkers)
            wanted = jnp.where(mine, within, wanted)
        sending.append(jnp.where(me == g, 0, wanted))
        sending_ref[g] = sending[g]
    for load in loads[1:]:
        load.wait()
    stores = []
    for g in range(groups):
        source = sending[g]
        stores.append(pltpu.make_async_copy(own_ref.at[source], out_ref.at[g], out_sem.at[g]))
    for store in stores:
        store.start()
    loads[0].wait()
    lane = lax.broadcasted_iota(jnp.int32, (8, 128), 1)
    tiles = []
    for w in range(walkers):
        group, place = meta_ref[w] // walkers, meta_ref[w] % walkers
        line = [info_ref[group, pl.ds(d * walkers + place, 1), :] for d in range(4)]
        line = jnp.concatenate(line, axis=0)
        tiles.append(jnp.concatenate([line, roll(line, 128 - MOVED)], axis=0))
    for b in range(NMOVE):
        state = jnp.zeros((8, 128), F32)
        for w in range(walkers):
            state = jnp.where(lane // K == w, roll(tiles[w], (w - b) * K), state)
        states_ref[b] = state
    for store in stores:
        store.wait()


def route_call(meta, info, own):
    groups = info.shape[0]
    return pl.pallas_call(
        route_kernel,
        name="route",
        out_shape=(
            jax.ShapeDtypeStruct((NMOVE, 8, 128), F32),
            jax.ShapeDtypeStruct((groups, *own.shape[1:]), F32),
            jax.ShapeDtypeStruct((groups,), jnp.int32),
        ),
        in_specs=[SMEM, ANY, ANY],
        out_specs=(VMEM, ANY, SMEM),
        scratch_shapes=[
            pltpu.VMEM(info.shape, F32),
            pltpu.VMEM(own.shape, F32),
            pltpu.SMEM((groups, own.shape[0], 128), F32),
            pltpu.SemaphoreType.DMA((3,)),
            pltpu.SemaphoreType.DMA((groups,)),
        ],
        compiler_params=params(ALMOST),
        cost_estimate=lasting(3),
    )(meta, info, own)


def select_kernel(meta_ref, own_ref, got_ref, grad_in, vm_ref, out_ref, grad_ref, sem):
    walkers = own_ref.shape[0]
    load = pltpu.make_async_copy(grad_in, grad_ref, sem.at[walkers])
    load.start()

    def copy(w, source):
        to = vm_ref.at[w * MOVED : (w + 1) * MOVED]
        return pltpu.make_async_copy(source.at[0:MOVED], to, sem.at[w])

    for w in range(walkers):
        here, place, group = parent_of(meta_ref, walkers, w)

        @pl.when(here)
        def _():
            copy(w, own_ref.at[place]).start()

        @pl.when(jnp.logical_not(here))
        def _():
            copy(w, got_ref.at[group]).start()

    for w in range(walkers):
        copy(w, own_ref.at[0]).wait()
    load.wait()
    drift_rows(0, vm_ref, grad_ref, out_ref, 0)


def drift_size(block):
    return 8 + 3 * K * block


def drift_rows(block, vm_ref, grad_ref, out_ref, at):
    n = grad_ref.shape[1] // 3
    size = K * block
    used = size + K
    rows = [vm_ref[w * MOVED : w * MOVED + used, :] for w in range(n // K)]
    big = dot(jnp.concatenate(rows, axis=0), grad_ref[...])
    out_ref[at + 3 : at + 8, :] = jnp.zeros((5, n), F32)
    for d in range(3):
        q = fold(big[:, d * n : (d + 1) * n])
        own = q[size:used, :] * unit(0, n)[0:K, :]
        out_ref[at + d : at + d + 1, :] = jnp.sum(own, axis=0, keepdims=True)
        if block:
            out_ref[at + 8 + d * size : at + 8 + (d + 1) * size, :] = q[0:size, :]


def drift_of(block, q, t):
    size = K * block
    lines = [q[0:3, :]]
    if block:
        lines[0] += jnp.concatenate(
            [
                jnp.sum(q[8 + d * size : 8 + (d + 1) * size, :] * t[0:size, :], axis=0)[None]
                for d in range(3)
            ],
            axis=0,
        )
    return lines[0]


def select_call(meta, own, got, grad):
    walkers, _, orbitals = own.shape
    n = grad.shape[1] // 3
    return pl.pallas_call(
        select_kernel,
        name="select",
        out_shape=(
            jax.ShapeDtypeStruct((walkers * MOVED, orbitals), F32),
            jax.ShapeDtypeStruct((drift_size(0), n), F32),
        ),
        in_specs=[SMEM, ANY, ANY, ANY],
        out_specs=(VMEM, VMEM),
        scratch_shapes=[
            pltpu.VMEM(grad.shape, F32),
            pltpu.SemaphoreType.DMA((walkers + 1,)),
        ],
        compiler_params=params(PART),
        cost_estimate=lasting(2),
    )(meta, own, got, grad)


def spread(x):
    n = x.shape[1]
    return jnp.concatenate([jnp.where(own_lanes(x.shape[0], n, w), x, 0.0) for w in range(n // K)], axis=0)


BLOCK_ROWS = 8 + MOVED


def log_rows(block, n, kind):
    start = block * (BLOCK_ROWS + n)
    if kind == "moved":
        return slice(start, start + 8)
    if kind == "t":
        return slice(start + 8, start + BLOCK_ROWS)
    return slice(start + BLOCK_ROWS, start + BLOCK_ROWS + n)


def log_y(n):
    start = NMOVE * (BLOCK_ROWS + n)
    return slice(start, start + n // K * MOVED)


def step_kernel(block, count, *refs):
    refs = list(refs)
    last = block == NMOVE - 1
    parts = [refs.pop(0) for _ in range(count)]
    before_ref = refs.pop(0)
    if last:
        meta_ref, whole_ref = refs.pop(0), refs.pop(0)
    else:
        later_ref = refs.pop(0)
    states_ref, vm_ref, table_ref = [refs.pop(0) for _ in range(3)]
    if last:
        mine_ref, give_ref = refs.pop(0), refs.pop(0)
    else:
        s_ref = refs.pop(0)
    log_ref, sum_ref, big_ref, wide_ref, mid_ref, edge_ref, wx_ref = refs
    orbitals, n = sum_ref.shape
    y_rows = log_y(n)
    phi_rows = slice(y_rows.stop, y_rows.stop + orbitals)
    if not last:
        s_ref[MOVED:, :] = later_ref[orbitals:, :]
        log_ref[phi_rows, :] = later_ref[0:orbitals, :]
    state = states_ref[block]
    if block == 0:
        phi_ref = before_ref
        t = unit(0, n)
        drifts = drift_of(0, total(parts), None)
    else:
        phi_ref = before_ref.at[phi_rows]
        done = slice(0, block * (BLOCK_ROWS + n))
        log_ref[done, :] = before_ref[done, :]
        t_before = before_ref[log_rows(block - 1, n, "t"), :]
        big_ref[0:MOVED, :] = tree([ref[0:MOVED, :] for ref in parts])
        if block > 1:
            y_before = before_ref[y_rows, 0:MOVED]
            big_ref[MOVED:, :] = dot(y_before, big_ref[0:MOVED, :])
            big_ref[0:MOVED, :] = big_ref[0:MOVED, :] - fold(big_ref[MOVED:, :])
        y_all = dot_nt(spread(big_ref[0:MOVED, :]), t_before)
        if block > 1:
            y_all = y_all + before_ref[y_rows, 0:MOVED]
        log_ref[y_rows, 0:MOVED] = y_all
        start = y_rows.start + block * K
        rows = jnp.concatenate(
            [
                log_ref[start + w * MOVED : start + w * MOVED + K, 0:MOVED]
                for w in range(n // K)
            ],
            axis=0,
        )
        log_ref[log_rows(block, n, "t"), :] = unit(block, n) - jnp.transpose(rows)
        t = log_ref[log_rows(block, n, "t"), :]
        q = tree([ref[MOVED:, :] for ref in parts])
        drifts = drift_of(block, q, t)
    if block == 0:
        log_ref[log_rows(0, n, "t"), :] = t
    speeds = jnp.sum(drifts * drifts, axis=0, keepdims=True)
    capped = drifts / jnp.sqrt(1.0 + TAU * speeds)
    moved = state[0:3, :] + state[3:4, :] * (TAU * capped + ROOT_TAU * state[4:7, :])
    moved_rows = log_rows(block, n, "moved")
    log_ref[moved_rows, :] = jnp.concatenate([moved, jnp.zeros((5, n), F32)], axis=0)
    wx, _ = axis_weights(moved[0:1, :], False)
    wy, _ = axis_weights(moved[1:2, :], False)
    wz, _ = axis_weights(moved[2:3, :], False)
    wx_ref[...] = wx
    fill(wide_ref, edge_ref, [products(wy, wz)])
    sum_ref[...] = jnp.zeros_like(sum_ref)

    def body(pair, carry):
        even, odd = plane_pair(table_ref, pair, wide_ref)
        w0, w1 = wx_ref[pl.ds(2 * pair, 1), :], wx_ref[pl.ds(2 * pair + 1, 1), :]
        middle_weights(mid_ref, edge_ref, pair, [(0, w0, w1)])
        sum_ref[...] += w0 * (even[:, 0:n] + even[:, n:]) + w1 * (odd[:, 0:n] + odd[:, n:])
        return carry

    lax.fori_loop(0, GRID // 2, body, 0, unroll=UNROLL)
    rest = middle(table_ref, mid_ref)
    change = sum_ref[...] + (rest[:, 0:n] + rest[:, n:]) - phi_ref[...]
    change_rows = log_rows(block, n, "change")
    log_ref[change_rows, 0:orbitals] = jnp.transpose(change)
    if not last:
        s_ref[0:MOVED, :] = fold(dot(vm_ref[...], change))
        return
    walkers = whole_ref.shape[0]
    for i in range(walkers // 2):
        for w, out_ref in zip(both_halves(meta_ref, walkers, i), (mine_ref, give_ref)):
            at = pl.ds(pl.multiple_of(change_rows.start + w * K, 8), K)
            out_ref[i] = dot(log_ref[at, 0:orbitals], whole_ref[w])


def step_call(block, parts, before, more, states, vm, table):
    orbitals, n = table.shape[0], states.shape[2]
    rows = vm.shape[0]
    operands = [*parts, before, *more, states, vm, table]
    specs = [VMEM] * len(operands)
    log = (log_y(n).stop + orbitals, 128)
    if block == NMOVE - 1:
        specs[len(parts) + 1] = SMEM
        walkers, _, electrons = more[1].shape
        shapes = [(walkers // 2, K, electrons)] * 2 + [log]
    else:
        shapes = [(MOVED + more[0].shape[0] - orbitals, n), log]
    return pl.pallas_call(
        functools.partial(step_kernel, block, len(parts)),
        name="step",
        out_shape=tuple(jax.ShapeDtypeStruct(shape, F32) for shape in shapes),
        in_specs=specs,
        out_specs=(VMEM,) * len(shapes),
        scratch_shapes=[
            pltpu.VMEM((orbitals, n), F32),
            pltpu.VMEM((MOVED + rows, n), F32),
            *weights_scratch(n, 1, 1),
        ],
        compiler_params=params(),
        cost_estimate=lasting(3),
    )(*operands)


def last_kernel(counts, *refs):
    refs = list(refs)
    sums = [[refs.pop(0) for _ in range(count)] for count in counts]
    log_ref, vm_ref, out_ref, l_ref = refs
    n = log_ref.shape[1]
    ts = [log_ref[log_rows(block, n, "t"), :] for block in range(NMOVE)]
    for block in range(NMOVE - 1):
        r = unit(block, ts[block].shape[1])
        if block:
            sums_of = tree([ref[0:MOVED, :] for ref in sums[block - 1]])
            r = r - fold(dot(l_ref[...], sums_of))
        more = dot_nt(spread(r), ts[block])
        l_ref[...] = l_ref[...] + more if block else more
    t = jnp.transpose(ts[-1])
    for w in range(out_ref.shape[0]):
        at = slice(w * MOVED, (w + 1) * MOVED)
        early = l_ref[w * MOVED : (w + 1) * MOVED - K, :]
        factor = jnp.concatenate([early, t[w * K : (w + 1) * K, :]], axis=0)
        out_ref[w] = jnp.transpose(dot(factor, vm_ref[at, :]))


def last_call(s_parts, log, vm):
    rows, orbitals = vm.shape
    operands = [part for parts in s_parts for part in parts] + [log, vm]
    return pl.pallas_call(
        functools.partial(last_kernel, [len(parts) for parts in s_parts]),
        name="last",
        out_shape=(
            jax.ShapeDtypeStruct((rows // MOVED, orbitals, MOVED), F32),
            jax.ShapeDtypeStruct((rows, MOVED), F32),
        ),
        in_specs=[VMEM] * len(operands),
        out_specs=(VMEM, VMEM),
        compiler_params=params(),
        cost_estimate=lasting(2),
    )(*operands)


def both_halves(meta_ref, walkers, i):
    parity = meta_ref[meta_ref.shape[0] - 1]
    half = walkers // 2
    return i + half * parity, i + half * (1 - parity)


def assemble_kernel(meta_ref, own_ref, got_ref, code_ref, *refs):
    log_ref, v_ref, mine_ref, give_ref, held_ref, sem = refs
    n = log_ref.shape[1]
    walkers, orbitals, electrons = own_ref.shape
    load = pltpu.make_async_copy(code_ref, held_ref, sem)
    load.start()
    load.wait()

    def body(i, carry):
        for w, out_ref in zip(both_halves(meta_ref, walkers, i), (mine_ref, give_ref)):
            here, place, group = parent_of(meta_ref, walkers, w)
            scale = jnp.concatenate(
                [
                    got_ref[group, MOVED + j : MOVED + j + 1, :]
                    for j in range(electrons // orbitals)
                ],
                axis=1,
            )
            level = held_ref[group].astype(jnp.int32).astype(F32) * (1.0 / LEVELS)
            v = jnp.where(here, own_ref[place], level * jnp.abs(level) * scale)
            v_ref[w] = v
            change = []
            for b in range(NMOVE - 1):
                at = log_rows(b, n, "change").start + w * K
                change.append(log_ref[pl.ds(pl.multiple_of(at, 8), K), 0:orbitals])
            change = jnp.concatenate(change, axis=0)
            out_ref[i] = dot(change, v)
        return carry

    lax.fori_loop(0, walkers // 2, body, 0)


def assemble_call(meta, inverse, got, code, log):
    walkers, orbitals, electrons = inverse.shape
    half = (walkers // 2, (NMOVE - 1) * K, electrons)
    return pl.pallas_call(
        assemble_kernel,
        name="assemble",
        out_shape=(
            jax.ShapeDtypeStruct(inverse.shape, F32),
            jax.ShapeDtypeStruct(half, F32),
            jax.ShapeDtypeStruct(half, F32),
        ),
        in_specs=[SMEM, VMEM, VMEM, ANY, VMEM],
        out_specs=(VMEM,) * 3,
        scratch_shapes=[
            pltpu.VMEM(code.shape, code.dtype),
            pltpu.SemaphoreType.DMA(()),
        ],
        compiler_params=params(),
        cost_estimate=lasting(4),
    )(meta, inverse, got, code, log)


def join_kernel(mine_ref, got_ref, sum_ref, code_ref, power_ref):
    for i in range(mine_ref.shape[0]):
        x = mine_ref[i] + got_ref[i]
        sum_ref[i] = x
        size = jnp.abs(x)
        top = jnp.max(size, axis=0, keepdims=True)
        power = jnp.ceil(jnp.log(jnp.where(top > 0.0, top, 1.0)) * LOG2_E)
        power = jnp.where(top > 0.0, jnp.maximum(power, -126.0), 0.0)
        level = jnp.floor(jnp.sqrt(size) * (LEVELS * jnp.exp2(-0.5 * power)) + 0.5)
        level = jnp.minimum(level, LEVELS)
        code_ref[i] = jnp.where(x < 0.0, -level, level).astype(jnp.int32).astype(jnp.int16)
        power_ref[i : i + 1, :] = power


def join_call(mine, got):
    half, _, electrons = mine.shape
    return pl.pallas_call(
        join_kernel,
        name="join",
        out_shape=(
            jax.ShapeDtypeStruct(mine.shape, F32),
            jax.ShapeDtypeStruct(mine.shape, jnp.int16),
            jax.ShapeDtypeStruct((half, electrons), F32),
        ),
        in_specs=[VMEM, VMEM],
        out_specs=(VMEM,) * 3,
        compiler_params=params(),
        cost_estimate=lasting(1),
    )(mine, got)


def decode(code, power):
    root = jnp.exp2(0.5 * power[:, None, :]) * (1.0 / LEVELS)
    level = code.astype(F32)
    return (level * root) * (jnp.abs(level) * root)


def update_kernel(meta_ref, v_ref, factor_ref, l_ref, *refs):
    sums_refs, (out_ref, new_ref, sem) = refs[:4], refs[4:]
    walkers = v_ref.shape[0]

    def store(w):
        return pltpu.make_async_copy(new_ref.at[w], out_ref.at[w], sem.at[w])

    order = [meta_ref[walkers + b] for b in range(NMOVE)]
    half = walkers // 2
    own = [both_halves(meta_ref, walkers, i) for i in range(half)]
    places = [(own[i][h], i, sums_refs[2 * h : 2 * h + 2]) for i in range(half) for h in range(2)]
    lates = []
    for w, i, (early_ref, late_ref) in places:
        moved = moved_lanes(late_ref[i], order)[:, 0:MOVED]
        rows = l_ref[pl.ds(pl.multiple_of(w * MOVED, MOVED), MOVED), :]
        lates.append(dot_nt(moved, rows)[:, 0 : MOVED - K])
    for n, (w, i, (early_ref, late_ref)) in enumerate(places):
        lates[n] = late_ref[i] - dot(lates[n], early_ref[i])
    for late, (w, i, (early_ref, _)) in zip(lates, places):
        sums = jnp.concatenate([early_ref[i], late], axis=0)
        new_ref[w] = v_ref[w] - dot(factor_ref[w], sums)
        store(w).start()
    for w in range(walkers):
        store(w).wait()


def update_call(meta, inverse, factor, rows, sums):
    return pl.pallas_call(
        update_kernel,
        name="update",
        out_shape=jax.ShapeDtypeStruct(inverse.shape, F32),
        in_specs=[SMEM] + [VMEM] * 7,
        out_specs=ANY,
        scratch_shapes=[
            pltpu.VMEM(inverse.shape, F32),
            pltpu.SemaphoreType.DMA((inverse.shape[0],)),
        ],
        compiler_params=params(),
        cost_estimate=lasting(2),
    )(meta, inverse, factor, rows, *sums)


def place_kernel(meta_ref, own_ref, got_ref, log_ref, out_ref):
    _, walkers, electrons = own_ref.shape
    parts = electrons // got_ref.shape[2]
    lane = lax.broadcasted_iota(jnp.int32, (1, electrons), 1)
    for w in range(walkers):
        here, place, group = parent_of(meta_ref, walkers, w)
        fresh = []
        for b in range(NMOVE):
            block = meta_ref[walkers + b]
            moved = log_ref[log_rows(b, log_ref.shape[1], "moved"), :]
            fresh.append((block, roll(moved, (block - w) * K)))
        for d in range(3):
            at = MOVED + (d + 1) * parts
            far = jnp.concatenate(
                [got_ref[group, at + i : at + i + 1, :] for i in range(parts)], axis=1
            )
            line = jnp.where(here, own_ref[d, pl.ds(place, 1), :], far)
            for block, moved in fresh:
                moved = jnp.concatenate([moved[d : d + 1, :]] * (electrons // 128), axis=1)
                line = jnp.where(lane // K == block, moved, line)
            out_ref[d, w : w + 1, :] = line


def place_call(meta, positions, got, log):
    return pl.pallas_call(
        place_kernel,
        name="place",
        out_shape=jax.ShapeDtypeStruct(positions.shape, F32),
        in_specs=[SMEM] + [VMEM] * 3,
        out_specs=VMEM,
        compiler_params=params(),
        cost_estimate=lasting(1),
    )(meta, positions, got, log)


def swap(x, axis, k):
    return lax.ppermute(x, axis, [(i, i ^ k) for i in range(lax.axis_size(axis))])


def exchange(part, axis):
    return [part] + [swap(part, axis, k) for k in range(1, lax.axis_size(axis))]


def add_up(early, late, axis, done):
    parts = [early, late]
    k = 2
    size = lax.axis_size(axis)
    while k < size:
        got = [[swap(x, axis, k) for x in part[1:]] for part in parts]
        got, done = together(got, done)
        added = [decode(*x) for x in got]
        if 2 * k < size:
            parts = [join_call(part[0], x) for part, x in zip(parts, added)]
        else:
            parts = [[part[0] + x] for part, x in zip(parts, added)]
        k *= 2
    return [(x, swap(x, axis, 1)) for (x,) in parts], done


def together(*values):
    return lax.optimization_barrier(values)


def alltoall(x):
    return lax.all_to_all(x, "walker", split_axis=0, concat_axis=0, tiled=True)


def local(positions, inverse, spline_table, gaussian, accepted, block_order, parent):
    groups = lax.axis_size("walker")
    me = lax.axis_index("walker").astype(jnp.int32)
    parity = lax.rem(lax.axis_index("orb"), 2).astype(jnp.int32)
    meta = jnp.concatenate([parent, block_order[:NMOVE], me[None], parity[None]])
    positions = jnp.transpose(positions, (1, 0, 2))
    gaussian = jnp.transpose(gaussian, (1, 0, 2))

    info = alltoall(pack_call(parent, block_order, positions, gaussian, accepted, groups))
    own, code = columns_call(block_order, inverse, positions)
    states, outgoing, sending = route_call(meta, info, own)
    got = alltoall(outgoing)
    phi, grad, code = slopes_call(sending, states, spline_table, code)
    got, code, phi, grad = together(got, code, phi, grad)
    code = alltoall(code)
    vm, first = select_call(meta, own, got, grad)
    p0 = exchange(first, "orb")

    def step(b, parts, before, more):
        return step_call(b, parts, before, more, states, vm, spline_table)

    later = later_call(1, states, spline_table, vm)
    p1, log = step(0, p0, phi, [later])
    p1 = exchange(p1, "orb")
    later = later_call(2, states, spline_table, vm)
    p2, log = step(1, p1, log, [later])
    p2 = exchange(p2, "orb")
    held, code = together(states, code)
    later = later_call(3, held, spline_table, vm)
    p3, log = step(2, p2, log, [later])
    p3 = exchange(p3, "orb")
    whole, mine, give = assemble_call(meta, inverse, got, code, log)
    p3, mine, give = together(p3, mine, give)
    early = join_call(mine, swap(give, "orb", 1))
    mine, give, log = step(3, p3, log, [meta, whole])
    late = join_call(mine, swap(give, "orb", 1))
    factor, rows = last_call([p2, p3], log, vm)
    new_positions = place_call(meta, positions, got, log)
    factor, new_positions = together(factor, new_positions)
    (early, late), factor = add_up(early, late, "orb", factor)
    new_inverse = update_call(meta, whole, factor, rows, [early[0], late[0], early[1], late[1]])
    return jnp.transpose(new_positions, (1, 0, 2)), new_inverse


def solution(mesh):
    return jax.shard_map(
        local,
        mesh=mesh,
        in_specs=(
            P("walker", None, None),
            P("walker", "orb", None),
            P("orb", None),
            P("walker", None, None),
            P("walker", None),
            P(),
            P("walker"),
        ),
        out_specs=(P("walker", None, None), P("walker", "orb", None)),
        check_vma=False,
    )
```

```python
import functools

import jax
import jax.numpy as jnp
from jax import lax
from jax.experimental import pallas as pl
from jax.experimental.pallas import tpu as pltpu
from jax.sharding import PartitionSpec as P

GRID = 24
PLANE = GRID * GRID
MAIN = 512
EDGE = PLANE - MAIN
UNROLL = 12
CHUNKS = (4, 4, 4)
K = 16
NMOVE = 4
MOVED = K * NMOVE
CAP = 1
TAU = 0.25
ROOT_TAU = 0.5
F32 = jnp.float32
BF16 = jnp.bfloat16
LEVELS = 32767.0
LOG2_E = 1.4426950408889634
HIGHEST = lax.Precision.HIGHEST
VMEM = pl.BlockSpec(memory_space=pltpu.VMEM)
SMEM = pl.BlockSpec(memory_space=pltpu.SMEM)
ANY = pl.BlockSpec(memory_space=pl.ANY)
LIMIT = 16 * 2**20
WHOLE = 60 * 2**20
PART = 59500000
ALMOST = 63300000


def axis_weights(u, with_slopes):
    floors = jnp.floor(u)
    t = u - floors
    remain = 1.0 - t
    square = t * t
    cubed = square * t
    values = (
        remain * remain * remain / 6.0,
        (3.0 * cubed - 6.0 * square + 4.0) / 6.0,
        (-3.0 * cubed + 3.0 * square + 3.0 * t + 1.0) / 6.0,
        cubed / 6.0,
    )
    lanes = u.shape[1]
    line = lax.broadcasted_iota(jnp.int32, (GRID, lanes), 0)
    step = line - (floors.astype(jnp.int32) - 1)
    step = jnp.where(step < 0, step + GRID, step)
    step = jnp.where(step < 0, step + GRID, step)
    step = jnp.where(step >= GRID, step - GRID, step)

    def spread(weights):
        out = jnp.zeros((GRID, lanes), F32)
        for a in range(4):
            out = jnp.where(step == a, jnp.broadcast_to(weights[a], (GRID, lanes)), out)
        return out

    if not with_slopes:
        return spread(values), None
    slopes = (
        -0.5 * remain * remain,
        1.5 * square - 2.0 * t,
        -1.5 * square + t + 0.5,
        0.5 * square,
    )
    return spread(values), spread(slopes)


def products(first, second):
    return jnp.concatenate([first[y : y + 1, :] * second for y in range(GRID)], axis=0)


def fill(whole_ref, edge_ref, weights):
    n = edge_ref.shape[1]
    for i, weight in enumerate(weights):
        for j, piece in enumerate(split(weight)):
            whole_ref[:, (2 * i + j) * n : (2 * i + j + 1) * n] = piece
        edge_ref[2 * EDGE * i : 2 * EDGE * i + EDGE, :] = weight[MAIN:PLANE, :]
        edge_ref[2 * EDGE * i + EDGE : 2 * EDGE * (i + 1), :] = weight[0:EDGE, :]


def plane_pair(table_ref, pair, whole_ref):
    start = pl.multiple_of(pair * 2 * PLANE, 128)
    even = table_ref[:, pl.ds(start, MAIN)]
    start = pl.multiple_of(pair * 2 * PLANE + MAIN + 128, 128)
    odd = table_ref[:, pl.ds(start, MAIN)]
    return (
        jnp.dot(even, whole_ref[0:MAIN, :], preferred_element_type=F32),
        jnp.dot(odd, whole_ref[EDGE:PLANE, :], preferred_element_type=F32),
    )


def middle_weights(mid_ref, edge_ref, pair, terms):
    n = edge_ref.shape[1]
    at = pl.ds(pl.multiple_of(pair * 128, 128), 128)
    for i, (kind, w0, w1) in enumerate(terms):
        start = 2 * EDGE * kind
        part = jnp.concatenate(
            [
                w0 * edge_ref[start : start + EDGE, :],
                w1 * edge_ref[start + EDGE : start + 2 * EDGE, :],
            ],
            axis=0,
        )
        for j, piece in enumerate(split(part)):
            mid_ref[at, (2 * i + j) * n : (2 * i + j + 1) * n] = piece


def middle(table_ref, mid_ref):
    lanes = [
        table_ref[:, q * 2 * PLANE + MAIN : q * 2 * PLANE + MAIN + 128] for q in range(GRID // 2)
    ]
    lanes = jnp.concatenate(lanes, axis=1)
    return jnp.dot(lanes, mid_ref[...], preferred_element_type=F32)


def slopes_kernel(
    state_ref, table_ref, phi_ref, grad_ref, whole_ref, mid_ref, edge_ref, wx_ref, sx_ref,
    loads=(), beside=()
):
    n = state_ref.shape[2]
    wx, sx = axis_weights(state_ref[0, 0:1, :], True)
    wy, sy = axis_weights(state_ref[0, 1:2, :], True)
    wz, sz = axis_weights(state_ref[0, 2:3, :], True)
    wx_ref[...] = wx
    sx_ref[...] = sx
    fill(whole_ref, edge_ref, [products(wy, wz), products(sy, wz), products(wy, sz)])
    phi_ref[...] = jnp.zeros_like(phi_ref)
    grad_ref[...] = jnp.zeros_like(grad_ref)

    def body(pair, carry):
        even, odd = plane_pair(table_ref, pair, whole_ref)
        w0, w1 = wx_ref[pl.ds(2 * pair, 1), :], wx_ref[pl.ds(2 * pair + 1, 1), :]
        s0, s1 = sx_ref[pl.ds(2 * pair, 1), :], sx_ref[pl.ds(2 * pair + 1, 1), :]
        terms = [(0, w0, w1), (0, s0, s1), (1, w0, w1), (2, w0, w1)]
        middle_weights(mid_ref, edge_ref, pair, terms)

        def both(i):
            at, to = slice(2 * i * n, (2 * i + 1) * n), slice((2 * i + 1) * n, (2 * i + 2) * n)
            return even[:, at] + even[:, to], odd[:, at] + odd[:, to]

        e, o = both(0)
        phi_ref[...] += w0 * e + w1 * o
        grad_ref[:, 0:n] += s0 * e + s1 * o
        for d in (1, 2):
            e, o = both(d)
            grad_ref[:, d * n : (d + 1) * n] += w0 * e + w1 * o
        return carry

    pairs = GRID // 2
    if loads:
        start = 0
        for i, (load, size) in enumerate(zip(loads, CHUNKS)):
            load.wait()
            if i + 1 < len(loads):
                loads[i + 1].start()
            if beside[i] is not None:
                beside[i]()
            lax.fori_loop(start, start + size, body, 0, unroll=size)
            start += size
    else:
        lax.fori_loop(0, pairs, body, 0, unroll=UNROLL)
    rest = middle(table_ref, mid_ref)
    phi_ref[...] += rest[:, 0:n] + rest[:, n : 2 * n]
    for d in range(3):
        at = 2 * (d + 1) * n
        grad_ref[:, d * n : (d + 1) * n] += rest[:, at : at + n] + rest[:, at + n : at + 2 * n]


def first_kernel(
    sending_ref, states_ref, table_ref, code_in, phi_out, grad_out, code_out, *refs
):
    held_ref, phi_ref, grad_ref, code_ref = refs[:4]
    scratch, (in_sem, out_sem, code_sem) = refs[4:-3], refs[-3:]
    groups = code_out.shape[0]
    loads = []
    start = 0
    for i, pairs in enumerate(CHUNKS):
        at = pl.ds(start, 2 * PLANE * pairs)
        start += 2 * PLANE * pairs
        loads.append(
            pltpu.make_async_copy(table_ref.at[:, at], held_ref.at[:, at], in_sem.at[i])
        )
    loads[0].start()
    codes = pltpu.make_async_copy(code_in, code_ref, code_sem.at[groups])
    picks = []
    for g in range(groups):
        source = code_ref.at[sending_ref[g]]
        picks.append(pltpu.make_async_copy(source, code_out.at[g], code_sem.at[g]))

    def pick():
        codes.wait()
        for copy in picks:
            copy.start()

    beside = (None, codes.start, pick)
    slopes_kernel(
        states_ref.at[0:1], held_ref, phi_ref, grad_ref, *scratch, loads=loads, beside=beside
    )
    stores = [
        pltpu.make_async_copy(phi_ref, phi_out, out_sem.at[0]),
        pltpu.make_async_copy(grad_ref, grad_out, out_sem.at[1]),
    ]
    for store in stores:
        store.start()
    for store in stores + picks:
        store.wait()


def slopes_call(sending, states, table, code):
    orbitals = table.shape[0]
    n = states.shape[2]
    groups = sending.shape[0]
    shapes = [(orbitals, n), (orbitals, 3 * n)]
    return pl.pallas_call(
        first_kernel,
        name="slopes",
        out_shape=tuple(jax.ShapeDtypeStruct(shape, F32) for shape in shapes)
        + (jax.ShapeDtypeStruct((groups, *code.shape[1:]), code.dtype),),
        in_specs=[SMEM, VMEM, ANY, ANY],
        out_specs=(ANY, ANY, ANY),
        scratch_shapes=[pltpu.VMEM(table.shape, BF16)]
        + [pltpu.VMEM(shape, F32) for shape in shapes]
        + [pltpu.VMEM(code.shape, code.dtype)]
        + slopes_scratch(n)
        + [
            pltpu.SemaphoreType.DMA((len(CHUNKS),)),
            pltpu.SemaphoreType.DMA((2,)),
            pltpu.SemaphoreType.DMA((groups + 1,)),
        ],
        compiler_params=params(WHOLE),
        cost_estimate=lasting(5),
    )(sending, states, table, code)


def slopes_scratch(n):
    return weights_scratch(n, 3, 4) + [pltpu.VMEM((GRID, n), F32)]


def weights_scratch(n, kinds, terms):
    return [
        pltpu.VMEM((PLANE, 2 * kinds * n), BF16),
        pltpu.VMEM((GRID // 2 * 128, 2 * terms * n), BF16),
        pltpu.VMEM((2 * EDGE * kinds, n), F32),
        pltpu.VMEM((GRID, n), F32),
    ]


def later_kernel(block, states_ref, table_ref, vm_ref, out_ref, grad_ref, *scratch):
    orbitals = table_ref.shape[0]
    phi_ref = out_ref.at[0:orbitals]
    slopes_kernel(states_ref.at[block : block + 1], table_ref, phi_ref, grad_ref, *scratch)
    drift_rows(block, vm_ref, grad_ref, out_ref, orbitals)


def later_call(block, states, table, vm):
    orbitals = table.shape[0]
    n = states.shape[2]
    return pl.pallas_call(
        functools.partial(later_kernel, block),
        name="later",
        out_shape=jax.ShapeDtypeStruct((orbitals + drift_size(block), n), F32),
        in_specs=[VMEM] * 3,
        out_specs=VMEM,
        scratch_shapes=[pltpu.VMEM((orbitals, 3 * n), F32)] + slopes_scratch(n),
        compiler_params=params(),
        cost_estimate=lasting(5),
    )(states, table, vm)


def split(x):
    high = x.astype(BF16)
    return high, (x - high.astype(F32)).astype(BF16)


def product(a, b, dims):
    (a0, a1), (b0, b1) = split(a), split(b)

    def one(x, y):
        return lax.dot_general(x, y, (dims, ((), ())), preferred_element_type=F32)

    return one(a0, b0) + (one(a0, b1) + one(a1, b0))


def dot(a, b):
    return product(a, b, ((1,), (0,)))


def dot_nt(a, b):
    return product(a, b, ((1,), (1,)))


def own_lanes(rows, n, walker):
    lane = lax.broadcasted_iota(jnp.int32, (rows, n), 1)
    return jnp.logical_and(lane >= walker * K, lane < (walker + 1) * K)


def fold(big):
    n = big.shape[1]
    rows = big.shape[0] // (n // K)
    total = jnp.zeros((rows, n), F32)
    for w in range(n // K):
        total = jnp.where(own_lanes(rows, n, w), big[w * rows : (w + 1) * rows, :], total)
    return total


def unit(block, n):
    row = lax.broadcasted_iota(jnp.int32, (MOVED, n), 0)
    lane = lax.broadcasted_iota(jnp.int32, (MOVED, n), 1)
    return jnp.where(row - block * K == lane % K, 1.0, 0.0).astype(F32)


def tree(parts):
    while len(parts) > 1:
        parts = [parts[i] + parts[i + 1] for i in range(0, len(parts), 2)]
    return parts[0]


def total(refs):
    return tree([ref[...] for ref in refs])


def params(limit=LIMIT):
    return pltpu.CompilerParams(vmem_limit_bytes=limit)


def lasting(us):
    return pl.CostEstimate(flops=int(us * 1e9), bytes_accessed=0, transcendentals=0)


def parent_of(meta_ref, walkers, w):
    parent = meta_ref[w]
    group = parent // walkers
    here = group == meta_ref[walkers + NMOVE]
    return here, jnp.where(here, parent % walkers, 0), jnp.where(here, 0, group)


def block_lanes(x, block):
    lane = lax.broadcasted_iota(jnp.int32, x.shape, 1)
    kept = jnp.where(lane // K == block, x, 0.0)
    return tree([kept[:, i : i + 128] for i in range(0, x.shape[1], 128)])


def roll(x, shift):
    if isinstance(shift, int):
        shift = shift % 128
        return x if shift == 0 else pltpu.roll(x, shift, 1)
    return pltpu.roll(x, lax.rem(shift + 1024, 128), 1)


def moved_lanes(x, order_ref):
    line = jnp.zeros((x.shape[0], 128), F32)
    for b in range(NMOVE):
        block = order_ref[b]
        line = line + roll(block_lanes(x, block), (b - block) * K)
    return line


def pack_kernel(parent_ref, order_ref, *refs):
    (out_ref, pos_ref, gauss_ref, acc_ref), sem = refs[3:-1], refs[-1]
    copies = [
        pltpu.make_async_copy(refs[i], refs[i + 4], sem.at[i]) for i in range(3)
    ]
    for copy in copies:
        copy.start()
    for copy in copies:
        copy.wait()
    walkers = pos_ref.shape[1]
    half = jnp.zeros((walkers, 128 - MOVED), F32)
    lane = lax.broadcasted_iota(jnp.int32, (walkers, 128), 1)
    row = lax.broadcasted_iota(jnp.int32, (walkers, 128), 0)
    lines = []
    for d in range(3):
        line = moved_lanes(pos_ref[d], order_ref)
        lines.append(line + jnp.concatenate([half, gauss_ref[d]], axis=1))
    parents = jnp.zeros((walkers, 128), jnp.int32)
    for w in range(walkers):
        parents = jnp.where(row == w, parent_ref[w], parents)
    decided = jnp.concatenate([acc_ref[...].astype(F32), half], axis=1)
    lines.append(jnp.where(lane < MOVED, decided, parents.astype(F32)))
    for g in range(out_ref.shape[0]):
        for d in range(4):
            out_ref[g, d * walkers : (d + 1) * walkers, :] = lines[d]


def pack_call(parent, order, positions, gaussian, accepted, groups):
    walkers = positions.shape[1]
    held = [positions, gaussian, accepted]
    return pl.pallas_call(
        pack_kernel,
        name="pack",
        out_shape=jax.ShapeDtypeStruct((groups, 4 * walkers, 128), F32),
        in_specs=[SMEM, SMEM, ANY, ANY, ANY],
        out_specs=VMEM,
        scratch_shapes=[pltpu.VMEM(x.shape, x.dtype) for x in held]
        + [pltpu.SemaphoreType.DMA((3,))],
        compiler_params=params(WHOLE),
        cost_estimate=lasting(1),
    )(parent, order, *held)


def columns_kernel(order_ref, v_in, pos_in, own_out, code_out, v_ref, pos_ref, own_ref, code_ref, sem):
    walkers, orbitals, electrons = v_ref.shape

    def load(w):
        return pltpu.make_async_copy(v_in.at[w], v_ref.at[w], sem.at[0, w])

    def store(w):
        return (
            pltpu.make_async_copy(own_ref.at[w], own_out.at[w], sem.at[1, w]),
            pltpu.make_async_copy(code_ref.at[w], code_out.at[w], sem.at[2, w]),
        )

    first = pltpu.make_async_copy(pos_in, pos_ref, sem.at[0, walkers])
    first.start()
    for w in range(walkers):
        load(w).start()
    first.wait()

    def body(w, carry):
        load(w).wait()
        v = v_ref[w]
        own_ref[w, 0:MOVED, :] = jnp.transpose(moved_lanes(v, order_ref))[0:MOVED, :]
        size = jnp.abs(v)
        scale = jnp.max(size, axis=0, keepdims=True)
        at = MOVED
        for line in [scale] + [pos_ref[d, pl.ds(w, 1), :] for d in range(3)]:
            for i in range(0, electrons, orbitals):
                own_ref[w, at : at + 1, :] = line[:, i : i + orbitals]
                at += 1
        some = scale > 0.0
        step = jnp.where(some, LEVELS / jnp.sqrt(jnp.where(some, scale, 1.0)), 0.0)
        level = jnp.minimum(jnp.floor(jnp.sqrt(size) * step + 0.5), LEVELS)
        code_ref[w] = jnp.where(v < 0.0, -level, level).astype(jnp.int32).astype(jnp.int16)
        for copy in store(w):
            copy.start()
        return carry

    lax.fori_loop(0, walkers, body, 0)
    for w in range(walkers):
        for copy in store(w):
            copy.wait()


def payload_rows(orbitals, electrons):
    return MOVED + 4 * electrons // orbitals


def columns_call(order, inverse, positions):
    walkers, orbitals, electrons = inverse.shape
    own = (walkers, payload_rows(orbitals, electrons), orbitals)
    return pl.pallas_call(
        columns_kernel,
        name="columns",
        out_shape=(
            jax.ShapeDtypeStruct(own, F32),
            jax.ShapeDtypeStruct(inverse.shape, jnp.int16),
        ),
        in_specs=[SMEM, ANY, ANY],
        out_specs=(ANY, ANY),
        scratch_shapes=[
            pltpu.VMEM(inverse.shape, F32),
            pltpu.VMEM(positions.shape, F32),
            pltpu.VMEM(own, F32),
            pltpu.VMEM(inverse.shape, jnp.int16),
            pltpu.SemaphoreType.DMA((3, walkers + 1)),
        ],
        compiler_params=params(WHOLE),
        cost_estimate=lasting(3),
    )(order, inverse, positions)


def route_kernel(meta_ref, info_in, own_in, states_ref, out_ref, sending_ref, *refs):
    info_ref, own_ref, parents_ref, sem, out_sem = refs
    walkers = own_ref.shape[0]
    groups = out_ref.shape[0]
    rows = 3 * walkers
    at = pl.ds(rows, walkers)
    asked = pltpu.make_async_copy(info_in.at[:, at], parents_ref, sem.at[2])
    asked.start()
    loads = [
        pltpu.make_async_copy(info_in, info_ref, sem.at[0]),
        pltpu.make_async_copy(own_in, own_ref, sem.at[1]),
    ]
    for load in loads:
        load.start()
    asked.wait()
    me = meta_ref[walkers + NMOVE]
    sending = []
    for g in range(groups):
        wanted = jnp.int32(0)
        for s in range(walkers):
            within = parents_ref[g, s, MOVED].astype(jnp.int32) - me * walkers
            mine = jnp.logical_and(within >= 0, within < walkers)
            wanted = jnp.where(mine, within, wanted)
        sending.append(jnp.where(me == g, 0, wanted))
        sending_ref[g] = sending[g]
    for load in loads[1:]:
        load.wait()
    stores = []
    for g in range(groups):
        source = sending[g]
        stores.append(pltpu.make_async_copy(own_ref.at[source], out_ref.at[g], out_sem.at[g]))
    for store in stores:
        store.start()
    loads[0].wait()
    lane = lax.broadcasted_iota(jnp.int32, (8, 128), 1)
    tiles = []
    for w in range(walkers):
        group, place = meta_ref[w] // walkers, meta_ref[w] % walkers
        line = [info_ref[group, pl.ds(d * walkers + place, 1), :] for d in range(4)]
        line = jnp.concatenate(line, axis=0)
        tiles.append(jnp.concatenate([line, roll(line, 128 - MOVED)], axis=0))
    for b in range(NMOVE):
        state = jnp.zeros((8, 128), F32)
        for w in range(walkers):
            state = jnp.where(lane // K == w, roll(tiles[w], (w - b) * K), state)
        states_ref[b] = state
    for store in stores:
        store.wait()


def route_call(meta, info, own):
    groups = info.shape[0]
    return pl.pallas_call(
        route_kernel,
        name="route",
        out_shape=(
            jax.ShapeDtypeStruct((NMOVE, 8, 128), F32),
            jax.ShapeDtypeStruct((groups, *own.shape[1:]), F32),
            jax.ShapeDtypeStruct((groups,), jnp.int32),
        ),
        in_specs=[SMEM, ANY, ANY],
        out_specs=(VMEM, ANY, SMEM),
        scratch_shapes=[
            pltpu.VMEM(info.shape, F32),
            pltpu.VMEM(own.shape, F32),
            pltpu.SMEM((groups, own.shape[0], 128), F32),
            pltpu.SemaphoreType.DMA((3,)),
            pltpu.SemaphoreType.DMA((groups,)),
        ],
        compiler_params=params(ALMOST),
        cost_estimate=lasting(3),
    )(meta, info, own)


def select_kernel(meta_ref, own_ref, got_ref, grad_in, vm_ref, out_ref, grad_ref, sem):
    walkers = own_ref.shape[0]
    load = pltpu.make_async_copy(grad_in, grad_ref, sem.at[walkers])
    load.start()

    def copy(w, source):
        to = vm_ref.at[w * MOVED : (w + 1) * MOVED]
        return pltpu.make_async_copy(source.at[0:MOVED], to, sem.at[w])

    for w in range(walkers):
        here, place, group = parent_of(meta_ref, walkers, w)

        @pl.when(here)
        def _():
            copy(w, own_ref.at[place]).start()

        @pl.when(jnp.logical_not(here))
        def _():
            copy(w, got_ref.at[group]).start()

    for w in range(walkers):
        copy(w, own_ref.at[0]).wait()
    load.wait()
    drift_rows(0, vm_ref, grad_ref, out_ref, 0)


def drift_size(block):
    return 8 + 3 * K * block


def drift_rows(block, vm_ref, grad_ref, out_ref, at):
    n = grad_ref.shape[1] // 3
    size = K * block
    used = size + K
    rows = [vm_ref[w * MOVED : w * MOVED + used, :] for w in range(n // K)]
    big = dot(jnp.concatenate(rows, axis=0), grad_ref[...])
    out_ref[at + 3 : at + 8, :] = jnp.zeros((5, n), F32)
    for d in range(3):
        q = fold(big[:, d * n : (d + 1) * n])
        own = q[size:used, :] * unit(0, n)[0:K, :]
        out_ref[at + d : at + d + 1, :] = jnp.sum(own, axis=0, keepdims=True)
        if block:
            out_ref[at + 8 + d * size : at + 8 + (d + 1) * size, :] = q[0:size, :]


def drift_of(block, q, t):
    size = K * block
    lines = [q[0:3, :]]
    if block:
        lines[0] += jnp.concatenate(
            [
                jnp.sum(q[8 + d * size : 8 + (d + 1) * size, :] * t[0:size, :], axis=0)[None]
                for d in range(3)
            ],
            axis=0,
        )
    return lines[0]


def select_call(meta, own, got, grad):
    walkers, _, orbitals = own.shape
    n = grad.shape[1] // 3
    return pl.pallas_call(
        select_kernel,
        name="select",
        out_shape=(
            jax.ShapeDtypeStruct((walkers * MOVED, orbitals), F32),
            jax.ShapeDtypeStruct((drift_size(0), n), F32),
        ),
        in_specs=[SMEM, ANY, ANY, ANY],
        out_specs=(VMEM, VMEM),
        scratch_shapes=[
            pltpu.VMEM(grad.shape, F32),
            pltpu.SemaphoreType.DMA((walkers + 1,)),
        ],
        compiler_params=params(PART),
        cost_estimate=lasting(2),
    )(meta, own, got, grad)


def spread(x):
    n = x.shape[1]
    return jnp.concatenate([jnp.where(own_lanes(x.shape[0], n, w), x, 0.0) for w in range(n // K)], axis=0)


BLOCK_ROWS = 8 + MOVED


def log_rows(block, n, kind):
    start = block * (BLOCK_ROWS + n)
    if kind == "moved":
        return slice(start, start + 8)
    if kind == "t":
        return slice(start + 8, start + BLOCK_ROWS)
    return slice(start + BLOCK_ROWS, start + BLOCK_ROWS + n)


def log_y(n):
    start = NMOVE * (BLOCK_ROWS + n)
    return slice(start, start + n // K * MOVED)


def step_kernel(block, count, *refs):
    refs = list(refs)
    last = block == NMOVE - 1
    parts = [refs.pop(0) for _ in range(count)]
    before_ref = refs.pop(0)
    if last:
        meta_ref, whole_ref = refs.pop(0), refs.pop(0)
    else:
        later_ref = refs.pop(0)
    states_ref, vm_ref, table_ref = [refs.pop(0) for _ in range(3)]
    if last:
        mine_ref, give_ref = refs.pop(0), refs.pop(0)
    else:
        s_ref = refs.pop(0)
    log_ref, sum_ref, big_ref, wide_ref, mid_ref, edge_ref, wx_ref = refs
    orbitals, n = sum_ref.shape
    y_rows = log_y(n)
    phi_rows = slice(y_rows.stop, y_rows.stop + orbitals)
    if not last:
        s_ref[MOVED:, :] = later_ref[orbitals:, :]
        log_ref[phi_rows, :] = later_ref[0:orbitals, :]
    state = states_ref[block]
    if block == 0:
        phi_ref = before_ref
        t = unit(0, n)
        drifts = drift_of(0, total(parts), None)
    else:
        phi_ref = before_ref.at[phi_rows]
        done = slice(0, block * (BLOCK_ROWS + n))
        log_ref[done, :] = before_ref[done, :]
        t_before = before_ref[log_rows(block - 1, n, "t"), :]
        big_ref[0:MOVED, :] = tree([ref[0:MOVED, :] for ref in parts])
        if block > 1:
            y_before = before_ref[y_rows, 0:MOVED]
            big_ref[MOVED:, :] = dot(y_before, big_ref[0:MOVED, :])
            big_ref[0:MOVED, :] = big_ref[0:MOVED, :] - fold(big_ref[MOVED:, :])
        y_all = dot_nt(spread(big_ref[0:MOVED, :]), t_before)
        if block > 1:
            y_all = y_all + before_ref[y_rows, 0:MOVED]
        log_ref[y_rows, 0:MOVED] = y_all
        start = y_rows.start + block * K
        rows = jnp.concatenate(
            [
                log_ref[start + w * MOVED : start + w * MOVED + K, 0:MOVED]
                for w in range(n // K)
            ],
            axis=0,
        )
        log_ref[log_rows(block, n, "t"), :] = unit(block, n) - jnp.transpose(rows)
        t = log_ref[log_rows(block, n, "t"), :]
        q = tree([ref[MOVED:, :] for ref in parts])
        drifts = drift_of(block, q, t)
    if block == 0:
        log_ref[log_rows(0, n, "t"), :] = t
    speeds = jnp.sum(drifts * drifts, axis=0, keepdims=True)
    capped = drifts / jnp.sqrt(1.0 + TAU * speeds)
    moved = state[0:3, :] + state[3:4, :] * (TAU * capped + ROOT_TAU * state[4:7, :])
    moved_rows = log_rows(block, n, "moved")
    log_ref[moved_rows, :] = jnp.concatenate([moved, jnp.zeros((5, n), F32)], axis=0)
    wx, _ = axis_weights(moved[0:1, :], False)
    wy, _ = axis_weights(moved[1:2, :], False)
    wz, _ = axis_weights(moved[2:3, :], False)
    wx_ref[...] = wx
    fill(wide_ref, edge_ref, [products(wy, wz)])
    sum_ref[...] = jnp.zeros_like(sum_ref)

    def body(pair, carry):
        even, odd = plane_pair(table_ref, pair, wide_ref)
        w0, w1 = wx_ref[pl.ds(2 * pair, 1), :], wx_ref[pl.ds(2 * pair + 1, 1), :]
        middle_weights(mid_ref, edge_ref, pair, [(0, w0, w1)])
        sum_ref[...] += w0 * (even[:, 0:n] + even[:, n:]) + w1 * (odd[:, 0:n] + odd[:, n:])
        return carry

    lax.fori_loop(0, GRID // 2, body, 0, unroll=UNROLL)
    rest = middle(table_ref, mid_ref)
    change = sum_ref[...] + (rest[:, 0:n] + rest[:, n:]) - phi_ref[...]
    change_rows = log_rows(block, n, "change")
    log_ref[change_rows, 0:orbitals] = jnp.transpose(change)
    if not last:
        s_ref[0:MOVED, :] = fold(dot(vm_ref[...], change))
        return
    walkers = whole_ref.shape[0]
    for i in range(walkers // 2):
        for w, out_ref in zip(both_halves(meta_ref, walkers, i), (mine_ref, give_ref)):
            at = pl.ds(pl.multiple_of(change_rows.start + w * K, 8), K)
            out_ref[i] = dot(log_ref[at, 0:orbitals], whole_ref[w])


def step_call(block, parts, before, more, states, vm, table):
    orbitals, n = table.shape[0], states.shape[2]
    rows = vm.shape[0]
    operands = [*parts, before, *more, states, vm, table]
    specs = [VMEM] * len(operands)
    log = (log_y(n).stop + orbitals, 128)
    if block == NMOVE - 1:
        specs[len(parts) + 1] = SMEM
        walkers, _, electrons = more[1].shape
        shapes = [(walkers // 2, K, electrons)] * 2 + [log]
    else:
        shapes = [(MOVED + more[0].shape[0] - orbitals, n), log]
    return pl.pallas_call(
        functools.partial(step_kernel, block, len(parts)),
        name="step",
        out_shape=tuple(jax.ShapeDtypeStruct(shape, F32) for shape in shapes),
        in_specs=specs,
        out_specs=(VMEM,) * len(shapes),
        scratch_shapes=[
            pltpu.VMEM((orbitals, n), F32),
            pltpu.VMEM((MOVED + rows, n), F32),
            *weights_scratch(n, 1, 1),
        ],
        compiler_params=params(),
        cost_estimate=lasting(3),
    )(*operands)


def last_kernel(counts, *refs):
    refs = list(refs)
    sums = [[refs.pop(0) for _ in range(count)] for count in counts]
    log_ref, vm_ref, out_ref, l_ref = refs
    n = log_ref.shape[1]
    ts = [log_ref[log_rows(block, n, "t"), :] for block in range(NMOVE)]
    for block in range(NMOVE - 1):
        r = unit(block, ts[block].shape[1])
        if block:
            sums_of = tree([ref[0:MOVED, :] for ref in sums[block - 1]])
            r = r - fold(dot(l_ref[...], sums_of))
        more = dot_nt(spread(r), ts[block])
        l_ref[...] = l_ref[...] + more if block else more
    t = jnp.transpose(ts[-1])
    for w in range(out_ref.shape[0]):
        at = slice(w * MOVED, (w + 1) * MOVED)
        early = l_ref[w * MOVED : (w + 1) * MOVED - K, :]
        factor = jnp.concatenate([early, t[w * K : (w + 1) * K, :]], axis=0)
        out_ref[w] = jnp.transpose(dot(factor, vm_ref[at, :]))


def last_call(s_parts, log, vm):
    rows, orbitals = vm.shape
    operands = [part for parts in s_parts for part in parts] + [log, vm]
    return pl.pallas_call(
        functools.partial(last_kernel, [len(parts) for parts in s_parts]),
        name="last",
        out_shape=(
            jax.ShapeDtypeStruct((rows // MOVED, orbitals, MOVED), F32),
            jax.ShapeDtypeStruct((rows, MOVED), F32),
        ),
        in_specs=[VMEM] * len(operands),
        out_specs=(VMEM, VMEM),
        compiler_params=params(),
        cost_estimate=lasting(2),
    )(*operands)


def both_halves(meta_ref, walkers, i):
    parity = meta_ref[meta_ref.shape[0] - 1]
    half = walkers // 2
    return i + half * parity, i + half * (1 - parity)


def assemble_kernel(meta_ref, own_ref, got_ref, code_ref, *refs):
    log_ref, v_ref, mine_ref, give_ref, held_ref, sem = refs
    n = log_ref.shape[1]
    walkers, orbitals, electrons = own_ref.shape
    load = pltpu.make_async_copy(code_ref, held_ref, sem)
    load.start()
    load.wait()

    def body(i, carry):
        for w, out_ref in zip(both_halves(meta_ref, walkers, i), (mine_ref, give_ref)):
            here, place, group = parent_of(meta_ref, walkers, w)
            scale = jnp.concatenate(
                [
                    got_ref[group, MOVED + j : MOVED + j + 1, :]
                    for j in range(electrons // orbitals)
                ],
                axis=1,
            )
            level = held_ref[group].astype(jnp.int32).astype(F32) * (1.0 / LEVELS)
            v = jnp.where(here, own_ref[place], level * jnp.abs(level) * scale)
            v_ref[w] = v
            change = []
            for b in range(NMOVE - 1):
                at = log_rows(b, n, "change").start + w * K
                change.append(log_ref[pl.ds(pl.multiple_of(at, 8), K), 0:orbitals])
            change = jnp.concatenate(change, axis=0)
            out_ref[i] = dot(change, v)
        return carry

    lax.fori_loop(0, walkers // 2, body, 0)


def assemble_call(meta, inverse, got, code, log):
    walkers, orbitals, electrons = inverse.shape
    half = (walkers // 2, (NMOVE - 1) * K, electrons)
    return pl.pallas_call(
        assemble_kernel,
        name="assemble",
        out_shape=(
            jax.ShapeDtypeStruct(inverse.shape, F32),
            jax.ShapeDtypeStruct(half, F32),
            jax.ShapeDtypeStruct(half, F32),
        ),
        in_specs=[SMEM, VMEM, VMEM, ANY, VMEM],
        out_specs=(VMEM,) * 3,
        scratch_shapes=[
            pltpu.VMEM(code.shape, code.dtype),
            pltpu.SemaphoreType.DMA(()),
        ],
        compiler_params=params(),
        cost_estimate=lasting(4),
    )(meta, inverse, got, code, log)


def join_kernel(mine_ref, got_ref, sum_ref, code_ref, power_ref):
    for i in range(mine_ref.shape[0]):
        x = mine_ref[i] + got_ref[i]
        sum_ref[i] = x
        size = jnp.abs(x)
        top = jnp.max(size, axis=0, keepdims=True)
        power = jnp.ceil(jnp.log(jnp.where(top > 0.0, top, 1.0)) * LOG2_E)
        power = jnp.where(top > 0.0, jnp.maximum(power, -126.0), 0.0)
        level = jnp.floor(jnp.sqrt(size) * (LEVELS * jnp.exp2(-0.5 * power)) + 0.5)
        level = jnp.minimum(level, LEVELS)
        code_ref[i] = jnp.where(x < 0.0, -level, level).astype(jnp.int32).astype(jnp.int16)
        power_ref[i : i + 1, :] = power


def join_call(mine, got):
    half, _, electrons = mine.shape
    return pl.pallas_call(
        join_kernel,
        name="join",
        out_shape=(
            jax.ShapeDtypeStruct(mine.shape, F32),
            jax.ShapeDtypeStruct(mine.shape, jnp.int16),
            jax.ShapeDtypeStruct((half, electrons), F32),
        ),
        in_specs=[VMEM, VMEM],
        out_specs=(VMEM,) * 3,
        compiler_params=params(),
        cost_estimate=lasting(1),
    )(mine, got)


def decode(code, power):
    root = jnp.exp2(0.5 * power[:, None, :]) * (1.0 / LEVELS)
    level = code.astype(F32)
    return (level * root) * (jnp.abs(level) * root)


def update_kernel(meta_ref, v_ref, factor_ref, l_ref, *refs):
    sums_refs, (out_ref, new_ref, sem) = refs[:4], refs[4:]
    walkers = v_ref.shape[0]

    def store(w):
        return pltpu.make_async_copy(new_ref.at[w], out_ref.at[w], sem.at[w])

    order = [meta_ref[walkers + b] for b in range(NMOVE)]
    half = walkers // 2
    own = [both_halves(meta_ref, walkers, i) for i in range(half)]
    places = [(own[i][h], i, sums_refs[2 * h : 2 * h + 2]) for i in range(half) for h in range(2)]
    lates = []
    for w, i, (early_ref, late_ref) in places:
        moved = moved_lanes(late_ref[i], order)[:, 0:MOVED]
        rows = l_ref[pl.ds(pl.multiple_of(w * MOVED, MOVED), MOVED), :]
        lates.append(dot_nt(moved, rows)[:, 0 : MOVED - K])
    for n, (w, i, (early_ref, late_ref)) in enumerate(places):
        lates[n] = late_ref[i] - dot(lates[n], early_ref[i])
    for late, (w, i, (early_ref, _)) in zip(lates, places):
        sums = jnp.concatenate([early_ref[i], late], axis=0)
        new_ref[w] = v_ref[w] - dot(factor_ref[w], sums)
        store(w).start()
    for w in range(walkers):
        store(w).wait()


def update_call(meta, inverse, factor, rows, sums):
    return pl.pallas_call(
        update_kernel,
        name="update",
        out_shape=jax.ShapeDtypeStruct(inverse.shape, F32),
        in_specs=[SMEM] + [VMEM] * 7,
        out_specs=ANY,
        scratch_shapes=[
            pltpu.VMEM(inverse.shape, F32),
            pltpu.SemaphoreType.DMA((inverse.shape[0],)),
        ],
        compiler_params=params(),
        cost_estimate=lasting(2),
    )(meta, inverse, factor, rows, *sums)


def place_kernel(meta_ref, own_ref, got_ref, log_ref, out_ref):
    _, walkers, electrons = own_ref.shape
    parts = electrons // got_ref.shape[2]
    lane = lax.broadcasted_iota(jnp.int32, (1, electrons), 1)
    for w in range(walkers):
        here, place, group = parent_of(meta_ref, walkers, w)
        fresh = []
        for b in range(NMOVE):
            block = meta_ref[walkers + b]
            moved = log_ref[log_rows(b, log_ref.shape[1], "moved"), :]
            fresh.append((block, roll(moved, (block - w) * K)))
        for d in range(3):
            at = MOVED + (d + 1) * parts
            far = jnp.concatenate(
                [got_ref[group, at + i : at + i + 1, :] for i in range(parts)], axis=1
            )
            line = jnp.where(here, own_ref[d, pl.ds(place, 1), :], far)
            for block, moved in fresh:
                moved = jnp.concatenate([moved[d : d + 1, :]] * (electrons // 128), axis=1)
                line = jnp.where(lane // K == block, moved, line)
            out_ref[d, w : w + 1, :] = line


def place_call(meta, positions, got, log):
    return pl.pallas_call(
        place_kernel,
        name="place",
        out_shape=jax.ShapeDtypeStruct(positions.shape, F32),
        in_specs=[SMEM] + [VMEM] * 3,
        out_specs=VMEM,
        compiler_params=params(),
        cost_estimate=lasting(1),
    )(meta, positions, got, log)


def swap(x, axis, k):
    return lax.ppermute(x, axis, [(i, i ^ k) for i in range(lax.axis_size(axis))])


def exchange(part, axis):
    return [part] + [swap(part, axis, k) for k in range(1, lax.axis_size(axis))]


def add_up(early, late, axis, done):
    parts = [early, late]
    k = 2
    size = lax.axis_size(axis)
    while k < size:
        got = [[swap(x, axis, k) for x in part[1:]] for part in parts]
        got, done = together(got, done)
        added = [decode(*x) for x in got]
        if 2 * k < size:
            parts = [join_call(part[0], x) for part, x in zip(parts, added)]
        else:
            parts = [[part[0] + x] for part, x in zip(parts, added)]
        k *= 2
    return [(x, swap(x, axis, 1)) for (x,) in parts], done


def together(*values):
    return lax.optimization_barrier(values)


def alltoall(x):
    return lax.all_to_all(x, "walker", split_axis=0, concat_axis=0, tiled=True)


def local(positions, inverse, spline_table, gaussian, accepted, block_order, parent):
    groups = lax.axis_size("walker")
    me = lax.axis_index("walker").astype(jnp.int32)
    parity = lax.rem(lax.axis_index("orb"), 2).astype(jnp.int32)
    meta = jnp.concatenate([parent, block_order[:NMOVE], me[None], parity[None]])
    positions = jnp.transpose(positions, (1, 0, 2))
    gaussian = jnp.transpose(gaussian, (1, 0, 2))

    info = alltoall(pack_call(parent, block_order, positions, gaussian, accepted, groups))
    own, code = columns_call(block_order, inverse, positions)
    states, outgoing, sending = route_call(meta, info, own)
    got = alltoall(outgoing)
    phi, grad, code = slopes_call(sending, states, spline_table, code)
    got, code, phi, grad = together(got, code, phi, grad)
    code = alltoall(code)
    vm, first = select_call(meta, own, got, grad)
    p0 = exchange(first, "orb")

    def step(b, parts, before, more):
        return step_call(b, parts, before, more, states, vm, spline_table)

    later = later_call(1, states, spline_table, vm)
    p1, log = step(0, p0, phi, [later])
    p1 = exchange(p1, "orb")
    later = later_call(2, states, spline_table, vm)
    p2, log = step(1, p1, log, [later])
    p2 = exchange(p2, "orb")
    held, code = together(states, code)
    later = later_call(3, held, spline_table, vm)
    p3, log = step(2, p2, log, [later])
    p3 = exchange(p3, "orb")
    whole, mine, give = assemble_call(meta, inverse, got, code, log)
    p3, mine, give = together(p3, mine, give)
    early = join_call(mine, swap(give, "orb", 1))
    mine, give, log = step(3, p3, log, [meta, whole])
    late = join_call(mine, swap(give, "orb", 1))
    factor, rows = last_call([p2, p3], log, vm)
    new_positions = place_call(meta, positions, got, log)
    factor, new_positions = together(factor, new_positions)
    (early, late), factor = add_up(early, late, "orb", factor)
    new_inverse = update_call(meta, whole, factor, rows, [early[0], late[0], early[1], late[1]])
    return jnp.transpose(new_positions, (1, 0, 2)), new_inverse


def solution(mesh):
    return jax.shard_map(
        local,
        mesh=mesh,
        in_specs=(
            P("walker", None, None),
            P("walker", "orb", None),
            P("orb", None),
            P("walker", None, None),
            P("walker", None),
            P(),
            P("walker"),
        ),
        out_specs=(P("walker", None, None), P("walker", "orb", None)),
        check_vma=False,
    )
```
